32 devices in a mesh: mem: 2 (over x), tile: 16 (over z, y, core).
Axes of the slice: x: 2, y: 2, z: 4, core: 2. Of those that a mesh axis runs over, the one named last changes fastest.
Arguments:
- fields: float32 [256, 8, 8192], P('mem', None, 'tile')
- coefficients: float32 [6, 8192], P(None, 'tile'), may hold values from 0.04 to 0.16
- neighbours: int32 [6, 8192], P(None, 'tile'), may hold values from 0 to 8191, as said below
- obs_cell: int32 [32768], P('tile'), may hold values from 0 to 511
- obs_level: int32 [32768], P('tile'), may hold values from 0 to 7
- obs_value: float32 [32768], replicated, may hold values from -6 to 6
- obs_rinv: float32 [32768], replicated, may hold values from 2 to 32
- obs_index: int32 [8, 16, 128], P('mem', 'tile'), may hold values from 0 to 6143, as said below
- obs_weight: int32 [8, 16, 128], P('mem', 'tile'), may hold values from 0 to 3
Outputs:
- analysis: bfloat16 [256, 8, 8192], P('mem', None, 'tile')
The draws below stay inside these ranges and needn't reach their ends.
Inputs may be any that keep to these rules, and one draw needn't show every extreme that they name: `neighbours`: each neighbour lies within 32 columns of its cell in the global column order, counted around the end of the order back to its start. `obs_index`: an entry indexes the observations of three consecutive tiles laid end to end: the tile before the block's tile, the block's own tile, and the tile after it, with wrap-around over tiles. `obs_weight`: level 0 marks a padding entry that carries no weight.
All inputs are finite; a program needn't handle non-finite values.
Results may differ from the reference program's by a relative error of at most 0.012.
Values may be sent and summed in bfloat16 or wider, within the bound.
No kernel may reach another device: no remote copies, remote signals or barrier semaphores. Data moves between devices by JAX's collectives and lax.ppermute only.
A program may use at most 64 MiB of HBM per device.

```python
import math
import jax
import jax.numpy as jnp
from jax import lax

SAMPLE_SIZE = 256
HEIGHT_LAYERS = 8
PATCH_SITES = 512
NOBS_T = 2048
NOBS_LOC = 128
HALO = 32
NS_ITERS = 8
MESH_SITES_ALL = 8192
NOBS = 32768
BPT = 8
N_TILE = 16


def draw_fields(key, part):
    key = jax.random.fold_in(key, 1)
    base_key, pert_key = jax.random.split(key, 2)
    base_state = jax.random.normal(base_key, (1, HEIGHT_LAYERS, MESH_SITES_ALL), jnp.float32)
    spread = jax.random.normal(pert_key, (SAMPLE_SIZE, HEIGHT_LAYERS, MESH_SITES_ALL), jnp.float32)
    return base_state + 0.8 * spread


def draw_neighbours(key, part):
    key = jax.random.fold_in(key, 2)
    reach_key, direction_key = jax.random.split(key, 2)
    reach_size = jax.random.randint(reach_key, (6, MESH_SITES_ALL), 1, HALO + 1)
    slot_number = jnp.arange(6, dtype=jnp.int32)[:, None]
    reach_size = jnp.where(slot_number == 0, HALO, reach_size)
    direction = 2 * jax.random.randint(direction_key, (6, MESH_SITES_ALL), 0, 2) - 1
    cell_number = jnp.arange(MESH_SITES_ALL, dtype=jnp.int32)[None, :]
    return ((cell_number + direction * reach_size + MESH_SITES_ALL) % MESH_SITES_ALL).astype(jnp.int32)


def draw_obs_index(key, part):
    key = jax.random.fold_in(key, 3)
    block_number = jnp.arange(BPT, dtype=jnp.int32)[:, None, None]
    centre = NOBS_T + block_number * NOBS_T // (BPT - 1)
    offset = jax.random.randint(key, (BPT, N_TILE, NOBS_LOC), -NOBS_T, NOBS_T + 1)
    slot_number = jnp.arange(NOBS_LOC, dtype=jnp.int32)[None, None, :]
    offset = jnp.where((block_number == 0) & (slot_number == 0), -NOBS_T, offset)
    offset = jnp.where((block_number == BPT - 1) & (slot_number == 0), NOBS_T, offset)
    return jnp.clip(centre + offset, 0, 3 * NOBS_T - 1).astype(jnp.int32)


def touch_ends(values, stream_key, low, largest):
    dims = values.shape
    place = [jax.random.randint(jax.random.fold_in(stream_key, axis), (), 0, dims[axis]) for axis in range(len(dims))]
    values = values.at[tuple(place)].set(low)
    longest = dims.index(max(dims))
    place[longest] = (place[longest] + 1) % dims[longest]
    return values.at[tuple(place)].set(largest)


def block_scale(stream_key, extent, cuts, low, top_value):
    gain, own = 1.0, jax.random.fold_in(stream_key, 6)
    for axis_at, blocks in cuts:
        draws = jnp.exp(jax.random.uniform(jax.random.fold_in(own, axis_at), (blocks,), jnp.float32, low / len(cuts), top_value / len(cuts)))
        gain = gain * jnp.repeat(draws, extent[axis_at] // blocks).reshape([-1 if axis == axis_at else 1 for axis in range(len(extent))])
    return gain


def centred(own_key, extent, scale, bound, kind=jnp.bfloat16):
    return jnp.clip(scale * jax.random.normal(own_key, extent, jnp.float32), -bound, bound).astype(kind)


def setup_inputs(seed: int = 0) -> dict:
    splits = jax.random.split(jax.random.key(seed), 10)
    return {
        "fields": draw_fields(jax.random.fold_in(splits[9], 71), 0),
        "coefficients": jnp.clip(jnp.exp(math.log(0.16) - 1.3862944 * jax.random.uniform(splits[1], (6, MESH_SITES_ALL), jnp.float32) ** block_scale(splits[1], (6, MESH_SITES_ALL), ((1, 16),), -0.2, 0.2)), 0.04, 0.16),
        "neighbours": draw_neighbours(jax.random.fold_in(splits[9], 71), 0),
        "obs_cell": touch_ends(jax.random.randint(splits[3], (NOBS,), 0, PATCH_SITES), jax.random.fold_in(splits[3], 1), 0, PATCH_SITES - 1).astype(jnp.int32),
        "obs_level": touch_ends(jax.random.randint(splits[4], (NOBS,), 0, HEIGHT_LAYERS), jax.random.fold_in(splits[4], 1), 0, HEIGHT_LAYERS - 1).astype(jnp.int32),
        "obs_value": centred(splits[5], (NOBS,), 1.0, 6.0, jnp.float32),
        "obs_rinv": jnp.clip(jnp.exp(jax.random.uniform(splits[6], (NOBS,), jnp.float32, math.log(2.0), math.log(32.0))), 2.0, 32.0),
        "obs_index": draw_obs_index(jax.random.fold_in(splits[9], 71), 0),
        "obs_weight": touch_ends(jax.random.randint(splits[8], (BPT, N_TILE, NOBS_LOC), 0, 4), jax.random.fold_in(splits[8], 1), 0, 3).astype(jnp.int32),
    }


def substep(system_fields, coefficients, neighbours):
    tendency = jnp.zeros_like(system_fields)
    for column in range(6):
        shifted = jnp.take(system_fields, neighbours[column], axis=2)
        tendency = tendency + coefficients[column] * (shifted - system_fields)
    return system_fields + tendency

def ensemble_weights(window, list_slots, levels, global_slots, obs_value, obs_rinv):
    highest = lax.Precision.HIGHEST
    window_mean = lax.optimization_barrier(jnp.mean(window.astype(jnp.float32), axis=0))
    picked = jnp.take(window, list_slots, axis=1).astype(jnp.float32)
    local_pert = (picked - window_mean[list_slots]).astype(jnp.bfloat16)
    weighting = obs_rinv[global_slots] * (levels.astype(jnp.float32) / 3.0)
    departure = obs_value[global_slots] - window_mean[list_slots]
    weighted = (local_pert.astype(jnp.float32) * weighting).astype(jnp.bfloat16)
    wide_weighted = weighted.astype(jnp.float32)
    wide_pert = local_pert.astype(jnp.float32)
    gram_matrix = jnp.einsum('kbo,jbo->bkj', wide_weighted, wide_pert, precision=highest)
    drive_term = jnp.einsum('kbo,bo->bk', wide_weighted, departure, precision=highest)
    members = gram_matrix.shape[1]
    trace_scale = members - 1.0 + jnp.trace(gram_matrix, axis1=1, axis2=2)
    identity = jnp.eye(members, dtype=jnp.float32)
    approx = (gram_matrix + (members - 1.0) * identity) / trace_scale[:, None, None]
    inverse_root = jnp.broadcast_to(identity, gram_matrix.shape)
    for repeat in range(NS_ITERS):
        factor = 1.5 * identity - 0.5 * jnp.einsum('bij,bjk->bik', inverse_root, approx, precision=highest)
        approx = jnp.einsum('bij,bjk->bik', approx, factor, precision=highest)
        inverse_root = jnp.einsum('bij,bjk->bik', factor, inverse_root, precision=highest)
    inner_term = jnp.einsum('bij,bj->bi', inverse_root, drive_term, precision=highest)
    mean_shift = jnp.einsum('bij,bj->bi', inverse_root, inner_term, precision=highest) / trace_scale[:, None]
    result = jnp.sqrt(members - 1.0) * inverse_root / jnp.sqrt(trace_scale)[:, None, None] + mean_shift[:, :, None]
    return result.astype(jnp.bfloat16)

def updated_sites(patch_prediction, coefficient_matrix):
    sample_size, layer_number, profile_sum = patch_prediction.shape
    blocks = coefficient_matrix.shape[0]
    sample_average = lax.optimization_barrier(jnp.mean(patch_prediction.astype(jnp.float32), axis=0))
    sample_anomaly = (patch_prediction.astype(jnp.float32) - sample_average).astype(jnp.bfloat16)
    shaped = sample_anomaly.reshape(sample_size, layer_number, blocks, profile_sum // blocks).astype(jnp.float32)
    mixed_sum = jnp.einsum('jlbc,bjk->klbc', shaped, coefficient_matrix.astype(jnp.float32), precision=lax.Precision.HIGHEST)
    return (mixed_sum.reshape(sample_size, layer_number, profile_sum) + sample_average).astype(jnp.bfloat16)

def reference(fields, coefficients, neighbours, obs_cell, obs_level, obs_value, obs_rinv, obs_index, obs_weight):

    def integrate_dynamics(group):
        system_fields = substep(substep(group, coefficients, neighbours), coefficients, neighbours)
        return system_fields.astype(jnp.bfloat16)
    patch_sorted = fields.reshape(SAMPLE_SIZE // 8, 8, HEIGHT_LAYERS, MESH_SITES_ALL)
    propagate_once = lax.map(integrate_dynamics, patch_sorted).reshape(SAMPLE_SIZE, HEIGHT_LAYERS, MESH_SITES_ALL)
    obs_tile = jnp.arange(NOBS, dtype=jnp.int32) // NOBS_T
    linear_offset = obs_level * MESH_SITES_ALL + obs_tile * PATCH_SITES + obs_cell
    background_readings = jnp.take(propagate_once.reshape(SAMPLE_SIZE, HEIGHT_LAYERS * MESH_SITES_ALL), linear_offset, axis=1)

    def tile_update(patch_location):
        window_index = (patch_location * NOBS_T - NOBS_T + NOBS + jnp.arange(3 * NOBS_T, dtype=jnp.int32)) % NOBS
        window = jnp.take(background_readings, window_index, axis=1)
        list_slots = jnp.take(obs_index, patch_location, axis=1)
        levels = jnp.take(obs_weight, patch_location, axis=1)
        global_slots = jnp.take(window_index, list_slots)
        coefficient_matrix = ensemble_weights(window, list_slots, levels, global_slots, obs_value, obs_rinv)
        patch_prediction = lax.dynamic_slice_in_dim(propagate_once, patch_location * PATCH_SITES, PATCH_SITES, axis=2)
        return updated_sites(patch_prediction, coefficient_matrix)
    tile_fields = lax.map(tile_update, jnp.arange(N_TILE, dtype=jnp.int32))
    return jnp.transpose(tile_fields, (1, 2, 0, 3)).reshape(SAMPLE_SIZE, HEIGHT_LAYERS, MESH_SITES_ALL)
```

```python
import functools

import jax
import jax.numpy as jnp
from jax import lax
from jax.experimental import pallas as pl
from jax.experimental.pallas import tpu as pltpu
from jax.sharding import PartitionSpec as P

HALO = 32
NS_ITERS = 8
LANES = 128
F32 = jnp.float32
BF16 = jnp.bfloat16
VMEM_LIMIT = 48 * 1024 * 1024

NN = (((1,), (0,)), ((), ()))
NT = (((1,), (1,)), ((), ()))
TN = (((0,), (0,)), ((), ()))


def dot(a, b, dims=NN):
    return lax.dot_general(a, b, dims, preferred_element_type=F32)


def split2(x):
    high = x.astype(BF16)
    return high, (x - high.astype(F32)).astype(BF16)


def split3(x):
    high = x.astype(BF16)
    rest = x - high.astype(F32)
    middle = rest.astype(BF16)
    return high, middle, (rest - middle.astype(F32)).astype(BF16)


def iota(shape, dim):
    return lax.broadcasted_iota(jnp.int32, shape, dim)


def is_odd_tile():
    return lax.axis_index("tile") % 2 == 1


def message_rows(field_rows):
    names = ("coef_high", "coef_low", "offset", "list_high", "list_low")
    return {name: field_rows + 16 * place for place, name in enumerate(names)}


def pack_kernel(
    left_ref, right_ref, coef_ref, nbr_ref, index_ref, weight_ref, a_ref, b_ref, lists_ref, offset_ref, *, tiles
):
    columns = coef_ref.shape[1]
    half = left_ref.shape[0] // 2
    rows = message_rows(half)
    odd = is_odd_tile()
    total = columns * tiles
    lane = iota((half, LANES), 1)
    left = jnp.where(lane < 64, left_ref[:half, :], pltpu.roll(left_ref[half:, :], 64, axis=1))
    right = jnp.where(lane < 64, pltpu.roll(right_ref[:half, :], 64, axis=1), right_ref[half:, :])
    a_ref[:half, :] = jnp.where(odd, right, left).astype(BF16)
    b_ref[:half, :] = jnp.where(odd, left, right).astype(BF16)

    place = lax.axis_index("tile") * columns + iota((6, columns), 1)
    offset = nbr_ref[...] - place
    offset = jnp.where(offset > HALO, offset - total, offset)
    offset = jnp.where(offset < -HALO, offset + total, offset).astype(F32)
    offset_ref[...] = jnp.zeros_like(offset_ref)
    offset_ref[:6, :] = offset
    coef_high, coef_low = split2(coef_ref[...])
    blank = jnp.zeros((16 - 6, LANES), F32)
    for name, value in (
        ("coef_high", coef_high.astype(F32)),
        ("coef_low", coef_low.astype(F32)),
        ("offset", offset),
    ):
        first = jnp.concatenate([value[:, :LANES], blank], axis=0)
        last = jnp.concatenate([value[:, columns - LANES :], blank], axis=0)
        start = rows[name]
        a_ref[start : start + 16, :] = jnp.where(odd, last, first).astype(BF16)
        b_ref[start : start + 16, :] = jnp.where(odd, first, last).astype(BF16)

    blocks = index_ref.shape[0]
    blank = jnp.zeros((16 - blocks, LANES), F32)
    index = index_ref[:, 0, :]
    list_high = jnp.concatenate([(index // 64).astype(F32), blank], axis=0).astype(BF16)
    list_low = jnp.concatenate([(index % 64).astype(F32), blank], axis=0).astype(BF16)
    weight = jnp.concatenate([weight_ref[:, 0, :].astype(F32), blank], axis=0).astype(BF16)
    for ref in (a_ref, b_ref):
        ref[rows["list_high"] : rows["list_high"] + 16, :] = list_high
        ref[rows["list_low"] : rows["list_low"] + 16, :] = list_low
    lists_ref[0:16, :] = list_high
    lists_ref[16:32, :] = list_low
    lists_ref[32:48, :] = weight


def fill_band(coefs, offsets, high_ref, low_ref, row, lane):
    spot = iota((LANES + 2 * HALO, LANES), 0)
    own = iota((LANES + 2 * HALO, LANES), 1) + HALO
    band = jnp.where(spot == own, 1.0 - jnp.sum(coefs, axis=0, keepdims=True), 0.0)
    target = iota(offsets.shape, 1) + HALO + offsets.astype(jnp.int32)
    for j in range(6):
        band = band + jnp.where(spot == target[j : j + 1, :], coefs[j : j + 1, :], 0.0)
    high, low = split2(band)
    high_ref[row : row + LANES + 2 * HALO, lane : lane + LANES] = high
    low_ref[row : row + LANES + 2 * HALO, lane : lane + LANES] = low


def forecast_kernel(
    *refs,
    groups,
):
    field_refs = refs[:groups]
    (
    a_ref,
    b_ref,
    coef_ref,
    offset_ref,
    out_ref,
    low_halo,
    high_halo,
    u_high,
    u_low,
    first_high,
    first_low,
    second_high,
    second_low,
    ) = refs[groups:]
    levels, members, columns = out_ref.shape
    half = low_halo.shape[0]
    rows = message_rows(half)
    odd = is_odd_tile()

    def side(start, count):
        a = a_ref[start : start + count, :].astype(F32)
        b = b_ref[start : start + count, :].astype(F32)
        return jnp.where(odd, b, a), jnp.where(odd, a, b)

    low, high = side(0, half)
    low_halo[...] = low
    high_halo[...] = high
    for level in range(levels):
        top = level * members
        mid = top + members // 2
        for group, ref in enumerate(field_refs):
            lane = group * LANES
            own_high, own_low = split2(ref[pl.ds(level, members, stride=levels), :])
            u_high[top : top + members, LANES + lane : 2 * LANES + lane] = own_high
            u_low[top : top + members, lane : lane + LANES] = own_low
        low = low_halo[pl.ds(level, members // 2, stride=levels), :]
        u_high[top:mid, 0:LANES] = pltpu.roll(low, 64, axis=1).astype(BF16)
        u_high[mid : top + members, 0:LANES] = low.astype(BF16)
        high = high_halo[pl.ds(level, members // 2, stride=levels), :]
        u_high[top:mid, LANES + columns :] = high.astype(BF16)
        u_high[mid : top + members, LANES + columns :] = pltpu.roll(high, 64, axis=1).astype(BF16)

    def edges(name):
        low, high = side(rows[name], 16)
        return low[:8, :], high[:8, :]

    blank = jnp.zeros((2, columns), F32)
    own_coef = jnp.concatenate([coef_ref[...], blank], axis=0)
    coef_high = edges("coef_high")
    coef_low = edges("coef_low")
    offset = edges("offset")
    pad = jnp.zeros((8, LANES), F32)
    coef = jnp.concatenate(
        [coef_high[0] + coef_low[0], own_coef, coef_high[1] + coef_low[1], pad], axis=1
    )
    reach = jnp.concatenate([offset[0], offset_ref[...], offset[1], pad], axis=1)
    wide = coef.shape[1]
    moved_coef = pltpu.roll(coef, wide - (LANES - HALO), axis=1)
    moved_reach = pltpu.roll(reach, wide - (LANES - HALO), axis=1)
    for ref in (first_high, first_low, second_high, second_low):
        ref[...] = jnp.zeros_like(ref)
    for group in range(columns // LANES + 1):
        lane = group * LANES
        fill_band(
            moved_coef[:, lane : lane + LANES],
            moved_reach[:, lane : lane + LANES],
            first_high,
            first_low,
            lane + 64,
            lane,
        )
    for group in range(columns // LANES):
        lane = group * LANES
        fill_band(
            coef[:, LANES + lane : 2 * LANES + lane],
            reach[:, LANES + lane : 2 * LANES + lane],
            second_high,
            second_low,
            lane,
            lane,
        )
    for start in range(0, columns, 256):
        f_high = first_high[start : start + 512, start : start + 384]
        f_low = first_low[start : start + 512, start : start + 384]
        s_high = second_high[start : start + 384, start : start + 256]
        s_low = second_low[start : start + 384, start : start + 256]
        both = dot(f_high, s_high) + (dot(f_high, s_low) + dot(f_low, s_high))
        both_high, both_low = split2(both)
        own_from = max(start, LANES)
        own_to = min(start + 512, LANES + columns)
        window = u_high[:, start : start + 512]
        result = dot(window, both_high) + (
            dot(window, both_low)
            + dot(
                u_low[:, own_from - LANES : own_to - LANES],
                both_high[own_from - start : own_to - start, :],
            )
        )
        for level in range(levels):
            out_ref[level, :, start : start + 256] = result[
                level * members : (level + 1) * members, :
            ].astype(BF16)


def gather_lists(own_ref, other_refs, start, blocks):
    parts = [own_ref[start : start + 16, :].astype(F32)]
    parts += [ref[...].astype(F32) for ref in other_refs]
    return jnp.concatenate([part[b : b + 1, :] for part in parts for b in range(blocks)], axis=1)


def read_places(table_ref, slot):
    wide = slot.shape[1]
    valid = (slot >= 0) & (slot < 16 * LANES)
    slot = jnp.where(valid, slot, 0)
    one = jnp.where(iota((LANES, wide), 0) == slot % LANES, 1.0, 0.0).astype(BF16)
    found = dot(table_ref[...], one)
    pick = iota((16, wide), 0) == slot // LANES
    values = [
        jnp.sum(jnp.where(pick, found[16 * k : 16 * k + 16, :], 0.0), axis=0, keepdims=True)
        for k in range(3)
    ]
    column = (values[1] * 16.0 + values[2]).astype(jnp.int32)
    return values[0].astype(jnp.int32), jnp.where(valid, column, -1)


def make_table(cell_ref, level_ref, table):
    cell = cell_ref[...]
    table[0:16, :] = level_ref[...].astype(F32).astype(BF16)
    table[16:32, :] = (cell // 16).astype(F32).astype(BF16)
    table[32:48, :] = (cell % 16).astype(F32).astype(BF16)


def read_forecast(field, level, column, out_ref, lane):
    members = out_ref.shape[0]
    wide = level.shape[1]
    one = jnp.where(iota((field.shape[1], wide), 0) == column, 1.0, 0.0).astype(BF16)
    found = dot(field, one)
    total = jnp.zeros((members, wide), F32)
    for l in range(field.shape[0] // members):
        total = total + jnp.where(level == l, found[l * members : (l + 1) * members, :], 0.0)
    out_ref[:, lane : lane + wide] = total.astype(BF16)


def neighbour_kernel(field_ref, a_ref, b_ref, *refs, others, blocks):
    other_refs = refs[:others]
    cell_ref, level_ref, ra_ref, rb_ref, table = refs[others:]
    levels, members, columns = field_ref.shape
    half = a_ref.shape[0] - 80
    rows = message_rows(half)
    odd = is_odd_tile()
    obs = 16 * LANES
    make_table(cell_ref, level_ref, table)
    field = field_ref[...].reshape(levels * members, columns)
    for turn, (ref, out_ref) in enumerate(((a_ref, ra_ref), (b_ref, rb_ref))):
        base = 32 * turn
        high = gather_lists(ref, [r.at[base : base + 16, :] for r in other_refs], rows["list_high"], blocks)
        low = gather_lists(ref, [r.at[base + 16 : base + 32, :] for r in other_refs], rows["list_low"], blocks)
        index = (high * 64.0 + low).astype(jnp.int32)
        skip = jnp.where(odd, 0, 2 * obs) if turn == 0 else jnp.where(odd, 2 * obs, 0)
        level, column = read_places(table, index - skip)
        for lane in range(0, index.shape[1], 256):
            read_forecast(
                field, level[:, lane : lane + 256], column[:, lane : lane + 256], out_ref, lane
            )


def own_kernel(field_ref, lists_ref, *refs, others, blocks, tiles):
    other_refs = refs[:others]
    cell_ref, level_ref, value_ref, rinv_ref, r_ref, weight_ref, target_ref, table = refs[others:]
    levels, members, columns = field_ref.shape
    obs = 16 * LANES
    make_table(cell_ref, level_ref, table)
    field = field_ref[...].reshape(levels * members, columns)

    def gathered(place):
        return gather_lists(
            lists_ref,
            [r.at[64 + 16 * place : 80 + 16 * place, :] for r in other_refs],
            16 * place,
            blocks,
        )

    index = (gathered(0) * 64.0 + gathered(1)).astype(jnp.int32)
    weight = gathered(2)
    wide = index.shape[1]
    level, column = read_places(table, index - obs)
    for lane in range(0, wide, 256):
        read_forecast(field, level[:, lane : lane + 256], column[:, lane : lane + 256], r_ref, lane)

    tile = lax.axis_index("tile")
    starts = [((tile + tiles + shift) % tiles) * 16 for shift in (-1, 0, 1)]
    one = jnp.where(iota((LANES, wide), 0) == index % LANES, 1.0, 0.0).astype(BF16)
    pick = iota((48, wide), 0) == index // LANES

    def looked_up(ref):
        window = jnp.concatenate([ref[pl.ds(pl.multiple_of(s, 16), 16), :] for s in starts], axis=0)
        high, middle, low = [dot(piece, one) for piece in split3(window)]
        return jnp.sum(jnp.where(pick, (high + middle) + low, 0.0), axis=0, keepdims=True)

    weight_ref[...] = jnp.broadcast_to(looked_up(rinv_ref) * (weight / 3.0), weight_ref.shape)
    target_ref[...] = jnp.broadcast_to(looked_up(value_ref), target_ref.shape)


def doubled(high, low):
    top = jnp.concatenate([high, low], axis=1)
    bottom = jnp.concatenate([high, jnp.zeros_like(low)], axis=1)
    return jnp.concatenate([top, bottom], axis=0)


def product(left, right):
    both = dot(left, right)
    wide = both.shape[1] // 2
    return both[:, :wide] + both[:, wide:]


def joined(pair):
    return jnp.concatenate(pair, axis=1)


def weights_kernel(*refs, others):
    r_refs = refs[: others + 1]
    weight_ref, target_ref, out_ref, pert, weighted, gram_right, hat, inner, outer = refs[others + 1 :]
    members, wide = r_refs[0].shape
    blocks = wide // LANES
    share = blocks // (others + 1)
    ensemble = members * (others + 1)
    free = ensemble - 1.0

    parts = [r_refs[0][...].astype(F32)]
    for k in range(others):
        other = r_refs[k + 1][...].astype(F32)
        turn = ((k + 1) * share * LANES) % wide
        parts.append(jnp.concatenate([other[:, wide - turn :], other[:, : wide - turn]], axis=1))
    total = sum(jnp.sum(part, axis=0, keepdims=True) for part in parts)
    mean = total * (1.0 / ensemble)
    weight = weight_ref[0:1, :]
    for k, part in enumerate(parts):
        rounded = (part - mean).astype(BF16)
        pert[k * members : (k + 1) * members, :] = rounded
        weighted[k * members : (k + 1) * members, :] = (rounded.astype(F32) * weight).astype(BF16)
    departure = target_ref[0:1, :] - mean

    eye = iota((LANES, LANES), 0) == iota((LANES, LANES), 1)

    def spread(value):
        return jnp.where(eye, value, 0.0)

    scales, xs, zs = [], [], []
    for b in range(blocks):
        lanes = slice(b * LANES, (b + 1) * LANES)
        gram = dot(weighted[:, lanes], pert[:, lanes], TN)
        trace = jnp.sum(jnp.sum(spread(gram), axis=0, keepdims=True), axis=1, keepdims=True)
        scale = jnp.broadcast_to(1.0 / (free + trace), (1, LANES))
        gram = gram * scale
        x = free * scale
        right = doubled(*split2(gram))
        gram_right[b] = right
        m = 1.5 - 0.5 * x
        factor = spread(1.5 - 0.5 * x) - 0.5 * gram
        v = m * x
        inner_next = product(
            joined(split2(factor)), doubled(*split2(factor - spread(0.5 * x)))
        ) - spread(0.5 * v)
        inner[b] = inner_next
        x = m * v
        hat[b] = spread(x) + product(joined(split2(inner_next)), right)
        outer[b] = spread(jnp.full((1, LANES), -0.5, F32))
        scales.append(scale)
        xs.append(x)
        zs.append(m)

    def step(_, carry):
        xs, zs = carry
        next_xs, next_zs = [], []
        for b in range(blocks):
            x, z = xs[b], zs[b]
            m = 1.5 - 0.5 * x
            v = m * x
            factor = spread(jnp.full((1, LANES), 1.5, F32)) - 0.5 * hat[b]
            f_high, f_low = split2(factor)
            left = joined((f_high, f_low))
            inside = inner[b]
            i_high, i_low = split2(inside)
            o_high, o_low = split2(outer[b])
            right_high = joined((i_high, o_high))
            both = dot(left, jnp.concatenate([right_high, right_high], axis=0)) + dot(
                f_high, joined((i_low, o_low))
            )
            half = both[:, :LANES] - (0.5 * x) * inside
            outer[b] = both[:, LANES:] - (0.5 * z) * inside
            new = product(left, doubled(*split2(half))) - (0.5 * v) * inside
            inner[b] = new
            x = m * v
            hat[b] = spread(x) + product(joined(split2(new)), gram_right[b])
            next_xs.append(x)
            next_zs.append(m * z)
        return tuple(next_xs), tuple(next_zs)

    xs, zs = lax.fori_loop(1, NS_ITERS - 1, step, (tuple(xs), tuple(zs)))

    own = iota((members, ensemble), 0) == iota((members, ensemble), 1)
    for b in range(blocks):
        lanes = slice(b * LANES, (b + 1) * LANES)
        x, z, scale = xs[b], zs[b], scales[b]
        factor = spread(jnp.full((1, LANES), 1.5, F32)) - 0.5 * hat[b]
        last = product(joined(split2(factor)), doubled(*split2(outer[b]))) - (0.5 * z) * inner[b]
        z = (1.5 - 0.5 * x) * z
        last_high, last_low = split2(last)
        last_right = doubled(last_high, last_low)
        row = jnp.broadcast_to(departure[:, lanes], (8, LANES))
        for _ in range(2):
            moved = product(joined(split2(row)), last_right)
            row = z * row + product(joined(split2(moved)), gram_right[b])
        row = row * scale
        root = jnp.sqrt(free * scale)
        mine = pert[:members, lanes]
        core = dot(joined((mine, mine)), jnp.concatenate([last_high, last_low], axis=0))
        core = core * (root * scale)
        all_rows = joined(split2(jnp.concatenate([core, row, row], axis=0)))
        block = weighted[:, lanes]
        found = dot(all_rows, joined((block, block)), NT)
        diagonal = jnp.where(own, (root * z)[:, 0:1], 0.0)
        out_ref[b] = (found[:members, :] + found[members : members + 1, :] + diagonal).astype(BF16)


def update_kernel(*refs, others):
    field_refs = refs[: others + 1]
    weight_ref, out_ref, stage = refs[others + 1 :]
    levels, members, columns = field_refs[0].shape
    blocks = weight_ref.shape[0]
    width = columns // blocks
    per = LANES // width
    ensemble = members * (others + 1)
    first = lax.axis_index("mem") * (blocks // (others + 1))
    lane = iota((members, LANES), 1)
    for group in range(columns // LANES):
        lanes = slice(group * LANES, (group + 1) * LANES)
        left = jnp.concatenate(
            [weight_ref[(group * per + k + blocks - first) % blocks] for k in range(per)], axis=0
        )
        for level in range(levels):
            parts = [ref[level, :, lanes].astype(F32) for ref in field_refs]
            total = sum(jnp.sum(part, axis=0, keepdims=True) for part in parts)
            mean = total * (1.0 / ensemble)
            moved = jnp.concatenate([(part - mean).astype(BF16) for part in parts], axis=0)
            found = dot(left, moved)
            result = found[:members, :]
            for k in range(1, per):
                result = jnp.where(lane < k * width, result, found[k * members : (k + 1) * members, :])
            stage[group, pl.ds(level, members, stride=levels), :] = result + mean
        out_ref[:, :, lanes] = stage[group].reshape(members, levels, LANES).astype(BF16)


def vmem():
    return pl.BlockSpec(memory_space=pltpu.VMEM)


def group_spec(rows, group):
    return pl.BlockSpec((rows, LANES), lambda i: (0, group))


def call(kernel, outs, inputs, scratch=(), in_specs=None, flops=0):
    return pl.pallas_call(
        kernel,
        grid=(1,),
        out_shape=outs,
        in_specs=in_specs or [vmem()] * len(inputs),
        out_specs=[vmem()] * len(outs),
        scratch_shapes=list(scratch),
        compiler_params=pltpu.CompilerParams(vmem_limit_bytes=VMEM_LIMIT),
        cost_estimate=pl.CostEstimate(flops=flops, bytes_accessed=4 << 20, transcendentals=0),
    )(*inputs)


def shards(
    fields,
    coefficients,
    neighbours,
    obs_cell,
    obs_level,
    obs_value,
    obs_rinv,
    obs_index,
    obs_weight,
):
    tiles = lax.axis_size("tile")
    sharers = lax.axis_size("mem")
    others = sharers - 1
    members, levels, columns = fields.shape
    blocks = obs_index.shape[0]
    entries = blocks * sharers * LANES
    half = members * levels // 2
    message = jax.ShapeDtypeStruct((half + 80, LANES), BF16)
    even_pairs = []
    odd_pairs = []
    for i in range(0, tiles, 2):
        even_pairs += [(i, i + 1), (i + 1, i)]
        low, high = i + 1, (i + 2) % tiles
        odd_pairs += [(low, high), (high, low)]
    turns = [[((i + r) % sharers, i) for i in range(sharers)] for r in range(1, sharers)]

    flat = fields.reshape(members * levels, columns)
    groups = columns // LANES
    a, b, lists, offset = call(
        functools.partial(pack_kernel, tiles=tiles),
        [
            message,
            message,
            jax.ShapeDtypeStruct((48, LANES), BF16),
            jax.ShapeDtypeStruct((8, columns), F32),
        ],
        [flat, flat, coefficients, neighbours, obs_index, obs_weight],
        in_specs=[group_spec(members * levels, 0), group_spec(members * levels, groups - 1)]
        + [vmem()] * 4,
    )
    from_a = lax.ppermute(a, "tile", odd_pairs)
    from_b = lax.ppermute(b, "tile", even_pairs)
    passed = jnp.concatenate([from_a[half + 48 :], from_b[half + 48 :], lists], axis=0)
    passed = [lax.ppermute(passed, "mem", turn) for turn in turns]

    wide = columns + 2 * LANES
    mid = columns + LANES
    (forecast,) = call(
        functools.partial(forecast_kernel, groups=groups),
        [jax.ShapeDtypeStruct((levels, members, columns), BF16)],
        [flat] * groups + [from_a, from_b, coefficients, offset],
        [
            pltpu.VMEM((half, LANES), F32),
            pltpu.VMEM((half, LANES), F32),
            pltpu.VMEM((members * levels, wide), BF16),
            pltpu.VMEM((members * levels, columns), BF16),
            pltpu.VMEM((wide + LANES, mid), BF16),
            pltpu.VMEM((wide + LANES, mid), BF16),
            pltpu.VMEM((mid + LANES, columns), BF16),
            pltpu.VMEM((mid + LANES, columns), BF16),
        ],
        in_specs=[group_spec(members * levels, group) for group in range(groups)] + [vmem()] * 4,
        flops=4 << 30,
    )
    cell = obs_cell.reshape(16, LANES)
    level = obs_level.reshape(16, LANES)
    reading = jax.ShapeDtypeStruct((members, entries), BF16)
    table = pltpu.VMEM((48, LANES), BF16)
    to_a, to_b = call(
        functools.partial(neighbour_kernel, others=others, blocks=blocks),
        [reading, reading],
        [forecast, from_a, from_b, *passed, cell, level],
        [table],
        flops=2 << 30,
    )
    back_a = lax.ppermute(to_a, "tile", odd_pairs)
    back_b = lax.ppermute(to_b, "tile", even_pairs)
    vector = jax.ShapeDtypeStruct((8, entries), F32)
    own, weight, target = call(
        functools.partial(own_kernel, others=others, blocks=blocks, tiles=tiles),
        [reading, vector, vector],
        [
            forecast,
            lists,
            *passed,
            cell,
            level,
            obs_value.reshape(-1, LANES),
            obs_rinv.reshape(-1, LANES),
        ],
        [table],
        flops=2 << 30,
    )
    readings = own + back_a + back_b
    readings = [readings] + [lax.ppermute(readings, "mem", turn) for turn in turns]
    forecasts = [forecast] + [lax.ppermute(forecast, "mem", turn) for turn in turns]
    ensemble = members * sharers
    total = blocks * sharers
    square = pltpu.VMEM((total, LANES, LANES), F32)
    (weights,) = call(
        functools.partial(weights_kernel, others=others),
        [jax.ShapeDtypeStruct((total, members, ensemble), BF16)],
        [*readings, weight, target],
        [
            pltpu.VMEM((ensemble, entries), BF16),
            pltpu.VMEM((ensemble, entries), BF16),
            pltpu.VMEM((total, 2 * LANES, 2 * LANES), BF16),
            square,
            square,
            square,
        ],
        flops=8 << 30,
    )
    (analysis,) = call(
        functools.partial(update_kernel, others=others),
        [jax.ShapeDtypeStruct((members, levels, columns), BF16)],
        [*forecasts, weights],
        [pltpu.VMEM((columns // LANES, members * levels, LANES), F32)],
        flops=1 << 30,
    )
    return analysis


def solution(mesh):
    in_specs = (
        P("mem", None, "tile"),
        P(None, "tile"),
        P(None, "tile"),
        P("tile"),
        P("tile"),
        P(),
        P(),
        P("mem", "tile", None),
        P("mem", "tile", None),
    )
    out_specs = P("mem", None, "tile")
    return jax.shard_map(shards, mesh=mesh, in_specs=in_specs, out_specs=out_specs, check_vma=False)
```

```python
import functools

import jax
import jax.numpy as jnp
from jax import lax
from jax.experimental import pallas as pl
from jax.experimental.pallas import tpu as pltpu
from jax.sharding import PartitionSpec as P

HALO = 32
NS_ITERS = 8
LANES = 128
F32 = jnp.float32
BF16 = jnp.bfloat16
VMEM_LIMIT = 48 * 1024 * 1024

NN = (((1,), (0,)), ((), ()))
NT = (((1,), (1,)), ((), ()))
TN = (((0,), (0,)), ((), ()))


def dot(a, b, dims=NN):
    return lax.dot_general(a, b, dims, preferred_element_type=F32)


def split2(x):
    high = x.astype(BF16)
    return high, (x - high.astype(F32)).astype(BF16)


def split3(x):
    high = x.astype(BF16)
    rest = x - high.astype(F32)
    middle = rest.astype(BF16)
    return high, middle, (rest - middle.astype(F32)).astype(BF16)


def iota(shape, dim):
    return lax.broadcasted_iota(jnp.int32, shape, dim)


def is_odd_tile():
    return lax.axis_index("tile") % 2 == 1


def message_rows(field_rows):
    names = ("coef_high", "coef_low", "offset", "list_high", "list_low")
    return {name: field_rows + 16 * place for place, name in enumerate(names)}


def pack_kernel(
    field_hbm,
    coef_hbm,
    nbr_hbm,
    index_hbm,
    weight_hbm,
    a_ref,
    b_ref,
    lists_ref,
    offset_ref,
    left_ref,
    right_ref,
    coef_ref,
    nbr_ref,
    index_ref,
    weight_ref,
    sems,
    *,
    tiles,
):
    columns = coef_ref.shape[1]
    levels = 8
    half = left_ref.shape[0] // 2
    members = half // levels
    rows = message_rows(half)
    odd = is_odd_tile()
    total = columns * tiles
    copies = [
        pltpu.make_async_copy(source, target, sems.at[k])
        for k, (source, target) in enumerate(
            (
                (field_hbm.at[:, 0:LANES], left_ref),
                (field_hbm.at[:, columns - LANES : columns], right_ref),
                (coef_hbm, coef_ref),
                (nbr_hbm, nbr_ref),
                (index_hbm, index_ref),
                (weight_hbm, weight_ref),
            )
        )
    ]
    for copy in copies:
        copy.start()
    for copy in copies[2:]:
        copy.wait()

    place = lax.axis_index("tile") * columns + iota((6, columns), 1)
    offset = nbr_ref[...] - place
    offset = jnp.where(offset > HALO, offset - total, offset)
    offset = jnp.where(offset < -HALO, offset + total, offset).astype(F32)
    offset_ref[...] = jnp.zeros_like(offset_ref)
    offset_ref[:6, :] = offset
    coef_high, coef_low = split2(coef_ref[...])
    blank = jnp.zeros((16 - 6, LANES), F32)
    for name, value in (
        ("coef_high", coef_high.astype(F32)),
        ("coef_low", coef_low.astype(F32)),
        ("offset", offset),
    ):
        first = jnp.concatenate([value[:, :LANES], blank], axis=0)
        last = jnp.concatenate([value[:, columns - LANES :], blank], axis=0)
        start = rows[name]
        a_ref[start : start + 16, :] = jnp.where(odd, last, first).astype(BF16)
        b_ref[start : start + 16, :] = jnp.where(odd, first, last).astype(BF16)

    blocks = index_ref.shape[0]
    blank = jnp.zeros((16 - blocks, LANES), F32)
    index = index_ref[:, 0, :]
    list_high = jnp.concatenate([(index // 64).astype(F32), blank], axis=0).astype(BF16)
    list_low = jnp.concatenate([(index % 64).astype(F32), blank], axis=0).astype(BF16)
    weight = jnp.concatenate([weight_ref[:, 0, :].astype(F32), blank], axis=0).astype(BF16)
    for ref in (a_ref, b_ref):
        ref[rows["list_high"] : rows["list_high"] + 16, :] = list_high
        ref[rows["list_low"] : rows["list_low"] + 16, :] = list_low
    lists_ref[0:16, :] = list_high
    lists_ref[16:32, :] = list_low
    lists_ref[32:48, :] = weight

    for copy in copies[:2]:
        copy.wait()
    lane = iota((members, LANES), 1)
    for level in range(levels):
        top = pl.ds(level, members, stride=levels)
        low = pl.ds(level + half, members, stride=levels)
        spot = slice(level * members, (level + 1) * members)
        left = jnp.where(lane < 64, left_ref[top, :], pltpu.roll(left_ref[low, :], 64, axis=1))
        right = jnp.where(lane < 64, pltpu.roll(right_ref[top, :], 64, axis=1), right_ref[low, :])
        a_ref[spot, :] = jnp.where(odd, right, left).astype(BF16)
        b_ref[spot, :] = jnp.where(odd, left, right).astype(BF16)


def band(coefs, offsets):
    shape = (LANES + 2 * HALO, LANES)
    spot = iota(shape, 0)
    result = jnp.where(
        spot == iota(shape, 1) + HALO, 1.0 - jnp.sum(coefs, axis=0, keepdims=True), 0.0
    )
    target = iota(offsets.shape, 1) + HALO + offsets.astype(jnp.int32)
    for j in range(6):
        result = result + jnp.where(spot == target[j : j + 1, :], coefs[j : j + 1, :], 0.0)
    return result


def dot3(left, right):
    return dot(left[0], right[0]) + (dot(left[0], right[1]) + dot(left[1], right[0]))


def padded(value, count):
    return jnp.concatenate([value, jnp.zeros((count, value.shape[1]), value.dtype)], axis=0)


def middle_kernel(*refs, groups):
    field_refs = refs[:groups]
    (
        coef_ref,
        offset_ref,
        out_ref,
        edge_high,
        edge_low,
        part_ref,
        second_ref,
        u_high,
        u_low,
        first_high,
        first_low,
        second_high,
        second_low,
    ) = refs[groups:]
    levels, members, middle = out_ref.shape
    columns = groups * LANES
    coef = padded(coef_ref[...], 2)
    reach = offset_ref[...]
    moved_coef = pltpu.roll(coef, HALO, axis=1)
    moved_reach = pltpu.roll(reach, HALO, axis=1)

    def lanes(value, group):
        return value[:, group * LANES : (group + 1) * LANES]

    firsts = {
        g: split2(band(lanes(moved_coef, g), lanes(moved_reach, g))) for g in range(1, groups)
    }
    seconds = [split2(band(lanes(coef, g), lanes(reach, g))) for g in range(groups)]
    for ref in (first_high, first_low, second_high, second_low):
        ref[...] = jnp.zeros_like(ref)
    for g in range(1, groups):
        row, lane = g * LANES - 64, (g - 1) * LANES
        count = min(LANES + 2 * HALO, columns - row)
        first_high[row : row + count, lane : lane + LANES] = firsts[g][0][:count, :]
        first_low[row : row + count, lane : lane + LANES] = firsts[g][1][:count, :]
    for g in range(1, groups - 1):
        row, lane = (g - 1) * LANES, (g - 1) * LANES
        second_high[row : row + LANES + 2 * HALO, lane : lane + LANES] = seconds[g][0]
        second_low[row : row + LANES + 2 * HALO, lane : lane + LANES] = seconds[g][1]
    both = split2(
        dot3((first_high[...], first_low[...]), (second_high[...], second_low[...]))
    )

    for k, g in enumerate((0, groups - 1)):
        second = [padded(value, 64) for value in seconds[g]]
        for j in range(2):
            second_ref[2 * k + j] = second[j]
        if k == 0:
            part = dot3([value[:128, :] for value in firsts[1]], [value[128:, :] for value in second])
            part_ref[k] = jnp.concatenate([jnp.zeros_like(part), part], axis=0)
        else:
            part_ref[k] = padded(dot3(firsts[g], [value[:128, :] for value in second]), 64)

    lane = iota((members, LANES), 1)
    for level in range(levels):
        spot = slice(level * members, (level + 1) * members)
        for group, ref in enumerate(field_refs):
            own = ref[pl.ds(level, members, stride=levels), :]
            high, low = split2(own)
            u_high[spot, group * LANES : (group + 1) * LANES] = high
            u_low[spot, group * LANES : (group + 1) * LANES] = low
        for pieces, ref in ((u_high, edge_high), (u_low, edge_low)):
            turned = [
                pltpu.roll(pieces[spot, g * LANES : (g + 1) * LANES].astype(F32), 64, axis=1)
                for g in (0, 1, groups - 2, groups - 1)
            ]
            zero = jnp.zeros_like(turned[0])
            ref[0, spot, 0:LANES] = jnp.where(lane < 64, zero, turned[0]).astype(BF16)
            ref[0, spot, LANES:] = jnp.where(lane < 64, turned[0], turned[1]).astype(BF16)
            ref[1, spot, 0:LANES] = jnp.where(lane < 64, turned[2], turned[3]).astype(BF16)
            ref[1, spot, LANES:] = jnp.where(lane < 64, turned[3], zero).astype(BF16)
    result = dot3((u_high[...], u_low[...]), both)
    for level in range(levels):
        out_ref[level] = result[level * members : (level + 1) * members, :].astype(BF16)


def edge_kernel(
    a_ref, b_ref, coef_ref, offset_ref, edge_high, edge_low, part_ref, second_ref, out_ref, u_high
):
    levels, members, _ = out_ref.shape
    columns = coef_ref.shape[1]
    half = members // 2
    rows = message_rows(levels * half)
    odd = is_odd_tile()

    def side(k, start, count):
        a = a_ref[start : start + count, :].astype(F32)
        b = b_ref[start : start + count, :].astype(F32)
        return jnp.where(odd, b, a) if k == 0 else jnp.where(odd, a, b)

    own_coef = padded(coef_ref[...], 2)
    lane8 = iota((8, LANES), 1)
    lane = iota((half, LANES), 1)
    operators = []
    for k in range(2):
        near = side(k, rows["coef_high"], 16)[:8] + side(k, rows["coef_low"], 16)[:8]
        reach = side(k, rows["offset"], 16)[:8]
        if k == 0:
            own = (own_coef[:, :LANES], offset_ref[:, :LANES])
            both = [
                jnp.where(
                    lane8 < HALO, pltpu.roll(x, HALO, axis=1), pltpu.roll(y, HALO, axis=1)
                )
                for x, y in zip((near, reach), own)
            ]
            first = split2(band(*both))
            second = [second_ref[j, :128, :] for j in range(2)]
            fresh = padded(dot3(first, second), 64)
        else:
            own = (own_coef[:, columns - LANES :], offset_ref[:, columns - LANES :])
            both = [
                jnp.where(
                    lane8 < HALO, pltpu.roll(y, HALO, axis=1), pltpu.roll(x, HALO, axis=1)
                )
                for x, y in zip((near, reach), own)
            ]
            first = [value[:128, :] for value in split2(band(*both))]
            second = [second_ref[2 + j, 128:, :] for j in range(2)]
            fresh = dot3(first, second)
            fresh = jnp.concatenate([jnp.zeros_like(fresh), fresh], axis=0)
        operators.append(split2(part_ref[k] + fresh))
    for k in range(2):
        for level in range(levels):
            top = level * members
            halo = side(k, level * half, half)
            other = pltpu.roll(halo, 64, axis=1)
            pair = (halo, other) if k == 0 else (other, halo)
            for j in range(2):
                spot = slice(top + j * half, top + (j + 1) * half)
                if k == 0:
                    own = edge_high[k, spot, 0:LANES].astype(F32)
                    u_high[k, spot, 0:LANES] = jnp.where(lane < 64, pair[j], own).astype(BF16)
                    u_high[k, spot, LANES:] = edge_high[k, spot, LANES:]
                else:
                    own = edge_high[k, spot, LANES:].astype(F32)
                    u_high[k, spot, LANES:] = jnp.where(lane < 64, own, pair[j]).astype(BF16)
                    u_high[k, spot, 0:LANES] = edge_high[k, spot, 0:LANES]
        result = dot3((u_high[k], edge_low[k]), operators[k])
        for level in range(levels):
            out_ref[level, :, k * LANES : (k + 1) * LANES] = result[
                level * members : (level + 1) * members, :
            ].astype(BF16)


def gather_lists(own_ref, other_refs, start, blocks):
    parts = [own_ref[start : start + 16, :].astype(F32)]
    parts += [ref[...].astype(F32) for ref in other_refs]
    return jnp.concatenate([part[b : b + 1, :] for part in parts for b in range(blocks)], axis=1)


def read_places(table_ref, slot):
    wide = slot.shape[1]
    valid = (slot >= 0) & (slot < 16 * LANES)
    slot = jnp.where(valid, slot, 0)
    one = jnp.where(iota((LANES, wide), 0) == slot % LANES, 1.0, 0.0).astype(BF16)
    found = dot(table_ref[...], one)
    pick = iota((16, wide), 0) == slot // LANES
    values = [
        jnp.sum(jnp.where(pick, found[16 * k : 16 * k + 16, :], 0.0), axis=0, keepdims=True)
        for k in range(3)
    ]
    column = (values[1] * 16.0 + values[2]).astype(jnp.int32)
    return values[0].astype(jnp.int32), jnp.where(valid, column, -1)


def make_table(cell_ref, level_ref, table):
    cell = cell_ref[...]
    table[0:16, :] = level_ref[...].astype(F32).astype(BF16)
    table[16:32, :] = (cell // 16).astype(F32).astype(BF16)
    table[32:48, :] = (cell % 16).astype(F32).astype(BF16)


def read_forecast(fields, level, column, out_ref, lane):
    members = out_ref.shape[0]
    wide = level.shape[1]
    middle, edge = fields
    inner = middle.shape[1]
    inside = (column >= LANES) & (column < LANES + inner)
    spot = jnp.where(inside, column - LANES, -1)
    one = jnp.where(iota((inner, wide), 0) == spot, 1.0, 0.0).astype(BF16)
    found = dot(middle, one)
    spot = jnp.where(column < LANES, column, column - inner)
    spot = jnp.where(inside, -1, spot)
    one = jnp.where(iota((2 * LANES, wide), 0) == spot, 1.0, 0.0).astype(BF16)
    found = found + dot(edge, one)
    total = jnp.zeros((members, wide), F32)
    for l in range(middle.shape[0] // members):
        total = total + jnp.where(level == l, found[l * members : (l + 1) * members, :], 0.0)
    out_ref[:, lane : lane + wide] = total.astype(BF16)


def neighbour_kernel(middle_ref, edge_ref, a_ref, b_ref, *refs, others, blocks):
    other_refs = refs[:others]
    cell_ref, level_ref, ra_ref, rb_ref, table = refs[others:]
    half = a_ref.shape[0] - 80
    rows = message_rows(half)
    odd = is_odd_tile()
    obs = 16 * LANES
    make_table(cell_ref, level_ref, table)
    fields = [ref[...].reshape(-1, ref.shape[2]) for ref in (middle_ref, edge_ref)]
    for turn, (ref, out_ref) in enumerate(((a_ref, ra_ref), (b_ref, rb_ref))):
        base = 32 * turn
        high = gather_lists(ref, [r.at[base : base + 16, :] for r in other_refs], rows["list_high"], blocks)
        low = gather_lists(ref, [r.at[base + 16 : base + 32, :] for r in other_refs], rows["list_low"], blocks)
        index = (high * 64.0 + low).astype(jnp.int32)
        skip = jnp.where(odd, 0, 2 * obs) if turn == 0 else jnp.where(odd, 2 * obs, 0)
        level, column = read_places(table, index - skip)
        for lane in range(0, index.shape[1], 256):
            read_forecast(
                fields, level[:, lane : lane + 256], column[:, lane : lane + 256], out_ref, lane
            )


def own_kernel(middle_ref, edge_ref, lists_ref, *refs, others, blocks, tiles):
    other_refs = refs[:others]
    cell_ref, level_ref, value_ref, rinv_ref, r_ref, weight_ref, target_ref, table = refs[others:]
    obs = 16 * LANES
    make_table(cell_ref, level_ref, table)
    fields = [ref[...].reshape(-1, ref.shape[2]) for ref in (middle_ref, edge_ref)]

    def gathered(place):
        return gather_lists(
            lists_ref,
            [r.at[64 + 16 * place : 80 + 16 * place, :] for r in other_refs],
            16 * place,
            blocks,
        )

    index = (gathered(0) * 64.0 + gathered(1)).astype(jnp.int32)
    weight = gathered(2)
    wide = index.shape[1]
    level, column = read_places(table, index - obs)
    for lane in range(0, wide, 256):
        read_forecast(fields, level[:, lane : lane + 256], column[:, lane : lane + 256], r_ref, lane)

    tile = lax.axis_index("tile")
    starts = [((tile + tiles + shift) % tiles) * 16 for shift in (-1, 0, 1)]
    one = jnp.where(iota((LANES, wide), 0) == index % LANES, 1.0, 0.0).astype(BF16)
    pick = iota((48, wide), 0) == index // LANES

    def looked_up(ref):
        window = jnp.concatenate([ref[pl.ds(pl.multiple_of(s, 16), 16), :] for s in starts], axis=0)
        high, middle, low = [dot(piece, one) for piece in split3(window)]
        return jnp.sum(jnp.where(pick, (high + middle) + low, 0.0), axis=0, keepdims=True)

    weight_ref[...] = jnp.broadcast_to(looked_up(rinv_ref) * (weight / 3.0), weight_ref.shape)
    target_ref[...] = jnp.broadcast_to(looked_up(value_ref), target_ref.shape)


def doubled(high, low):
    top = jnp.concatenate([high, low], axis=1)
    bottom = jnp.concatenate([high, jnp.zeros_like(low)], axis=1)
    return jnp.concatenate([top, bottom], axis=0)


def product(left, right):
    both = dot(left, right)
    wide = both.shape[1] // 2
    return both[:, :wide] + both[:, wide:]


def joined(pair):
    return jnp.concatenate(pair, axis=1)


def weights_kernel(*refs, others):
    r_refs = refs[: others + 1]
    weight_ref, target_ref, out_ref, pert, weighted, turned, gram_right, hat, inner, outer = refs[others + 1 :]
    members, wide = r_refs[0].shape
    blocks = wide // LANES
    share = blocks // (others + 1)
    ensemble = members * (others + 1)
    free = ensemble - 1.0

    parts = [r_refs[0][...].astype(F32)]
    for k in range(others):
        other = r_refs[k + 1][...].astype(F32)
        turn = ((k + 1) * share * LANES) % wide
        parts.append(jnp.concatenate([other[:, wide - turn :], other[:, : wide - turn]], axis=1))
    total = sum(jnp.sum(part, axis=0, keepdims=True) for part in parts)
    mean = total * (1.0 / ensemble)
    weight = weight_ref[0:1, :]
    for k, part in enumerate(parts):
        rounded = (part - mean).astype(BF16)
        pert[k * members : (k + 1) * members, :] = rounded
        weighted[k * members : (k + 1) * members, :] = (rounded.astype(F32) * weight).astype(BF16)
    departure = target_ref[0:1, :] - mean

    eye = iota((LANES, LANES), 0) == iota((LANES, LANES), 1)

    def spread(value):
        return jnp.where(eye, value, 0.0)

    scales, xs, zs, grams, lefts, inners = [], [], [], [], [], []
    for b in range(blocks):
        lanes = slice(b * LANES, (b + 1) * LANES)
        turned[b] = weighted[:, lanes].T
    for b in range(blocks):
        lanes = slice(b * LANES, (b + 1) * LANES)
        grams.append(dot(turned[b], pert[:, lanes]))
    for b in range(blocks):
        trace = jnp.sum(jnp.sum(spread(grams[b]), axis=0, keepdims=True), axis=1, keepdims=True)
        scales.append(jnp.broadcast_to(1.0 / (free + trace), (1, LANES)))
    for b in range(blocks):
        gram = grams[b] * scales[b]
        x = free * scales[b]
        gram_right[b] = doubled(*split2(gram))
        m = 1.5 - 0.5 * x
        factor = spread(m) - 0.5 * gram
        v = m * x
        inners.append(
            product(joined(split2(factor)), doubled(*split2(factor - spread(0.5 * x))))
            - spread(0.5 * v)
        )
        xs.append(m * v)
        zs.append(m)
    for b in range(blocks):
        inner[b] = inners[b]
        hat[b] = spread(xs[b]) + product(joined(split2(inners[b])), gram_right[b])
        outer[b] = spread(jnp.full((1, LANES), -0.5, F32))

    def step(_, carry):
        xs, zs = carry
        next_xs, next_zs = [], []
        for base in range(0, blocks, 8):
            group = range(base, min(base + 8, blocks))
            lefts, halves = {}, {}
            for b in group:
                x, z = xs[b], zs[b]
                factor = spread(jnp.full((1, LANES), 1.5, F32)) - 0.5 * hat[b]
                f_high, f_low = split2(factor)
                lefts[b] = joined((f_high, f_low))
                inside = inner[b]
                i_high, i_low = split2(inside)
                o_high, o_low = split2(outer[b])
                right_high = joined((i_high, o_high))
                both = dot(lefts[b], jnp.concatenate([right_high, right_high], axis=0)) + dot(
                    f_high, joined((i_low, o_low))
                )
                halves[b] = both[:, :LANES] - (0.5 * x) * inside
                outer[b] = both[:, LANES:] - (0.5 * z) * inside
            for b in group:
                x, z = xs[b], zs[b]
                m = 1.5 - 0.5 * x
                v = m * x
                inner[b] = product(lefts[b], doubled(*split2(halves[b]))) - (0.5 * v) * inner[b]
            for b in group:
                x, z = xs[b], zs[b]
                m = 1.5 - 0.5 * x
                x = m * m * x
                hat[b] = spread(x) + product(joined(split2(inner[b])), gram_right[b])
                next_xs.append(x)
                next_zs.append(m * z)
        return tuple(next_xs), tuple(next_zs)

    xs, zs = lax.fori_loop(1, NS_ITERS - 1, step, (tuple(xs), tuple(zs)))
    zs = list(zs)

    own = iota((members, ensemble), 0) == iota((members, ensemble), 1)
    lasts, rights, rows, cores = [], [], [], []
    for b in range(blocks):
        x, z = xs[b], zs[b]
        factor = spread(jnp.full((1, LANES), 1.5, F32)) - 0.5 * hat[b]
        last = product(joined(split2(factor)), doubled(*split2(outer[b]))) - (0.5 * z) * inner[b]
        zs[b] = (1.5 - 0.5 * x) * z
        lasts.append(split2(last))
    for b in range(blocks):
        rights.append(doubled(*lasts[b]))
        rows.append(jnp.broadcast_to(departure[:, b * LANES : (b + 1) * LANES], (8, LANES)))
    for _ in range(2):
        moved = [product(joined(split2(rows[b])), rights[b]) for b in range(blocks)]
        moved = [product(joined(split2(moved[b])), gram_right[b]) for b in range(blocks)]
        rows = [zs[b] * rows[b] + moved[b] for b in range(blocks)]
    for b in range(blocks):
        mine = pert[:members, b * LANES : (b + 1) * LANES]
        cores.append(dot(joined((mine, mine)), jnp.concatenate(lasts[b], axis=0)))
    for b in range(blocks):
        root = jnp.sqrt(free * scales[b])
        core = cores[b] * (root * scales[b])
        row = rows[b] * scales[b]
        all_rows = joined(split2(jnp.concatenate([core, row, row], axis=0)))
        found = dot(all_rows, jnp.concatenate([turned[b], turned[b]], axis=0))
        diagonal = jnp.where(own, (root * zs[b])[:, 0:1], 0.0)
        out_ref[b] = (found[:members, :] + found[members : members + 1, :] + diagonal).astype(BF16)


def update_kernel(*refs, others):
    middle_refs = refs[: others + 1]
    edge_refs = refs[others + 1 : 2 * others + 2]
    weight_ref, out_ref, stage = refs[2 * others + 2 :]
    members, levels, columns = out_ref.shape
    groups = columns // LANES
    blocks = weight_ref.shape[0]
    width = columns // blocks
    per = LANES // width
    ensemble = members * (others + 1)
    first = lax.axis_index("mem") * (blocks // (others + 1))
    lane = iota((members, LANES), 1)
    for group in range(groups):
        if group in (0, groups - 1):
            field_refs, start = edge_refs, 0 if group == 0 else LANES
        else:
            field_refs, start = middle_refs, (group - 1) * LANES
        lanes = slice(start, start + LANES)
        left = jnp.concatenate(
            [weight_ref[(group * per + k + blocks - first) % blocks] for k in range(per)], axis=0
        )
        for level in range(levels):
            parts = [ref[level, :, lanes].astype(F32) for ref in field_refs]
            total = sum(jnp.sum(part, axis=0, keepdims=True) for part in parts)
            mean = total * (1.0 / ensemble)
            moved = jnp.concatenate([(part - mean).astype(BF16) for part in parts], axis=0)
            found = dot(left, moved)
            result = found[:members, :]
            for k in range(1, per):
                result = jnp.where(lane < k * width, result, found[k * members : (k + 1) * members, :])
            stage[group, pl.ds(level, members, stride=levels), :] = result + mean
        out_ref[:, :, group * LANES : (group + 1) * LANES] = stage[group].reshape(members, levels, LANES).astype(BF16)


def vmem():
    return pl.BlockSpec(memory_space=pltpu.VMEM)


def group_spec(rows, group):
    return pl.BlockSpec((rows, LANES), lambda i: (0, group))


def call(kernel, outs, inputs, scratch=(), in_specs=None, flops=0):
    return pl.pallas_call(
        kernel,
        grid=(1,),
        out_shape=outs,
        in_specs=in_specs or [vmem()] * len(inputs),
        out_specs=[vmem()] * len(outs),
        scratch_shapes=list(scratch),
        compiler_params=pltpu.CompilerParams(vmem_limit_bytes=VMEM_LIMIT),
        cost_estimate=pl.CostEstimate(flops=flops, bytes_accessed=1 << 10, transcendentals=0),
    )(*inputs)


def shards(
    fields,
    coefficients,
    neighbours,
    obs_cell,
    obs_level,
    obs_value,
    obs_rinv,
    obs_index,
    obs_weight,
):
    tiles = lax.axis_size("tile")
    sharers = lax.axis_size("mem")
    others = sharers - 1
    members, levels, columns = fields.shape
    blocks = obs_index.shape[0]
    entries = blocks * sharers * LANES
    half = members * levels // 2
    message = jax.ShapeDtypeStruct((half + 80, LANES), BF16)
    even_pairs = []
    odd_pairs = []
    for i in range(0, tiles, 2):
        even_pairs += [(i, i + 1), (i + 1, i)]
        low, high = i + 1, (i + 2) % tiles
        odd_pairs += [(low, high), (high, low)]
    turns = [[((i + r) % sharers, i) for i in range(sharers)] for r in range(1, sharers)]

    flat = fields.reshape(members * levels, columns)
    groups = columns // LANES
    hbm = pl.BlockSpec(memory_space=pltpu.HBM)
    a, b, lists, offset = call(
        functools.partial(pack_kernel, tiles=tiles),
        [
            message,
            message,
            jax.ShapeDtypeStruct((48, LANES), BF16),
            jax.ShapeDtypeStruct((8, columns), F32),
        ],
        [flat, coefficients, neighbours, obs_index, obs_weight],
        [
            pltpu.VMEM((members * levels, LANES), F32),
            pltpu.VMEM((members * levels, LANES), F32),
            pltpu.VMEM((6, columns), F32),
            pltpu.VMEM((6, columns), jnp.int32),
            pltpu.VMEM(obs_index.shape, jnp.int32),
            pltpu.VMEM(obs_index.shape, jnp.int32),
            pltpu.SemaphoreType.DMA((6,)),
        ],
        in_specs=[hbm] * 5,
    )
    from_b = lax.ppermute(b, "tile", even_pairs)
    from_a = lax.ppermute(a, "tile", odd_pairs)
    flat_rows = members * levels
    middle = columns - 2 * LANES
    forecast, edge_high, edge_low, part, second = call(
        functools.partial(middle_kernel, groups=groups),
        [
            jax.ShapeDtypeStruct((levels, members, middle), BF16),
            jax.ShapeDtypeStruct((2, flat_rows, 2 * LANES), BF16),
            jax.ShapeDtypeStruct((2, flat_rows, 2 * LANES), BF16),
            jax.ShapeDtypeStruct((2, 2 * LANES, LANES), F32),
            jax.ShapeDtypeStruct((4, 2 * LANES, LANES), BF16),
        ],
        [flat] * groups + [coefficients, offset],
        [
            pltpu.VMEM((flat_rows, columns), BF16),
            pltpu.VMEM((flat_rows, columns), BF16),
            pltpu.VMEM((columns, columns - LANES), BF16),
            pltpu.VMEM((columns, columns - LANES), BF16),
            pltpu.VMEM((columns - LANES, middle), BF16),
            pltpu.VMEM((columns - LANES, middle), BF16),
        ],
        in_specs=[group_spec(flat_rows, group) for group in range(groups)] + [vmem()] * 2,
    )
    forecasts = [forecast] + [lax.ppermute(forecast, "mem", turn) for turn in turns]
    passed = jnp.concatenate([from_a[half + 48 :], from_b[half + 48 :], lists], axis=0)
    passed = [lax.ppermute(passed, "mem", turn) for turn in turns]
    (edge,) = call(
        edge_kernel,
        [jax.ShapeDtypeStruct((levels, members, 2 * LANES), BF16)],
        [from_a, from_b, coefficients, offset, edge_high, edge_low, part, second],
        [pltpu.VMEM((2, flat_rows, 2 * LANES), BF16)],
    )
    cell = obs_cell.reshape(16, LANES)
    level = obs_level.reshape(16, LANES)
    reading = jax.ShapeDtypeStruct((members, entries), BF16)
    table = pltpu.VMEM((48, LANES), BF16)
    to_a, to_b = call(
        functools.partial(neighbour_kernel, others=others, blocks=blocks),
        [reading, reading],
        [forecast, edge, from_a, from_b, *passed, cell, level],
        [table],
    )
    back_a = lax.ppermute(to_a, "tile", odd_pairs)
    back_b = lax.ppermute(to_b, "tile", even_pairs)
    vector = jax.ShapeDtypeStruct((8, entries), F32)
    own, weight, target = call(
        functools.partial(own_kernel, others=others, blocks=blocks, tiles=tiles),
        [reading, vector, vector],
        [
            forecast,
            edge,
            lists,
            *passed,
            cell,
            level,
            obs_value.reshape(-1, LANES),
            obs_rinv.reshape(-1, LANES),
        ],
        [table],
    )
    readings = own + back_a + back_b
    readings = [readings] + [lax.ppermute(readings, "mem", turn) for turn in turns]
    edges = [edge] + [lax.ppermute(edge, "mem", turn) for turn in turns]
    ensemble = members * sharers
    total = blocks * sharers
    square = pltpu.VMEM((total, LANES, LANES), F32)
    (weights,) = call(
        functools.partial(weights_kernel, others=others),
        [jax.ShapeDtypeStruct((total, members, ensemble), BF16)],
        [*readings, weight, target],
        [
            pltpu.VMEM((ensemble, entries), BF16),
            pltpu.VMEM((ensemble, entries), BF16),
            pltpu.VMEM((total, LANES, ensemble), BF16),
            pltpu.VMEM((total, 2 * LANES, 2 * LANES), BF16),
            square,
            square,
            square,
        ],
    )
    (analysis,) = call(
        functools.partial(update_kernel, others=others),
        [jax.ShapeDtypeStruct((members, levels, columns), BF16)],
        [*forecasts, *edges, weights],
        [pltpu.VMEM((columns // LANES, members * levels, LANES), F32)],
    )
    return analysis


def solution(mesh):
    in_specs = (
        P("mem", None, "tile"),
        P(None, "tile"),
        P(None, "tile"),
        P("tile"),
        P("tile"),
        P(),
        P(),
        P("mem", "tile", None),
        P("mem", "tile", None),
    )
    out_specs = P("mem", None, "tile")
    return jax.shard_map(shards, mesh=mesh, in_specs=in_specs, out_specs=out_specs, check_vma=False)
```

```python
import functools

import jax
import jax.numpy as jnp
from jax import lax
from jax.experimental import pallas as pl
from jax.experimental.pallas import tpu as pltpu
from jax.sharding import PartitionSpec as P

HALO = 32
NS_ITERS = 8
LANES = 128
F32 = jnp.float32
BF16 = jnp.bfloat16
VMEM_LIMIT = 48 * 1024 * 1024

NN = (((1,), (0,)), ((), ()))
NT = (((1,), (1,)), ((), ()))
TN = (((0,), (0,)), ((), ()))


def dot(a, b, dims=NN):
    return lax.dot_general(a, b, dims, preferred_element_type=F32)


def split2(x):
    high = x.astype(BF16)
    return high, (x - high.astype(F32)).astype(BF16)


def split3(x):
    high = x.astype(BF16)
    rest = x - high.astype(F32)
    middle = rest.astype(BF16)
    return high, middle, (rest - middle.astype(F32)).astype(BF16)


def iota(shape, dim):
    return lax.broadcasted_iota(jnp.int32, shape, dim)


def is_odd_tile():
    return lax.axis_index("tile") % 2 == 1


def message_rows(field_rows):
    names = ("coef_high", "coef_low", "offset", "list_high", "list_low")
    return {name: field_rows + 16 * place for place, name in enumerate(names)}


def pack_kernel(
    field_hbm,
    coef_hbm,
    nbr_hbm,
    index_hbm,
    weight_hbm,
    a_ref,
    b_ref,
    lists_ref,
    small_ref,
    left_ref,
    right_ref,
    coef_ref,
    nbr_ref,
    index_ref,
    weight_ref,
    sems,
    *,
    tiles,
):
    columns = coef_ref.shape[1]
    levels = 8
    half = left_ref.shape[0] // 2
    members = half // levels
    rows = message_rows(half)
    odd = is_odd_tile()
    total = columns * tiles
    copies = [
        pltpu.make_async_copy(source, target, sems.at[k])
        for k, (source, target) in enumerate(
            (
                (coef_hbm, coef_ref),
                (nbr_hbm, nbr_ref),
                (index_hbm, index_ref),
                (weight_hbm, weight_ref),
                (field_hbm.at[:, 0:LANES], left_ref),
                (field_hbm.at[:, columns - LANES : columns], right_ref),
            )
        )
    ]
    for copy in copies:
        copy.start()
    for copy in copies[:4]:
        copy.wait()

    place = lax.axis_index("tile") * columns + iota((6, columns), 1)
    offset = nbr_ref[...] - place
    offset = jnp.where(offset > HALO, offset - total, offset)
    offset = jnp.where(offset < -HALO, offset + total, offset).astype(F32)
    small_ref[...] = jnp.zeros_like(small_ref)
    small_ref[0:6, :] = coef_ref[...]
    small_ref[8:14, :] = offset
    coef_high, coef_low = split2(coef_ref[...])
    for name, value in (
        ("coef_high", coef_high.astype(F32)),
        ("coef_low", coef_low.astype(F32)),
        ("offset", offset),
    ):
        first = padded(value[:, :LANES], 10)
        last = padded(value[:, columns - LANES :], 10)
        start = rows[name]
        a_ref[start : start + 16, :] = jnp.where(odd, last, first).astype(BF16)
        b_ref[start : start + 16, :] = jnp.where(odd, first, last).astype(BF16)
    blocks = index_ref.shape[0]
    index = padded(index_ref[:, 0, :].astype(F32), 16 - blocks)
    high = jnp.floor(index * (1.0 / 64.0))
    for k, value in enumerate((high, index - 64.0 * high)):
        value = value.astype(BF16)
        start = rows["list_high"] + 16 * k
        a_ref[start : start + 16, :] = value
        b_ref[start : start + 16, :] = value
        lists_ref[16 * k : 16 * k + 16, :] = value
    lists_ref[32:48, :] = padded(weight_ref[:, 0, :].astype(F32), 16 - blocks).astype(BF16)

    for copy in copies[4:]:
        copy.wait()
    lane = iota((members, LANES), 1)
    for level in range(levels):
        top = pl.ds(level, members, stride=levels)
        low = pl.ds(level + half, members, stride=levels)
        spot = slice(level * members, (level + 1) * members)
        left = jnp.where(lane < 64, left_ref[top, :], pltpu.roll(left_ref[low, :], 64, axis=1))
        right = jnp.where(lane < 64, pltpu.roll(right_ref[top, :], 64, axis=1), right_ref[low, :])
        a_ref[spot, :] = jnp.where(odd, right, left).astype(BF16)
        b_ref[spot, :] = jnp.where(odd, left, right).astype(BF16)


def band(coefs, offsets):
    shape = (LANES + 2 * HALO, LANES)
    spot = iota(shape, 0)
    result = jnp.where(
        spot == iota(shape, 1) + HALO, 1.0 - jnp.sum(coefs, axis=0, keepdims=True), 0.0
    )
    target = iota(offsets.shape, 1) + HALO + offsets.astype(jnp.int32)
    for j in range(6):
        result = result + jnp.where(spot == target[j : j + 1, :], coefs[j : j + 1, :], 0.0)
    return result


def dot3(left, right):
    return dot(left[0], right[0]) + (dot(left[0], right[1]) + dot(left[1], right[0]))


def padded(value, count):
    return jnp.concatenate([value, jnp.zeros((count, value.shape[1]), value.dtype)], axis=0)


def middle_kernel(*refs, groups):
    field_refs = refs[:groups]
    (
        small_ref,
        out_ref,
        edge_high,
        edge_low,
        part_ref,
        second_ref,
        u_high,
        u_low,
        first_high,
        first_low,
        second_high,
        second_low,
    ) = refs[groups:]
    levels, members, middle = out_ref.shape
    columns = groups * LANES
    coef = padded(small_ref[0:6, :], 2)
    reach = padded(small_ref[8:14, :], 2)
    moved_coef = pltpu.roll(coef, HALO, axis=1)
    moved_reach = pltpu.roll(reach, HALO, axis=1)

    def lanes(value, group):
        return value[:, group * LANES : (group + 1) * LANES]

    firsts = {
        g: split2(band(lanes(moved_coef, g), lanes(moved_reach, g))) for g in range(1, groups)
    }
    seconds = [split2(band(lanes(coef, g), lanes(reach, g))) for g in range(groups)]
    for ref in (first_high, first_low, second_high, second_low):
        ref[...] = jnp.zeros_like(ref)
    for g in range(1, groups):
        row, lane = g * LANES - 64, (g - 1) * LANES
        count = min(LANES + 2 * HALO, columns - row)
        first_high[row : row + count, lane : lane + LANES] = firsts[g][0][:count, :]
        first_low[row : row + count, lane : lane + LANES] = firsts[g][1][:count, :]
    for g in range(1, groups - 1):
        row, lane = (g - 1) * LANES, (g - 1) * LANES
        second_high[row : row + LANES + 2 * HALO, lane : lane + LANES] = seconds[g][0]
        second_low[row : row + LANES + 2 * HALO, lane : lane + LANES] = seconds[g][1]
    both = split2(
        dot3((first_high[...], first_low[...]), (second_high[...], second_low[...]))
    )

    for k, g in enumerate((0, groups - 1)):
        second = [padded(value, 64) for value in seconds[g]]
        for j in range(2):
            second_ref[2 * k + j] = second[j]
        if k == 0:
            part = dot3([value[:128, :] for value in firsts[1]], [value[128:, :] for value in second])
            part_ref[k] = jnp.concatenate([jnp.zeros_like(part), part], axis=0)
        else:
            part_ref[k] = padded(dot3(firsts[g], [value[:128, :] for value in second]), 64)

    lane = iota((members, LANES), 1)
    for level in range(levels):
        spot = slice(level * members, (level + 1) * members)
        for group, ref in enumerate(field_refs):
            own = ref[pl.ds(level, members, stride=levels), :]
            high, low = split2(own)
            u_high[spot, group * LANES : (group + 1) * LANES] = high
            u_low[spot, group * LANES : (group + 1) * LANES] = low
        for pieces, ref in ((u_high, edge_high), (u_low, edge_low)):
            turned = [
                pltpu.roll(pieces[spot, g * LANES : (g + 1) * LANES].astype(F32), 64, axis=1)
                for g in (0, 1, groups - 2, groups - 1)
            ]
            zero = jnp.zeros_like(turned[0])
            ref[0, spot, 0:LANES] = jnp.where(lane < 64, zero, turned[0]).astype(BF16)
            ref[0, spot, LANES:] = jnp.where(lane < 64, turned[0], turned[1]).astype(BF16)
            ref[1, spot, 0:LANES] = jnp.where(lane < 64, turned[2], turned[3]).astype(BF16)
            ref[1, spot, LANES:] = jnp.where(lane < 64, turned[3], zero).astype(BF16)
    result = dot3((u_high[...], u_low[...]), both)
    for level in range(levels):
        out_ref[level] = result[level * members : (level + 1) * members, :].astype(BF16)


def edge_kernel(
    a_ref, b_ref, small_ref, edge_high, edge_low, part_ref, second_ref, left_ref, right_ref, u_high
):
    levels, members, _ = left_ref.shape
    columns = small_ref.shape[1]
    half = members // 2
    rows = message_rows(levels * half)
    odd = is_odd_tile()

    def side(k, start, count):
        a = a_ref[start : start + count, :].astype(F32)
        b = b_ref[start : start + count, :].astype(F32)
        return jnp.where(odd, b, a) if k == 0 else jnp.where(odd, a, b)

    own_coef = padded(small_ref[0:6, :], 2)
    own_reach = padded(small_ref[8:14, :], 2)
    lane8 = iota((8, LANES), 1)
    lane = iota((half, LANES), 1)
    operators = []
    for k in range(2):
        near = side(k, rows["coef_high"], 16)[:8] + side(k, rows["coef_low"], 16)[:8]
        reach = side(k, rows["offset"], 16)[:8]
        if k == 0:
            own = (own_coef[:, :LANES], own_reach[:, :LANES])
            both = [
                jnp.where(
                    lane8 < HALO, pltpu.roll(x, HALO, axis=1), pltpu.roll(y, HALO, axis=1)
                )
                for x, y in zip((near, reach), own)
            ]
            first = split2(band(*both))
            second = [second_ref[j, :128, :] for j in range(2)]
            fresh = padded(dot3(first, second), 64)
        else:
            own = (own_coef[:, columns - LANES :], own_reach[:, columns - LANES :])
            both = [
                jnp.where(
                    lane8 < HALO, pltpu.roll(y, HALO, axis=1), pltpu.roll(x, HALO, axis=1)
                )
                for x, y in zip((near, reach), own)
            ]
            first = [value[:128, :] for value in split2(band(*both))]
            second = [second_ref[2 + j, 128:, :] for j in range(2)]
            fresh = dot3(first, second)
            fresh = jnp.concatenate([jnp.zeros_like(fresh), fresh], axis=0)
        operators.append(split2(part_ref[k] + fresh))
    for k in range(2):
        for level in range(levels):
            top = level * members
            halo = side(k, level * half, half)
            other = pltpu.roll(halo, 64, axis=1)
            pair = (halo, other) if k == 0 else (other, halo)
            for j in range(2):
                spot = slice(top + j * half, top + (j + 1) * half)
                if k == 0:
                    own = edge_high[k, spot, 0:LANES].astype(F32)
                    u_high[k, spot, 0:LANES] = jnp.where(lane < 64, pair[j], own).astype(BF16)
                    u_high[k, spot, LANES:] = edge_high[k, spot, LANES:]
                else:
                    own = edge_high[k, spot, LANES:].astype(F32)
                    u_high[k, spot, LANES:] = jnp.where(lane < 64, own, pair[j]).astype(BF16)
                    u_high[k, spot, 0:LANES] = edge_high[k, spot, 0:LANES]
        result = dot3((u_high[k], edge_low[k]), operators[k])
        out_ref = (left_ref, right_ref)[k]
        for level in range(levels):
            out_ref[level] = result[level * members : (level + 1) * members, :].astype(BF16)


def gather_lists(parts, blocks):
    return jnp.concatenate(
        [part[b : b + 1, :].astype(F32) for part in parts for b in range(blocks)], axis=1
    )


def read_places(table_ref, slot):
    wide = slot.shape[1]
    valid = (slot >= 0) & (slot < 16 * LANES)
    slot = jnp.where(valid, slot, 0)
    one = jnp.where(iota((LANES, wide), 0) == slot % LANES, 1.0, 0.0).astype(BF16)
    found = dot(table_ref[...], one)
    pick = iota((16, wide), 0) == slot // LANES
    values = [
        jnp.sum(jnp.where(pick, found[16 * k : 16 * k + 16, :], 0.0), axis=0, keepdims=True)
        for k in range(3)
    ]
    column = (values[1] * 16.0 + values[2]).astype(jnp.int32)
    return values[0].astype(jnp.int32), jnp.where(valid, column, -1)


def make_table(cell_ref, level_ref, table):
    cell = cell_ref[...]
    table[0:16, :] = level_ref[...].astype(F32).astype(BF16)
    table[16:32, :] = (cell // 16).astype(F32).astype(BF16)
    table[32:48, :] = (cell % 16).astype(F32).astype(BF16)


def read_forecast(fields, level, column, out_ref, lane):
    members = out_ref.shape[0]
    wide = level.shape[1]
    middle, left, right = fields
    inner = middle.shape[1]
    inside = (column >= LANES) & (column < LANES + inner)
    spot = jnp.where(inside, column - LANES, -1)
    one = jnp.where(iota((inner, wide), 0) == spot, 1.0, 0.0).astype(BF16)
    found = dot(middle, one)
    spot = jnp.where(column < LANES, column, column - inner)
    spot = jnp.where(inside, -1, spot)
    one = jnp.where(iota((2 * LANES, wide), 0) == spot, 1.0, 0.0).astype(BF16)
    found = found + dot(jnp.concatenate([left, right], axis=1), one)
    total = jnp.zeros((members, wide), F32)
    for l in range(middle.shape[0] // members):
        total = total + jnp.where(level == l, found[l * members : (l + 1) * members, :], 0.0)
    out_ref[:, lane : lane + wide] = total.astype(BF16)


def neighbour_kernel(middle_ref, left_ref, right_ref, a_ref, b_ref, *refs, others, blocks):
    other_refs = refs[:others]
    cell_ref, level_ref, ra_ref, rb_ref, table = refs[others:]
    half = a_ref.shape[0] - 80
    rows = message_rows(half)
    odd = is_odd_tile()
    obs = 16 * LANES
    make_table(cell_ref, level_ref, table)
    fields = [ref[...].reshape(-1, ref.shape[2]) for ref in (middle_ref, left_ref, right_ref)]
    for turn, (ref, out_ref) in enumerate(((a_ref, ra_ref), (b_ref, rb_ref))):
        base = 32 * turn
        parts = [ref[rows["list_high"] : rows["list_high"] + 32, :]]
        parts += [r[base : base + 32, :] for r in other_refs]
        high = gather_lists([part[:16, :] for part in parts], blocks)
        low = gather_lists([part[16:, :] for part in parts], blocks)
        index = (high * 64.0 + low).astype(jnp.int32)
        skip = jnp.where(odd, 0, 2 * obs) if turn == 0 else jnp.where(odd, 2 * obs, 0)
        level, column = read_places(table, index - skip)
        for lane in range(0, index.shape[1], 256):
            read_forecast(
                fields, level[:, lane : lane + 256], column[:, lane : lane + 256], out_ref, lane
            )


def own_kernel(middle_ref, left_ref, right_ref, lists_ref, *refs, others, blocks, tiles):
    other_refs = refs[:others]
    cell_ref, level_ref, value_ref, rinv_ref, r_ref, weight_ref, target_ref, table = refs[others:]
    obs = 16 * LANES
    make_table(cell_ref, level_ref, table)
    fields = [ref[...].reshape(-1, ref.shape[2]) for ref in (middle_ref, left_ref, right_ref)]

    parts = [lists_ref[...]] + [r[64:112, :] for r in other_refs]
    passed = [gather_lists([part[16 * k : 16 * k + 16, :] for part in parts], blocks) for k in range(3)]
    index = (passed[0] * 64.0 + passed[1]).astype(jnp.int32)
    weight = passed[2]
    wide = index.shape[1]
    level, column = read_places(table, index - obs)
    for lane in range(0, wide, 256):
        read_forecast(fields, level[:, lane : lane + 256], column[:, lane : lane + 256], r_ref, lane)

    tile = lax.axis_index("tile")
    starts = [((tile + tiles + shift) % tiles) * 16 for shift in (-1, 0, 1)]
    one = jnp.where(iota((LANES, wide), 0) == index % LANES, 1.0, 0.0).astype(BF16)
    pick = iota((48, wide), 0) == index // LANES

    def looked_up(ref):
        window = jnp.concatenate([ref[pl.ds(pl.multiple_of(s, 16), 16), :] for s in starts], axis=0)
        high, middle, low = [dot(piece, one) for piece in split3(window)]
        return jnp.sum(jnp.where(pick, (high + middle) + low, 0.0), axis=0, keepdims=True)

    weight_ref[...] = jnp.broadcast_to(looked_up(rinv_ref) * (weight / 3.0), weight_ref.shape)
    target_ref[...] = jnp.broadcast_to(looked_up(value_ref), target_ref.shape)


def merge_kernel(own_ref, a_ref, b_ref, *refs):
    out_ref = refs[-1]
    out_ref[...] = (
        own_ref[...].astype(F32) + (a_ref[...].astype(F32) + b_ref[...].astype(F32))
    ).astype(BF16)


def doubled(high, low):
    top = jnp.concatenate([high, low], axis=1)
    bottom = jnp.concatenate([high, jnp.zeros_like(low)], axis=1)
    return jnp.concatenate([top, bottom], axis=0)


def product(left, right):
    both = dot(left, right)
    wide = both.shape[1] // 2
    return both[:, :wide] + both[:, wide:]


def joined(pair):
    return jnp.concatenate(pair, axis=1)


def weights_kernel(*refs, others):
    r_refs = refs[: others + 1]
    weight_ref, target_ref, out_ref, pert, weighted, turned, gram_right, hat, inner, outer = refs[others + 1 :]
    members, wide = r_refs[0].shape
    blocks = wide // LANES
    share = blocks // (others + 1)
    ensemble = members * (others + 1)
    free = ensemble - 1.0

    parts = [r_refs[0][...].astype(F32)]
    for k in range(others):
        other = r_refs[k + 1][...].astype(F32)
        turn = ((k + 1) * share * LANES) % wide
        parts.append(jnp.concatenate([other[:, wide - turn :], other[:, : wide - turn]], axis=1))
    total = sum(jnp.sum(part, axis=0, keepdims=True) for part in parts)
    mean = total * (1.0 / ensemble)
    weight = weight_ref[0:1, :]
    for k, part in enumerate(parts):
        rounded = (part - mean).astype(BF16)
        pert[k * members : (k + 1) * members, :] = rounded
        weighted[k * members : (k + 1) * members, :] = (rounded.astype(F32) * weight).astype(BF16)
    departure = target_ref[0:1, :] - mean

    eye = iota((LANES, LANES), 0) == iota((LANES, LANES), 1)

    def spread(value):
        return jnp.where(eye, value, 0.0)

    scales, xs, zs, grams, lefts, inners = [], [], [], [], [], []
    for b in range(blocks):
        lanes = slice(b * LANES, (b + 1) * LANES)
        turned[b] = weighted[:, lanes].T
    for b in range(blocks):
        lanes = slice(b * LANES, (b + 1) * LANES)
        grams.append(dot(turned[b], pert[:, lanes]))
    for b in range(blocks):
        trace = jnp.sum(jnp.sum(spread(grams[b]), axis=0, keepdims=True), axis=1, keepdims=True)
        scales.append(jnp.broadcast_to(1.0 / (free + trace), (1, LANES)))
    for b in range(blocks):
        gram = grams[b] * scales[b]
        x = free * scales[b]
        gram_right[b] = doubled(*split2(gram))
        m = 1.5 - 0.5 * x
        factor = spread(m) - 0.5 * gram
        v = m * x
        inners.append(
            product(joined(split2(factor)), doubled(*split2(factor - spread(0.5 * x))))
            - spread(0.5 * v)
        )
        xs.append(m * v)
        zs.append(m)
    for b in range(blocks):
        inner[b] = inners[b]
        hat[b] = spread(xs[b]) + product(joined(split2(inners[b])), gram_right[b])
        outer[b] = spread(jnp.full((1, LANES), -0.5, F32))

    def step(_, carry):
        xs, zs = carry
        next_xs, next_zs = [], []
        for base in range(0, blocks, 8):
            group = range(base, min(base + 8, blocks))
            lefts, halves = {}, {}
            for b in group:
                x, z = xs[b], zs[b]
                factor = spread(jnp.full((1, LANES), 1.5, F32)) - 0.5 * hat[b]
                f_high, f_low = split2(factor)
                lefts[b] = joined((f_high, f_low))
                inside = inner[b]
                i_high, i_low = split2(inside)
                o_high, o_low = split2(outer[b])
                right_high = joined((i_high, o_high))
                both = dot(lefts[b], jnp.concatenate([right_high, right_high], axis=0)) + dot(
                    f_high, joined((i_low, o_low))
                )
                halves[b] = both[:, :LANES] - (0.5 * x) * inside
                outer[b] = both[:, LANES:] - (0.5 * z) * inside
            for b in group:
                x, z = xs[b], zs[b]
                m = 1.5 - 0.5 * x
                v = m * x
                inner[b] = product(lefts[b], doubled(*split2(halves[b]))) - (0.5 * v) * inner[b]
            for b in group:
                x, z = xs[b], zs[b]
                m = 1.5 - 0.5 * x
                x = m * m * x
                hat[b] = spread(x) + product(joined(split2(inner[b])), gram_right[b])
                next_xs.append(x)
                next_zs.append(m * z)
        return tuple(next_xs), tuple(next_zs)

    xs, zs = lax.fori_loop(1, NS_ITERS - 1, step, (tuple(xs), tuple(zs)))
    zs = list(zs)

    own = iota((members, ensemble), 0) == iota((members, ensemble), 1)
    lasts, rights, rows, cores = [], [], [], []
    for b in range(blocks):
        x, z = xs[b], zs[b]
        factor = spread(jnp.full((1, LANES), 1.5, F32)) - 0.5 * hat[b]
        last = product(joined(split2(factor)), doubled(*split2(outer[b]))) - (0.5 * z) * inner[b]
        zs[b] = (1.5 - 0.5 * x) * z
        lasts.append(split2(last))
    for b in range(blocks):
        rights.append(doubled(*lasts[b]))
        rows.append(jnp.broadcast_to(departure[:, b * LANES : (b + 1) * LANES], (8, LANES)))
    for _ in range(2):
        moved = [product(joined(split2(rows[b])), rights[b]) for b in range(blocks)]
        moved = [product(joined(split2(moved[b])), gram_right[b]) for b in range(blocks)]
        rows = [zs[b] * rows[b] + moved[b] for b in range(blocks)]
    for b in range(blocks):
        mine = pert[:members, b * LANES : (b + 1) * LANES]
        cores.append(dot(joined((mine, mine)), jnp.concatenate(lasts[b], axis=0)))
    for b in range(blocks):
        root = jnp.sqrt(free * scales[b])
        core = cores[b] * (root * scales[b])
        row = rows[b] * scales[b]
        all_rows = joined(split2(jnp.concatenate([core, row, row], axis=0)))
        found = dot(all_rows, jnp.concatenate([turned[b], turned[b]], axis=0))
        diagonal = jnp.where(own, (root * zs[b])[:, 0:1], 0.0)
        out_ref[b] = (found[:members, :] + found[members : members + 1, :] + diagonal).astype(BF16)


def update_kernel(*refs, others):
    middle_refs = refs[: others + 1]
    left_refs = refs[others + 1 : 2 * others + 2]
    right_refs = refs[2 * others + 2 : 3 * others + 3]
    weight_ref, out_ref, stage = refs[3 * others + 3 :]
    members, levels, columns = out_ref.shape
    groups = columns // LANES
    blocks = weight_ref.shape[0]
    width = columns // blocks
    per = LANES // width
    ensemble = members * (others + 1)
    first = lax.axis_index("mem") * (blocks // (others + 1))
    lane = iota((members, LANES), 1)
    for group in range(groups):
        if group in (0, groups - 1):
            field_refs, start = (left_refs if group == 0 else right_refs), 0
        else:
            field_refs, start = middle_refs, (group - 1) * LANES
        lanes = slice(start, start + LANES)
        left = jnp.concatenate(
            [weight_ref[(group * per + k + blocks - first) % blocks] for k in range(per)], axis=0
        )
        for level in range(levels):
            parts = [ref[level, :, lanes].astype(F32) for ref in field_refs]
            total = sum(jnp.sum(part, axis=0, keepdims=True) for part in parts)
            mean = total * (1.0 / ensemble)
            moved = jnp.concatenate([(part - mean).astype(BF16) for part in parts], axis=0)
            found = dot(left, moved)
            result = found[:members, :]
            for k in range(1, per):
                result = jnp.where(lane < k * width, result, found[k * members : (k + 1) * members, :])
            stage[group, pl.ds(level, members, stride=levels), :] = result + mean
        out_ref[:, :, group * LANES : (group + 1) * LANES] = stage[group].reshape(members, levels, LANES).astype(BF16)


def vmem():
    return pl.BlockSpec(memory_space=pltpu.VMEM)


def group_spec(rows, group):
    return pl.BlockSpec((rows, LANES), lambda i: (0, group))


def call(kernel, outs, inputs, scratch=(), in_specs=None, cost=0, limit=VMEM_LIMIT):
    return pl.pallas_call(
        kernel,
        grid=(1,),
        out_shape=outs,
        in_specs=in_specs or [vmem()] * len(inputs),
        out_specs=[vmem()] * len(outs),
        scratch_shapes=list(scratch),
        compiler_params=pltpu.CompilerParams(vmem_limit_bytes=limit),
        cost_estimate=pl.CostEstimate(flops=cost << 30, bytes_accessed=1 << 10, transcendentals=0),
    )(*inputs)


def shards(
    fields,
    coefficients,
    neighbours,
    obs_cell,
    obs_level,
    obs_value,
    obs_rinv,
    obs_index,
    obs_weight,
):
    tiles = lax.axis_size("tile")
    sharers = lax.axis_size("mem")
    others = sharers - 1
    members, levels, columns = fields.shape
    blocks = obs_index.shape[0]
    entries = blocks * sharers * LANES
    half = members * levels // 2
    message = jax.ShapeDtypeStruct((half + 80, LANES), BF16)
    even_pairs = []
    odd_pairs = []
    for i in range(0, tiles, 2):
        even_pairs += [(i, i + 1), (i + 1, i)]
        low, high = i + 1, (i + 2) % tiles
        odd_pairs += [(low, high), (high, low)]
    turns = [[((i + r) % sharers, i) for i in range(sharers)] for r in range(1, sharers)]

    flat = fields.reshape(members * levels, columns)
    groups = columns // LANES
    hbm = pl.BlockSpec(memory_space=pltpu.HBM)
    a, b, lists, small = call(
        functools.partial(pack_kernel, tiles=tiles),
        [
            message,
            message,
            jax.ShapeDtypeStruct((48, LANES), BF16),
            jax.ShapeDtypeStruct((16, columns), F32),
        ],
        [flat, coefficients, neighbours, obs_index, obs_weight],
        [
            pltpu.VMEM((members * levels, LANES), F32),
            pltpu.VMEM((members * levels, LANES), F32),
            pltpu.VMEM((6, columns), F32),
            pltpu.VMEM((6, columns), jnp.int32),
            pltpu.VMEM(obs_index.shape, jnp.int32),
            pltpu.VMEM(obs_index.shape, jnp.int32),
            pltpu.SemaphoreType.DMA((6,)),
        ],
        in_specs=[hbm] * 5,
        limit=64 * 1024 * 1024,
    )
    from_b = lax.ppermute(b, "tile", even_pairs)
    from_a = lax.ppermute(a, "tile", odd_pairs)
    flat_rows = members * levels
    middle = columns - 2 * LANES
    forecast, edge_high, edge_low, part, second = call(
        functools.partial(middle_kernel, groups=groups),
        [
            jax.ShapeDtypeStruct((levels, members, middle), BF16),
            jax.ShapeDtypeStruct((2, flat_rows, 2 * LANES), BF16),
            jax.ShapeDtypeStruct((2, flat_rows, 2 * LANES), BF16),
            jax.ShapeDtypeStruct((2, 2 * LANES, LANES), F32),
            jax.ShapeDtypeStruct((4, 2 * LANES, LANES), BF16),
        ],
        [flat] * groups + [small],
        [
            pltpu.VMEM((flat_rows, columns), BF16),
            pltpu.VMEM((flat_rows, columns), BF16),
            pltpu.VMEM((columns, columns - LANES), BF16),
            pltpu.VMEM((columns, columns - LANES), BF16),
            pltpu.VMEM((columns - LANES, middle), BF16),
            pltpu.VMEM((columns - LANES, middle), BF16),
        ],
        in_specs=[group_spec(flat_rows, group) for group in range(groups)] + [vmem()],
        cost=4,
    )
    passed = jnp.concatenate([from_a[half + 48 :], from_b[half + 48 :], lists], axis=0)
    passed, sent = lax.optimization_barrier((passed, forecast))
    forecasts = [forecast] + [lax.ppermute(sent, "mem", turn) for turn in turns]
    passed = [lax.ppermute(passed, "mem", turn) for turn in turns]
    left, right = call(
        edge_kernel,
        [jax.ShapeDtypeStruct((levels, members, LANES), BF16)] * 2,
        [from_a, from_b, small, edge_high, edge_low, part, second],
        [pltpu.VMEM((2, flat_rows, 2 * LANES), BF16)],
        cost=2,
    )
    cell = obs_cell.reshape(16, LANES)
    level = obs_level.reshape(16, LANES)
    reading = jax.ShapeDtypeStruct((members, entries), BF16)
    table = pltpu.VMEM((48, LANES), BF16)
    to_a, to_b = call(
        functools.partial(neighbour_kernel, others=others, blocks=blocks),
        [reading, reading],
        [forecast, left, right, from_a, from_b, *passed, cell, level],
        [table],
        cost=3,
    )
    back_a = lax.ppermute(to_a, "tile", odd_pairs)
    back_b = lax.ppermute(to_b, "tile", even_pairs)
    vector = jax.ShapeDtypeStruct((8, entries), F32)
    own, weight, target = call(
        functools.partial(own_kernel, others=others, blocks=blocks, tiles=tiles),
        [reading, vector, vector],
        [
            forecast,
            left,
            right,
            lists,
            *passed,
            cell,
            level,
            obs_value.reshape(-1, LANES),
            obs_rinv.reshape(-1, LANES),
        ],
        [table],
        cost=2,
    )
    unused = forecasts[1:]
    (readings,) = call(
        merge_kernel,
        [reading],
        [own, back_a, back_b, *unused],
        in_specs=[vmem()] * 3 + [pl.BlockSpec(memory_space=pl.ANY)] * len(unused),
        cost=0,
    )
    readings, sent_left, sent = lax.optimization_barrier((readings, left, right))
    lefts = [left] + [lax.ppermute(sent_left, "mem", turn) for turn in turns]
    rights = [right] + [lax.ppermute(sent, "mem", turn) for turn in turns]
    readings = [readings] + [lax.ppermute(readings, "mem", turn) for turn in turns]
    ensemble = members * sharers
    total = blocks * sharers
    square = pltpu.VMEM((total, LANES, LANES), F32)
    (weights,) = call(
        functools.partial(weights_kernel, others=others),
        [jax.ShapeDtypeStruct((total, members, ensemble), BF16)],
        [*readings, weight, target],
        [
            pltpu.VMEM((ensemble, entries), BF16),
            pltpu.VMEM((ensemble, entries), BF16),
            pltpu.VMEM((total, LANES, ensemble), BF16),
            pltpu.VMEM((total, 2 * LANES, 2 * LANES), BF16),
            square,
            square,
            square,
        ],
        cost=8,
    )
    (analysis,) = call(
        functools.partial(update_kernel, others=others),
        [jax.ShapeDtypeStruct((members, levels, columns), BF16)],
        [*forecasts, *lefts, *rights, weights],
        [pltpu.VMEM((columns // LANES, members * levels, LANES), F32)],
        cost=3,
    )
    return analysis


def solution(mesh):
    in_specs = (
        P("mem", None, "tile"),
        P(None, "tile"),
        P(None, "tile"),
        P("tile"),
        P("tile"),
        P(),
        P(),
        P("mem", "tile", None),
        P("mem", "tile", None),
    )
    out_specs = P("mem", None, "tile")
    return jax.shard_map(shards, mesh=mesh, in_specs=in_specs, out_specs=out_specs, check_vma=False)
```

```python
import functools

import jax
import jax.numpy as jnp
from jax import lax
from jax.experimental import pallas as pl
from jax.experimental.pallas import tpu as pltpu
from jax.sharding import PartitionSpec as P

HALO = 32
NS_ITERS = 8
LANES = 128
F32 = jnp.float32
BF16 = jnp.bfloat16
VMEM_LIMIT = 48 * 1024 * 1024

NN = (((1,), (0,)), ((), ()))
NT = (((1,), (1,)), ((), ()))
TN = (((0,), (0,)), ((), ()))


def dot(a, b, dims=NN):
    return lax.dot_general(a, b, dims, preferred_element_type=F32)


def split2(x):
    high = x.astype(BF16)
    return high, (x - high.astype(F32)).astype(BF16)


def split3(x):
    high = x.astype(BF16)
    rest = x - high.astype(F32)
    middle = rest.astype(BF16)
    return high, middle, (rest - middle.astype(F32)).astype(BF16)


def iota(shape, dim):
    return lax.broadcasted_iota(jnp.int32, shape, dim)


def is_odd_tile():
    return lax.axis_index("tile") % 2 == 1


def message_rows(field_rows):
    names = ("coef_high", "coef_low", "offset", "list_high", "list_low")
    return {name: field_rows + 16 * place for place, name in enumerate(names)}


def pack_kernel(
    field_hbm,
    coef_hbm,
    nbr_hbm,
    index_hbm,
    weight_hbm,
    a_ref,
    b_ref,
    lists_ref,
    small_ref,
    left_ref,
    right_ref,
    coef_ref,
    nbr_ref,
    index_ref,
    weight_ref,
    sems,
    *,
    tiles,
):
    columns = coef_ref.shape[1]
    levels = 8
    half = left_ref.shape[0] // 2
    members = half // levels
    rows = message_rows(half)
    odd = is_odd_tile()
    total = columns * tiles
    copies = [
        pltpu.make_async_copy(source, target, sems.at[k])
        for k, (source, target) in enumerate(
            (
                (coef_hbm, coef_ref),
                (nbr_hbm, nbr_ref),
                (index_hbm, index_ref),
                (weight_hbm, weight_ref),
                (field_hbm.at[:, 0:LANES], left_ref),
                (field_hbm.at[:, columns - LANES : columns], right_ref),
            )
        )
    ]
    for copy in copies:
        copy.start()
    for copy in copies[:4]:
        copy.wait()

    place = lax.axis_index("tile") * columns + iota((6, columns), 1)
    offset = nbr_ref[...] - place
    offset = jnp.where(offset > HALO, offset - total, offset)
    offset = jnp.where(offset < -HALO, offset + total, offset).astype(F32)
    small_ref[...] = jnp.zeros_like(small_ref)
    small_ref[0:6, :] = coef_ref[...]
    small_ref[8:14, :] = offset
    coef_high, coef_low = split2(coef_ref[...])
    for name, value in (
        ("coef_high", coef_high.astype(F32)),
        ("coef_low", coef_low.astype(F32)),
        ("offset", offset),
    ):
        first = padded(value[:, :LANES], 10)
        last = padded(value[:, columns - LANES :], 10)
        start = rows[name]
        a_ref[start : start + 16, :] = jnp.where(odd, last, first).astype(BF16)
        b_ref[start : start + 16, :] = jnp.where(odd, first, last).astype(BF16)
    blocks = index_ref.shape[0]
    index = padded(index_ref[:, 0, :].astype(F32), 16 - blocks)
    high = jnp.floor(index * (1.0 / 64.0))
    for k, value in enumerate((high, index - 64.0 * high)):
        value = value.astype(BF16)
        start = rows["list_high"] + 16 * k
        a_ref[start : start + 16, :] = value
        b_ref[start : start + 16, :] = value
        lists_ref[16 * k : 16 * k + 16, :] = value
    lists_ref[32:48, :] = padded(weight_ref[:, 0, :].astype(F32), 16 - blocks).astype(BF16)

    for copy in copies[4:]:
        copy.wait()
    lane = iota((members, LANES), 1)
    for level in range(levels):
        top = pl.ds(level, members, stride=levels)
        low = pl.ds(level + half, members, stride=levels)
        spot = slice(level * members, (level + 1) * members)
        left = jnp.where(lane < 64, left_ref[top, :], pltpu.roll(left_ref[low, :], 64, axis=1))
        right = jnp.where(lane < 64, pltpu.roll(right_ref[top, :], 64, axis=1), right_ref[low, :])
        a_ref[spot, :] = jnp.where(odd, right, left).astype(BF16)
        b_ref[spot, :] = jnp.where(odd, left, right).astype(BF16)


def band(coefs, offsets):
    shape = (LANES + 2 * HALO, LANES)
    spot = iota(shape, 0)
    result = jnp.where(
        spot == iota(shape, 1) + HALO, 1.0 - jnp.sum(coefs, axis=0, keepdims=True), 0.0
    )
    target = iota(offsets.shape, 1) + HALO + offsets.astype(jnp.int32)
    for j in range(6):
        result = result + jnp.where(spot == target[j : j + 1, :], coefs[j : j + 1, :], 0.0)
    return result


def dot3(left, right):
    return dot(left[0], right[0]) + (dot(left[0], right[1]) + dot(left[1], right[0]))


def padded(value, count):
    return jnp.concatenate([value, jnp.zeros((count, value.shape[1]), value.dtype)], axis=0)


def middle_kernel(*refs, groups):
    field_refs = refs[:groups]
    small_ref, middle_ref, kept_ref = refs[groups : groups + 3]
    (
        edge_high,
        edge_low,
        part_ref,
        second_ref,
        u_high,
        u_low,
        first_high,
        first_low,
        second_high,
        second_low,
    ) = refs[groups + 3 :]
    late, members, _ = kept_ref.shape
    levels = 2 * late
    early = (groups - 2) * levels - late
    columns = groups * LANES
    coef = padded(small_ref[0:6, :], 2)
    reach = padded(small_ref[8:14, :], 2)
    moved_coef = pltpu.roll(coef, HALO, axis=1)
    moved_reach = pltpu.roll(reach, HALO, axis=1)

    def lanes(value, group):
        return value[:, group * LANES : (group + 1) * LANES]

    firsts = {
        g: split2(band(lanes(moved_coef, g), lanes(moved_reach, g))) for g in range(1, groups)
    }
    seconds = [split2(band(lanes(coef, g), lanes(reach, g))) for g in range(groups)]
    for ref in (first_high, first_low, second_high, second_low):
        ref[...] = jnp.zeros_like(ref)
    for g in range(1, groups):
        row, lane = g * LANES - 64, (g - 1) * LANES
        count = min(LANES + 2 * HALO, columns - row)
        first_high[row : row + count, lane : lane + LANES] = firsts[g][0][:count, :]
        first_low[row : row + count, lane : lane + LANES] = firsts[g][1][:count, :]
    for g in range(1, groups - 1):
        row, lane = (g - 1) * LANES, (g - 1) * LANES
        second_high[row : row + LANES + 2 * HALO, lane : lane + LANES] = seconds[g][0]
        second_low[row : row + LANES + 2 * HALO, lane : lane + LANES] = seconds[g][1]
    both = split2(
        dot3((first_high[...], first_low[...]), (second_high[...], second_low[...]))
    )

    for k, g in enumerate((0, groups - 1)):
        second = [padded(value, 64) for value in seconds[g]]
        for j in range(2):
            second_ref[2 * k + j] = second[j]
        if k == 0:
            part = dot3([value[:128, :] for value in firsts[1]], [value[128:, :] for value in second])
            part_ref[k] = jnp.concatenate([jnp.zeros_like(part), part], axis=0)
        else:
            part_ref[k] = padded(dot3(firsts[g], [value[:128, :] for value in second]), 64)

    lane = iota((members, LANES), 1)
    for level in range(levels):
        spot = slice(level * members, (level + 1) * members)
        for group, ref in enumerate(field_refs):
            own = ref[pl.ds(level, members, stride=levels), :]
            high, low = split2(own)
            u_high[spot, group * LANES : (group + 1) * LANES] = high
            u_low[spot, group * LANES : (group + 1) * LANES] = low
        for pieces, ref in ((u_high, edge_high), (u_low, edge_low)):
            turned = [
                pltpu.roll(pieces[spot, g * LANES : (g + 1) * LANES].astype(F32), 64, axis=1)
                for g in (0, 1, groups - 2, groups - 1)
            ]
            zero = jnp.zeros_like(turned[0])
            ref[0, spot, 0:LANES] = jnp.where(lane < 64, zero, turned[0]).astype(BF16)
            ref[0, spot, LANES:] = jnp.where(lane < 64, turned[0], turned[1]).astype(BF16)
            ref[1, spot, 0:LANES] = jnp.where(lane < 64, turned[2], turned[3]).astype(BF16)
            ref[1, spot, LANES:] = jnp.where(lane < 64, turned[3], zero).astype(BF16)
    result = dot3((u_high[...], u_low[...]), both)
    for k in range((groups - 2) * levels):
        level, lane = k % levels, (k // levels) * LANES
        value = result[level * members : (level + 1) * members, lane : lane + LANES].astype(BF16)
        if k < early:
            middle_ref[k] = value
        else:
            kept_ref[k - early] = value


def edge_kernel(
    a_ref, b_ref, small_ref, edge_high, edge_low, part_ref, second_ref, kept_ref, first_ref, next_ref, last_ref, u_high
):
    levels, members, _ = next_ref.shape
    columns = small_ref.shape[1]
    half = members // 2
    rows = message_rows(levels * half)
    odd = is_odd_tile()

    def side(k, start, count):
        a = a_ref[start : start + count, :].astype(F32)
        b = b_ref[start : start + count, :].astype(F32)
        return jnp.where(odd, b, a) if k == 0 else jnp.where(odd, a, b)

    own_coef = padded(small_ref[0:6, :], 2)
    own_reach = padded(small_ref[8:14, :], 2)
    lane8 = iota((8, LANES), 1)
    lane = iota((half, LANES), 1)
    operators = []
    for k in range(2):
        near = side(k, rows["coef_high"], 16)[:8] + side(k, rows["coef_low"], 16)[:8]
        reach = side(k, rows["offset"], 16)[:8]
        if k == 0:
            own = (own_coef[:, :LANES], own_reach[:, :LANES])
            both = [
                jnp.where(
                    lane8 < HALO, pltpu.roll(x, HALO, axis=1), pltpu.roll(y, HALO, axis=1)
                )
                for x, y in zip((near, reach), own)
            ]
            first = split2(band(*both))
            second = [second_ref[j, :128, :] for j in range(2)]
            fresh = padded(dot3(first, second), 64)
        else:
            own = (own_coef[:, columns - LANES :], own_reach[:, columns - LANES :])
            both = [
                jnp.where(
                    lane8 < HALO, pltpu.roll(y, HALO, axis=1), pltpu.roll(x, HALO, axis=1)
                )
                for x, y in zip((near, reach), own)
            ]
            first = [value[:128, :] for value in split2(band(*both))]
            second = [second_ref[2 + j, 128:, :] for j in range(2)]
            fresh = dot3(first, second)
            fresh = jnp.concatenate([jnp.zeros_like(fresh), fresh], axis=0)
        operators.append(split2(part_ref[k] + fresh))
    for k in range(2):
        for level in range(levels):
            top = level * members
            halo = side(k, level * half, half)
            other = pltpu.roll(halo, 64, axis=1)
            pair = (halo, other) if k == 0 else (other, halo)
            for j in range(2):
                spot = slice(top + j * half, top + (j + 1) * half)
                if k == 0:
                    own = edge_high[k, spot, 0:LANES].astype(F32)
                    u_high[k, spot, 0:LANES] = jnp.where(lane < 64, pair[j], own).astype(BF16)
                    u_high[k, spot, LANES:] = edge_high[k, spot, LANES:]
                else:
                    own = edge_high[k, spot, LANES:].astype(F32)
                    u_high[k, spot, LANES:] = jnp.where(lane < 64, own, pair[j]).astype(BF16)
                    u_high[k, spot, 0:LANES] = edge_high[k, spot, 0:LANES]
        result = dot3((u_high[k], edge_low[k]), operators[k])
        part = levels // 2
        if k == 0:
            first_ref[:part] = kept_ref[...]
        for level in range(levels):
            value = result[level * members : (level + 1) * members, :].astype(BF16)
            if k == 0 and level < part:
                first_ref[part + level] = value
            elif k == 0:
                next_ref[level - part] = value
            elif level < part:
                next_ref[part + level] = value
            else:
                last_ref[level - part] = value


def gather_lists(parts, blocks):
    count = len(parts)
    me = lax.axis_index("mem")
    rows = [
        jnp.concatenate([part[b : b + 1, :].astype(F32) for b in range(blocks)], axis=1)
        for part in parts
    ]
    placed = []
    for place in range(count):
        value = rows[0]
        for shift in range(1, count):
            value = jnp.where((me + shift) % count == place, rows[shift], value)
        placed.append(value)
    return jnp.concatenate(placed, axis=1)


def read_places(table_ref, slot):
    wide = slot.shape[1]
    valid = (slot >= 0) & (slot < 16 * LANES)
    slot = jnp.where(valid, slot, 0)
    one = jnp.where(iota((LANES, wide), 0) == slot % LANES, 1.0, 0.0).astype(BF16)
    found = dot(table_ref[...], one)
    pick = iota((16, wide), 0) == slot // LANES
    values = [
        jnp.sum(jnp.where(pick, found[16 * k : 16 * k + 16, :], 0.0), axis=0, keepdims=True)
        for k in range(3)
    ]
    column = (values[1] * 16.0 + values[2]).astype(jnp.int32)
    return values[0].astype(jnp.int32), jnp.where(valid, column, -1)


def make_table(cell_ref, level_ref, table):
    cell = cell_ref[...]
    table[0:16, :] = level_ref[...].astype(F32).astype(BF16)
    table[16:32, :] = (cell // 16).astype(F32).astype(BF16)
    table[32:48, :] = (cell % 16).astype(F32).astype(BF16)


def read_forecast(field, level, column, out_ref, lane):
    members = out_ref.shape[0]
    wide = level.shape[1]
    one = jnp.where(iota((field.shape[1], wide), 0) == column, 1.0, 0.0).astype(BF16)
    found = dot(field, one)
    total = jnp.zeros((members, wide), F32)
    for l in range(field.shape[0] // members):
        total = total + jnp.where(level == l, found[l * members : (l + 1) * members, :], 0.0)
    out_ref[:, lane : lane + wide] = total.astype(BF16)


def whole(middle_ref, first_ref, next_ref, last_ref):
    part, members, _ = last_ref.shape
    middle = jnp.concatenate([middle_ref[...], first_ref[:part]], axis=0)
    groups = [
        jnp.concatenate([first_ref[part:], next_ref[:part]], axis=0),
        *(middle[k : k + 2 * part] for k in range(0, middle.shape[0], 2 * part)),
        jnp.concatenate([next_ref[part:], last_ref[...]], axis=0),
    ]
    return joined([group.reshape(-1, LANES) for group in groups])


def neighbour_kernel(*refs, others, blocks, turn):
    message_ref = refs[4]
    other_refs = refs[5 : 5 + others]
    cell_ref, level_ref = refs[5 + others : 7 + others]
    out_ref, table = refs[-2:]
    half = message_ref.shape[0] - 80
    rows = message_rows(half)
    odd = is_odd_tile()
    obs = 16 * LANES
    make_table(cell_ref, level_ref, table)
    field = whole(*refs[:4])
    base = 32 * turn
    parts = [message_ref[rows["list_high"] : rows["list_high"] + 32, :]]
    parts += [r[base : base + 32, :] for r in other_refs]
    high = gather_lists([part[:16, :] for part in parts], blocks)
    low = gather_lists([part[16:, :] for part in parts], blocks)
    index = (high * 64.0 + low).astype(jnp.int32)
    skip = jnp.where(odd, 0, 2 * obs) if turn == 0 else jnp.where(odd, 2 * obs, 0)
    level, column = read_places(table, index - skip)
    for lane in range(0, index.shape[1], 256):
        read_forecast(
            field, level[:, lane : lane + 256], column[:, lane : lane + 256], out_ref, lane
        )


def own_kernel(*refs, others, blocks, tiles):
    lists_ref = refs[4]
    other_refs = refs[5 : 5 + others]
    (
        cell_ref,
        level_ref,
        value_ref,
        rinv_ref,
        r_ref,
        weight_ref,
        target_ref,
        table,
    ) = refs[5 + others :]
    obs = 16 * LANES
    make_table(cell_ref, level_ref, table)
    field = whole(*refs[:4])

    parts = [lists_ref[...]] + [r[64:112, :] for r in other_refs]
    passed = [gather_lists([part[16 * k : 16 * k + 16, :] for part in parts], blocks) for k in range(3)]
    index = (passed[0] * 64.0 + passed[1]).astype(jnp.int32)
    weight = passed[2]
    wide = index.shape[1]
    level, column = read_places(table, index - obs)
    for lane in range(0, wide, 256):
        read_forecast(field, level[:, lane : lane + 256], column[:, lane : lane + 256], r_ref, lane)

    tile = lax.axis_index("tile")
    starts = [((tile + tiles + shift) % tiles) * 16 for shift in (-1, 0, 1)]
    one = jnp.where(iota((LANES, wide), 0) == index % LANES, 1.0, 0.0).astype(BF16)
    pick = iota((48, wide), 0) == index // LANES

    def looked_up(ref):
        window = jnp.concatenate([ref[pl.ds(pl.multiple_of(s, 16), 16), :] for s in starts], axis=0)
        high, middle, low = [dot(piece, one) for piece in split3(window)]
        return jnp.sum(jnp.where(pick, (high + middle) + low, 0.0), axis=0, keepdims=True)

    weight_ref[...] = jnp.broadcast_to(looked_up(rinv_ref) * (weight / 3.0), weight_ref.shape)
    target_ref[...] = jnp.broadcast_to(looked_up(value_ref), target_ref.shape)


def merge_kernel(own_ref, a_ref, b_ref, *refs):
    out_ref = refs[-1]
    out_ref[...] = (
        own_ref[...].astype(F32) + (a_ref[...].astype(F32) + b_ref[...].astype(F32))
    ).astype(BF16)


def doubled(high, low):
    top = jnp.concatenate([high, low], axis=1)
    bottom = jnp.concatenate([high, jnp.zeros_like(low)], axis=1)
    return jnp.concatenate([top, bottom], axis=0)


def product(left, right):
    both = dot(left, right)
    wide = both.shape[1] // 2
    return both[:, :wide] + both[:, wide:]


def joined(pair):
    return jnp.concatenate(pair, axis=1)


def weights_kernel(*refs, others):
    r_refs = refs[: others + 1]
    weight_ref, target_ref = refs[others + 1 : others + 3]
    out_ref, pert, weighted, turned, gram_right, hat, inner, outer = refs[-8:]
    members, wide = r_refs[0].shape
    blocks = wide // LANES
    ensemble = members * (others + 1)
    free = ensemble - 1.0

    parts = [ref[...].astype(F32) for ref in r_refs]
    total = sum(jnp.sum(part, axis=0, keepdims=True) for part in parts)
    mean = total * (1.0 / ensemble)
    weight = weight_ref[0:1, :]
    for k, part in enumerate(parts):
        rounded = (part - mean).astype(BF16)
        pert[k * members : (k + 1) * members, :] = rounded
        weighted[k * members : (k + 1) * members, :] = (rounded.astype(F32) * weight).astype(BF16)
    departure = target_ref[0:1, :] - mean

    eye = iota((LANES, LANES), 0) == iota((LANES, LANES), 1)

    def spread(value):
        return jnp.where(eye, value, 0.0)

    scales, xs, zs, grams, lefts, inners = [], [], [], [], [], []
    for b in range(blocks):
        lanes = slice(b * LANES, (b + 1) * LANES)
        turned[b] = weighted[:, lanes].T
    for b in range(blocks):
        lanes = slice(b * LANES, (b + 1) * LANES)
        grams.append(dot(turned[b], pert[:, lanes]))
    for b in range(blocks):
        trace = jnp.sum(jnp.sum(spread(grams[b]), axis=0, keepdims=True), axis=1, keepdims=True)
        scales.append(jnp.broadcast_to(1.0 / (free + trace), (1, LANES)))
    for b in range(blocks):
        gram = grams[b] * scales[b]
        x = free * scales[b]
        gram_right[b] = doubled(*split2(gram))
        m = 1.5 - 0.5 * x
        factor = spread(m) - 0.5 * gram
        v = m * x
        inners.append(
            product(joined(split2(factor)), doubled(*split2(factor - spread(0.5 * x))))
            - spread(0.5 * v)
        )
        xs.append(m * v)
        zs.append(m)
    for b in range(blocks):
        inner[b] = inners[b]
        hat[b] = spread(xs[b]) + product(joined(split2(inners[b])), gram_right[b])

    for turn in range(1, NS_ITERS - 1):
        lefts, halves = [], []
        for b in range(blocks):
            x, z = xs[b], zs[b]
            factor = spread(jnp.full((1, LANES), 1.5, F32)) - 0.5 * hat[b]
            f_high, f_low = split2(factor)
            lefts.append(joined((f_high, f_low)))
            inside = inner[b]
            if turn == 1:
                halves.append(product(lefts[b], doubled(*split2(inside))) - (0.5 * x) * inside)
                outer[b] = -0.5 * factor - (0.5 * z) * inside
                continue
            i_high, i_low = split2(inside)
            o_high, o_low = split2(outer[b])
            right_high = joined((i_high, o_high))
            both = dot(lefts[b], jnp.concatenate([right_high, right_high], axis=0)) + dot(
                f_high, joined((i_low, o_low))
            )
            halves.append(both[:, :LANES] - (0.5 * x) * inside)
            outer[b] = both[:, LANES:] - (0.5 * z) * inside
        for b in range(blocks):
            m = 1.5 - 0.5 * xs[b]
            inner[b] = product(lefts[b], doubled(*split2(halves[b]))) - (0.5 * m * xs[b]) * inner[b]
        for b in range(blocks):
            m = 1.5 - 0.5 * xs[b]
            xs[b] = m * m * xs[b]
            zs[b] = m * zs[b]
            hat[b] = spread(xs[b]) + product(joined(split2(inner[b])), gram_right[b])

    own = iota((members, ensemble), 0) == iota((members, ensemble), 1)
    lasts, rights, rows, cores = [], [], [], []
    for b in range(blocks):
        x, z = xs[b], zs[b]
        factor = spread(jnp.full((1, LANES), 1.5, F32)) - 0.5 * hat[b]
        last = product(joined(split2(factor)), doubled(*split2(outer[b]))) - (0.5 * z) * inner[b]
        zs[b] = (1.5 - 0.5 * x) * z
        lasts.append(split2(last))
    for b in range(blocks):
        rights.append(doubled(*lasts[b]))
        rows.append(jnp.broadcast_to(departure[:, b * LANES : (b + 1) * LANES], (8, LANES)))
    for _ in range(2):
        moved = [product(joined(split2(rows[b])), rights[b]) for b in range(blocks)]
        moved = [product(joined(split2(moved[b])), gram_right[b]) for b in range(blocks)]
        rows = [zs[b] * rows[b] + moved[b] for b in range(blocks)]
    for b in range(blocks):
        mine = pert[:members, b * LANES : (b + 1) * LANES]
        cores.append(dot(joined((mine, mine)), jnp.concatenate(lasts[b], axis=0)))
    for b in range(blocks):
        root = jnp.sqrt(free * scales[b])
        core = cores[b] * (root * scales[b])
        row = rows[b] * scales[b]
        all_rows = joined(split2(jnp.concatenate([core, row, row], axis=0)))
        found = dot(all_rows, jnp.concatenate([turned[b], turned[b]], axis=0))
        diagonal = jnp.where(own, (root * zs[b])[:, 0:1], 0.0)
        out_ref[b] = (found[:members, :] + found[members : members + 1, :] + diagonal).astype(BF16)


def updated(left, parts, width):
    members = parts[0].shape[0]
    parts = [part.astype(F32) for part in parts]
    total = sum(jnp.sum(part, axis=0, keepdims=True) for part in parts)
    mean = total * (1.0 / (members * len(parts)))
    found = dot(left, jnp.concatenate([(part - mean).astype(BF16) for part in parts], axis=0))
    result = found[:members, :]
    lane = iota(result.shape, 1)
    for k in range(1, LANES // width):
        result = jnp.where(lane < k * width, result, found[k * members : (k + 1) * members, :])
    return result + mean


def weights_of(weight_ref, group, columns):
    per = weight_ref.shape[0] * LANES // columns
    return jnp.concatenate([weight_ref[group * per + k] for k in range(per)], axis=0)


def update_kernel(*refs, others):
    count = others + 1
    middles, firsts, afters = [refs[k * count : (k + 1) * count] for k in range(3)]
    weight_ref, out_hbm, rest_ref, stage, done, sems = refs[3 * count :]
    members, levels, columns = out_hbm.shape
    width = columns // weight_ref.shape[0]
    part = levels // 2
    groups = columns // LANES
    copies = []
    for group in (*range(1, groups - 1), 0):
        left = weights_of(weight_ref, group, columns)
        for level in range(levels):
            place = (group - 1) * levels + level
            if group == groups - 2 and level >= part:
                parts = [ref[level - part] for ref in firsts]
            elif group:
                parts = [ref[place] for ref in middles]
            elif level < part:
                parts = [ref[part + level] for ref in firsts]
            else:
                parts = [ref[level - part] for ref in afters]
            stage[group, pl.ds(level, members, stride=levels), :] = updated(left, parts, width)
        done[group] = stage[group].reshape(members, levels, LANES).astype(BF16)
        lanes = slice(group * LANES, (group + 1) * LANES)
        copies.append(pltpu.make_async_copy(done.at[group], out_hbm.at[:, :, lanes], sems.at[group]))
        copies[-1].start()
    left = weights_of(weight_ref, groups - 1, columns)
    for level in range(part):
        rest_ref[pl.ds(level, members, stride=levels), :] = updated(
            left, [ref[part + level] for ref in afters], width
        )
    for level in range(part, levels):
        rest_ref[pl.ds(level, members, stride=levels), :] = jnp.zeros((members, LANES), F32)
    for copy in copies:
        copy.wait()


def finish_kernel(*refs, others):
    count = others + 1
    lasts = refs[:count]
    weight_ref, rest_ref, _, out_hbm, stage, done, sem = refs[count:]
    members, levels, columns = out_hbm.shape
    width = columns // weight_ref.shape[0]
    part = levels // 2
    left = weights_of(weight_ref, columns // LANES - 1, columns)
    stage[...] = rest_ref[...]
    for level in range(part):
        stage[pl.ds(part + level, members, stride=levels), :] = updated(
            left, [ref[level] for ref in lasts], width
        )
    done[...] = stage[...].reshape(members, levels, LANES).astype(BF16)
    copy = pltpu.make_async_copy(done, out_hbm.at[:, :, columns - LANES : columns], sem)
    copy.start()
    copy.wait()


def vmem():
    return pl.BlockSpec(memory_space=pltpu.VMEM)


def group_spec(rows, group):
    return pl.BlockSpec((rows, LANES), lambda i: (0, group))


def call(kernel, outs, inputs, scratch=(), in_specs=None, out_specs=None, aliases=None, cost=0, limit=VMEM_LIMIT):
    return pl.pallas_call(
        kernel,
        grid=(1,),
        out_shape=outs,
        in_specs=in_specs or [vmem()] * len(inputs),
        out_specs=out_specs or [vmem()] * len(outs),
        scratch_shapes=list(scratch),
        input_output_aliases=aliases or {},
        compiler_params=pltpu.CompilerParams(vmem_limit_bytes=limit),
        cost_estimate=pl.CostEstimate(flops=cost << 30, bytes_accessed=1 << 10, transcendentals=0),
    )(*inputs)


def shards(
    fields,
    coefficients,
    neighbours,
    obs_cell,
    obs_level,
    obs_value,
    obs_rinv,
    obs_index,
    obs_weight,
):
    tiles = lax.axis_size("tile")
    sharers = lax.axis_size("mem")
    others = sharers - 1
    members, levels, columns = fields.shape
    blocks = obs_index.shape[0]
    entries = blocks * sharers * LANES
    half = members * levels // 2
    message = jax.ShapeDtypeStruct((half + 80, LANES), BF16)
    even_pairs = []
    odd_pairs = []
    for i in range(0, tiles, 2):
        even_pairs += [(i, i + 1), (i + 1, i)]
        low, high = i + 1, (i + 2) % tiles
        odd_pairs += [(low, high), (high, low)]
    turns = [[((i + r) % sharers, i) for i in range(sharers)] for r in range(1, sharers)]

    flat = fields.reshape(members * levels, columns)
    groups = columns // LANES
    hbm = pl.BlockSpec(memory_space=pltpu.HBM)
    a, b, lists, small = call(
        functools.partial(pack_kernel, tiles=tiles),
        [
            message,
            message,
            jax.ShapeDtypeStruct((48, LANES), BF16),
            jax.ShapeDtypeStruct((16, columns), F32),
        ],
        [flat, coefficients, neighbours, obs_index, obs_weight],
        [
            pltpu.VMEM((members * levels, LANES), F32),
            pltpu.VMEM((members * levels, LANES), F32),
            pltpu.VMEM((6, columns), F32),
            pltpu.VMEM((6, columns), jnp.int32),
            pltpu.VMEM(obs_index.shape, jnp.int32),
            pltpu.VMEM(obs_index.shape, jnp.int32),
            pltpu.SemaphoreType.DMA((6,)),
        ],
        in_specs=[hbm] * 5,
        limit=64 * 1024 * 1024,
    )
    from_b = lax.ppermute(b, "tile", even_pairs)
    from_a = lax.ppermute(a, "tile", odd_pairs)
    flat_rows = members * levels
    middle, kept, edge_high, edge_low, part, second = call(
        functools.partial(middle_kernel, groups=groups),
        [
            jax.ShapeDtypeStruct(((groups - 2) * levels - levels // 2, members, LANES), BF16),
            jax.ShapeDtypeStruct((levels // 2, members, LANES), BF16),
            jax.ShapeDtypeStruct((2, flat_rows, 2 * LANES), BF16),
            jax.ShapeDtypeStruct((2, flat_rows, 2 * LANES), BF16),
            jax.ShapeDtypeStruct((2, 2 * LANES, LANES), F32),
            jax.ShapeDtypeStruct((4, 2 * LANES, LANES), BF16),
        ],
        [flat] * groups + [small],
        [
            pltpu.VMEM((flat_rows, columns), BF16),
            pltpu.VMEM((flat_rows, columns), BF16),
            pltpu.VMEM((columns, columns - LANES), BF16),
            pltpu.VMEM((columns, columns - LANES), BF16),
            pltpu.VMEM((columns - LANES, columns - 2 * LANES), BF16),
            pltpu.VMEM((columns - LANES, columns - 2 * LANES), BF16),
        ],
        in_specs=[group_spec(flat_rows, group) for group in range(groups)] + [vmem()],
        cost=4,
    )
    passed = jnp.concatenate([from_a[half + 48 :], from_b[half + 48 :], lists], axis=0)

    def swapped(value, sent):
        return [value] + [lax.ppermute(sent, "mem", turn) for turn in turns]

    passed, sent = lax.optimization_barrier((passed, middle))
    middles = swapped(middle, sent)
    passed = [lax.ppermute(passed, "mem", turn) for turn in turns]
    first, after, last = call(
        edge_kernel,
        [
            jax.ShapeDtypeStruct((levels, members, LANES), BF16),
            jax.ShapeDtypeStruct((levels, members, LANES), BF16),
            jax.ShapeDtypeStruct((levels // 2, members, LANES), BF16),
        ],
        [from_a, from_b, small, edge_high, edge_low, part, second, kept],
        [pltpu.VMEM((2, flat_rows, 2 * LANES), BF16)],
        cost=2,
    )
    pieces = [middle, first, after, last]
    cell = obs_cell.reshape(16, LANES)
    level = obs_level.reshape(16, LANES)
    reading = jax.ShapeDtypeStruct((members, entries), BF16)
    table = pltpu.VMEM((48, LANES), BF16)
    to_neighbour = []
    for turn, received in enumerate((from_a, from_b)):
        inputs = [*pieces, received, *passed, cell, level]
        to_neighbour += call(
            functools.partial(
                neighbour_kernel, others=others, blocks=blocks, turn=turn
            ),
            [reading],
            [*inputs, *to_neighbour],
            [table],
            in_specs=[vmem()] * len(inputs) + [pl.BlockSpec(memory_space=pl.ANY)] * turn,
            cost=2,
        )
    to_a, to_b = to_neighbour
    to_b, sent = lax.optimization_barrier((to_b, first))
    firsts = swapped(first, sent)
    back_a = lax.ppermute(to_a, "tile", odd_pairs)
    back_b = lax.ppermute(to_b, "tile", even_pairs)
    vector = jax.ShapeDtypeStruct((8, entries), F32)
    own, weight, target = call(
        functools.partial(own_kernel, others=others, blocks=blocks, tiles=tiles),
        [reading, vector, vector],
        [
            *pieces,
            lists,
            *passed,
            cell,
            level,
            obs_value.reshape(-1, LANES),
            obs_rinv.reshape(-1, LANES),
        ],
        [table],
        cost=2,
    )
    unused = middles[1:]
    (readings,) = call(
        merge_kernel,
        [reading],
        [own, back_a, back_b, *unused],
        in_specs=[vmem()] * 3 + [pl.BlockSpec(memory_space=pl.ANY)] * len(unused),
        cost=0,
    )
    readings, sent, sent_last = lax.optimization_barrier((readings, after, last))
    readings = swapped(readings, readings)
    afters = swapped(after, sent)
    lasts = swapped(last, sent_last)
    unused = firsts[1:]
    ensemble = members * sharers
    total = blocks * sharers
    square = pltpu.VMEM((total, LANES, LANES), F32)
    (weights,) = call(
        functools.partial(weights_kernel, others=others),
        [jax.ShapeDtypeStruct((total, members, ensemble), BF16)],
        [*readings, weight, target, *unused],
        [
            pltpu.VMEM((ensemble, entries), BF16),
            pltpu.VMEM((ensemble, entries), BF16),
            pltpu.VMEM((total, LANES, ensemble), BF16),
            pltpu.VMEM((total, 2 * LANES, 2 * LANES), BF16),
            square,
            square,
            square,
        ],
        in_specs=[vmem()] * (sharers + 2) + [pl.BlockSpec(memory_space=pl.ANY)] * len(unused),
        cost=8,
    )
    rows = members * levels
    result = jax.ShapeDtypeStruct((members, levels, columns), BF16)
    inputs = [*middles, *firsts, *afters, weights]
    analysis, rest = call(
        functools.partial(update_kernel, others=others),
        [result, jax.ShapeDtypeStruct((rows, LANES), F32)],
        inputs,
        [
            pltpu.VMEM((groups - 1, rows, LANES), F32),
            pltpu.VMEM((groups - 1, members, levels, LANES), BF16),
            pltpu.SemaphoreType.DMA((groups - 1,)),
        ],
        out_specs=[hbm, vmem()],
        cost=2,
    )
    inputs = [*lasts, weights, rest, analysis]
    (analysis,) = call(
        functools.partial(finish_kernel, others=others),
        [result],
        inputs,
        [
            pltpu.VMEM((rows, LANES), F32),
            pltpu.VMEM((members, levels, LANES), BF16),
            pltpu.SemaphoreType.DMA,
        ],
        in_specs=[vmem()] * (len(inputs) - 1) + [hbm],
        out_specs=[hbm],
        aliases={len(inputs) - 1: 0},
        cost=1,
    )
    return analysis


def solution(mesh):
    in_specs = (
        P("mem", None, "tile"),
        P(None, "tile"),
        P(None, "tile"),
        P("tile"),
        P("tile"),
        P(),
        P(),
        P("mem", "tile", None),
        P("mem", "tile", None),
    )
    out_specs = P("mem", None, "tile")
    return jax.shard_map(shards, mesh=mesh, in_specs=in_specs, out_specs=out_specs, check_vma=False)
```

```python
import functools

import jax
import jax.numpy as jnp
from jax import lax
from jax.experimental import pallas as pl
from jax.experimental.pallas import tpu as pltpu
from jax.sharding import PartitionSpec as P

HALO = 32
NS_ITERS = 8
LANES = 128
F32 = jnp.float32
BF16 = jnp.bfloat16
VMEM_LIMIT = 48 * 1024 * 1024

NN = (((1,), (0,)), ((), ()))
NT = (((1,), (1,)), ((), ()))
TN = (((0,), (0,)), ((), ()))


def dot(a, b, dims=NN):
    return lax.dot_general(a, b, dims, preferred_element_type=F32)


def split2(x):
    high = x.astype(BF16)
    return high, (x - high.astype(F32)).astype(BF16)


def split3(x):
    high = x.astype(BF16)
    rest = x - high.astype(F32)
    middle = rest.astype(BF16)
    return high, middle, (rest - middle.astype(F32)).astype(BF16)


def iota(shape, dim):
    return lax.broadcasted_iota(jnp.int32, shape, dim)


def is_odd_tile():
    return lax.axis_index("tile") % 2 == 1


def message_rows(field_rows):
    names = ("coef_high", "coef_low", "offset", "list_high", "list_low")
    return {name: field_rows + 16 * place for place, name in enumerate(names)}


def pack_kernel(
    field_hbm,
    coef_hbm,
    nbr_hbm,
    index_hbm,
    weight_hbm,
    a_ref,
    b_ref,
    lists_ref,
    small_ref,
    left_ref,
    right_ref,
    coef_ref,
    nbr_ref,
    index_ref,
    weight_ref,
    sems,
    *,
    tiles,
):
    columns = coef_ref.shape[1]
    levels = 8
    half = left_ref.shape[0] // 2
    members = half // levels
    rows = message_rows(half)
    odd = is_odd_tile()
    total = columns * tiles
    copies = [
        pltpu.make_async_copy(source, target, sems.at[k])
        for k, (source, target) in enumerate(
            (
                (coef_hbm, coef_ref),
                (nbr_hbm, nbr_ref),
                (index_hbm, index_ref),
                (weight_hbm, weight_ref),
                (field_hbm.at[:, 0:LANES], left_ref),
                (field_hbm.at[:, columns - LANES : columns], right_ref),
            )
        )
    ]
    for copy in copies:
        copy.start()
    for copy in copies[:4]:
        copy.wait()

    place = lax.axis_index("tile") * columns + iota((6, columns), 1)
    offset = nbr_ref[...] - place
    offset = jnp.where(offset > HALO, offset - total, offset)
    offset = jnp.where(offset < -HALO, offset + total, offset).astype(F32)
    small_ref[...] = jnp.zeros_like(small_ref)
    small_ref[0:6, :] = coef_ref[...]
    small_ref[8:14, :] = offset
    coef_high, coef_low = split2(coef_ref[...])
    for name, value in (
        ("coef_high", coef_high.astype(F32)),
        ("coef_low", coef_low.astype(F32)),
        ("offset", offset),
    ):
        first = padded(value[:, :LANES], 10)
        last = padded(value[:, columns - LANES :], 10)
        start = rows[name]
        a_ref[start : start + 16, :] = jnp.where(odd, last, first).astype(BF16)
        b_ref[start : start + 16, :] = jnp.where(odd, first, last).astype(BF16)
    blocks = index_ref.shape[0]
    index = padded(index_ref[:, 0, :].astype(F32), 16 - blocks)
    high = jnp.floor(index * (1.0 / 64.0))
    for k, value in enumerate((high, index - 64.0 * high)):
        value = value.astype(BF16)
        start = rows["list_high"] + 16 * k
        a_ref[start : start + 16, :] = value
        b_ref[start : start + 16, :] = value
        lists_ref[16 * k : 16 * k + 16, :] = value
    lists_ref[32:48, :] = padded(weight_ref[:, 0, :].astype(F32), 16 - blocks).astype(BF16)

    for copy in copies[4:]:
        copy.wait()
    lane = iota((members, LANES), 1)
    for level in range(levels):
        top = pl.ds(level, members, stride=levels)
        low = pl.ds(level + half, members, stride=levels)
        spot = slice(level * members, (level + 1) * members)
        left = jnp.where(lane < 64, left_ref[top, :], pltpu.roll(left_ref[low, :], 64, axis=1))
        right = jnp.where(lane < 64, pltpu.roll(right_ref[top, :], 64, axis=1), right_ref[low, :])
        a_ref[spot, :] = jnp.where(odd, right, left).astype(BF16)
        b_ref[spot, :] = jnp.where(odd, left, right).astype(BF16)


def band(coefs, offsets):
    shape = (LANES + 2 * HALO, LANES)
    spot = iota(shape, 0)
    result = jnp.where(
        spot == iota(shape, 1) + HALO, 1.0 - jnp.sum(coefs, axis=0, keepdims=True), 0.0
    )
    target = iota(offsets.shape, 1) + HALO + offsets.astype(jnp.int32)
    for j in range(6):
        result = result + jnp.where(spot == target[j : j + 1, :], coefs[j : j + 1, :], 0.0)
    return result


def dot3(left, right):
    return dot(left[0], right[0]) + (dot(left[0], right[1]) + dot(left[1], right[0]))


def padded(value, count):
    return jnp.concatenate([value, jnp.zeros((count, value.shape[1]), value.dtype)], axis=0)


def middle_kernel(*refs, groups):
    field_refs = refs[:groups]
    small_ref, middle_ref, kept_ref = refs[groups : groups + 3]
    (
        edge_high,
        edge_low,
        part_ref,
        second_ref,
        u_high,
        u_low,
        first_high,
        first_low,
        second_high,
        second_low,
    ) = refs[groups + 3 :]
    late, members, _ = kept_ref.shape
    levels = 2 * late
    early = (groups - 2) * levels - late
    columns = groups * LANES
    coef = padded(small_ref[0:6, :], 2)
    reach = padded(small_ref[8:14, :], 2)
    moved_coef = pltpu.roll(coef, HALO, axis=1)
    moved_reach = pltpu.roll(reach, HALO, axis=1)

    def lanes(value, group):
        return value[:, group * LANES : (group + 1) * LANES]

    firsts = {
        g: split2(band(lanes(moved_coef, g), lanes(moved_reach, g))) for g in range(1, groups)
    }
    seconds = [split2(band(lanes(coef, g), lanes(reach, g))) for g in range(groups)]
    for ref in (first_high, first_low, second_high, second_low):
        ref[...] = jnp.zeros_like(ref)
    for g in range(1, groups):
        row, lane = g * LANES - 64, (g - 1) * LANES
        count = min(LANES + 2 * HALO, columns - row)
        first_high[row : row + count, lane : lane + LANES] = firsts[g][0][:count, :]
        first_low[row : row + count, lane : lane + LANES] = firsts[g][1][:count, :]
    for g in range(1, groups - 1):
        row, lane = (g - 1) * LANES, (g - 1) * LANES
        second_high[row : row + LANES + 2 * HALO, lane : lane + LANES] = seconds[g][0]
        second_low[row : row + LANES + 2 * HALO, lane : lane + LANES] = seconds[g][1]
    both = split2(
        dot3((first_high[...], first_low[...]), (second_high[...], second_low[...]))
    )

    for k, g in enumerate((0, groups - 1)):
        second = [padded(value, 64) for value in seconds[g]]
        for j in range(2):
            second_ref[2 * k + j] = second[j]
        if k == 0:
            part = dot3([value[:128, :] for value in firsts[1]], [value[128:, :] for value in second])
            part_ref[k] = jnp.concatenate([jnp.zeros_like(part), part], axis=0)
        else:
            part_ref[k] = padded(dot3(firsts[g], [value[:128, :] for value in second]), 64)

    lane = iota((members, LANES), 1)
    for level in range(levels):
        spot = slice(level * members, (level + 1) * members)
        for group, ref in enumerate(field_refs):
            own = ref[pl.ds(level, members, stride=levels), :]
            high, low = split2(own)
            u_high[spot, group * LANES : (group + 1) * LANES] = high
            u_low[spot, group * LANES : (group + 1) * LANES] = low
        for pieces, ref in ((u_high, edge_high), (u_low, edge_low)):
            turned = [
                pltpu.roll(pieces[spot, g * LANES : (g + 1) * LANES].astype(F32), 64, axis=1)
                for g in (0, 1, groups - 2, groups - 1)
            ]
            zero = jnp.zeros_like(turned[0])
            ref[0, spot, 0:LANES] = jnp.where(lane < 64, zero, turned[0]).astype(BF16)
            ref[0, spot, LANES:] = jnp.where(lane < 64, turned[0], turned[1]).astype(BF16)
            ref[1, spot, 0:LANES] = jnp.where(lane < 64, turned[2], turned[3]).astype(BF16)
            ref[1, spot, LANES:] = jnp.where(lane < 64, turned[3], zero).astype(BF16)
    result = dot3((u_high[...], u_low[...]), both)
    for k in range((groups - 2) * levels):
        level, lane = k % levels, (k // levels) * LANES
        value = result[level * members : (level + 1) * members, lane : lane + LANES].astype(BF16)
        if k < early:
            middle_ref[k] = value
        else:
            kept_ref[k - early] = value


def edge_kernel(
    a_ref, b_ref, small_ref, edge_high, edge_low, part_ref, second_ref, kept_ref, first_ref, next_ref, last_ref, u_high
):
    levels, members, _ = next_ref.shape
    columns = small_ref.shape[1]
    half = members // 2
    rows = message_rows(levels * half)
    odd = is_odd_tile()

    def side(k, start, count):
        a = a_ref[start : start + count, :].astype(F32)
        b = b_ref[start : start + count, :].astype(F32)
        return jnp.where(odd, b, a) if k == 0 else jnp.where(odd, a, b)

    own_coef = padded(small_ref[0:6, :], 2)
    own_reach = padded(small_ref[8:14, :], 2)
    lane8 = iota((8, LANES), 1)
    lane = iota((half, LANES), 1)
    operators = []
    for k in range(2):
        near = side(k, rows["coef_high"], 16)[:8] + side(k, rows["coef_low"], 16)[:8]
        reach = side(k, rows["offset"], 16)[:8]
        if k == 0:
            own = (own_coef[:, :LANES], own_reach[:, :LANES])
            both = [
                jnp.where(
                    lane8 < HALO, pltpu.roll(x, HALO, axis=1), pltpu.roll(y, HALO, axis=1)
                )
                for x, y in zip((near, reach), own)
            ]
            first = split2(band(*both))
            second = [second_ref[j, :128, :] for j in range(2)]
            fresh = padded(dot3(first, second), 64)
        else:
            own = (own_coef[:, columns - LANES :], own_reach[:, columns - LANES :])
            both = [
                jnp.where(
                    lane8 < HALO, pltpu.roll(y, HALO, axis=1), pltpu.roll(x, HALO, axis=1)
                )
                for x, y in zip((near, reach), own)
            ]
            first = [value[:128, :] for value in split2(band(*both))]
            second = [second_ref[2 + j, 128:, :] for j in range(2)]
            fresh = dot3(first, second)
            fresh = jnp.concatenate([jnp.zeros_like(fresh), fresh], axis=0)
        operators.append(split2(part_ref[k] + fresh))
    for k in range(2):
        for level in range(levels):
            top = level * members
            halo = side(k, level * half, half)
            other = pltpu.roll(halo, 64, axis=1)
            pair = (halo, other) if k == 0 else (other, halo)
            for j in range(2):
                spot = slice(top + j * half, top + (j + 1) * half)
                if k == 0:
                    own = edge_high[k, spot, 0:LANES].astype(F32)
                    u_high[k, spot, 0:LANES] = jnp.where(lane < 64, pair[j], own).astype(BF16)
                    u_high[k, spot, LANES:] = edge_high[k, spot, LANES:]
                else:
                    own = edge_high[k, spot, LANES:].astype(F32)
                    u_high[k, spot, LANES:] = jnp.where(lane < 64, own, pair[j]).astype(BF16)
                    u_high[k, spot, 0:LANES] = edge_high[k, spot, 0:LANES]
        result = dot3((u_high[k], edge_low[k]), operators[k])
        part = levels // 2
        if k == 0:
            first_ref[:part] = kept_ref[...]
        for level in range(levels):
            value = result[level * members : (level + 1) * members, :].astype(BF16)
            if k == 0 and level < part:
                first_ref[part + level] = value
            elif k == 0:
                next_ref[level - part] = value
            elif level < part:
                next_ref[part + level] = value
            else:
                last_ref[level - part] = value


def gather_lists(parts, blocks):
    count = len(parts)
    me = lax.axis_index("mem")
    rows = [
        jnp.concatenate([part[b : b + 1, :].astype(F32) for b in range(blocks)], axis=1)
        for part in parts
    ]
    placed = []
    for place in range(count):
        value = rows[0]
        for shift in range(1, count):
            value = jnp.where((me + shift) % count == place, rows[shift], value)
        placed.append(value)
    return jnp.concatenate(placed, axis=1)


def read_places(table_ref, slot):
    wide = slot.shape[1]
    valid = (slot >= 0) & (slot < 16 * LANES)
    slot = jnp.where(valid, slot, 0)
    one = jnp.where(iota((LANES, wide), 0) == slot % LANES, 1.0, 0.0).astype(BF16)
    found = dot(table_ref[...], one)
    pick = iota((16, wide), 0) == slot // LANES
    values = [
        jnp.sum(jnp.where(pick, found[16 * k : 16 * k + 16, :], 0.0), axis=0, keepdims=True)
        for k in range(3)
    ]
    column = (values[1] * 16.0 + values[2]).astype(jnp.int32)
    return values[0].astype(jnp.int32), jnp.where(valid, column, -1)


def make_table(cell_ref, level_ref, table):
    cell = cell_ref[...]
    table[0:16, :] = level_ref[...].astype(F32).astype(BF16)
    table[16:32, :] = (cell // 16).astype(F32).astype(BF16)
    table[32:48, :] = (cell % 16).astype(F32).astype(BF16)


def read_forecast(field, level, column, out_ref, lane):
    members = out_ref.shape[0]
    wide = level.shape[1]
    one = jnp.where(iota((field.shape[1], wide), 0) == column, 1.0, 0.0).astype(BF16)
    found = dot(field, one)
    total = jnp.zeros((members, wide), F32)
    for l in range(field.shape[0] // members):
        total = total + jnp.where(level == l, found[l * members : (l + 1) * members, :], 0.0)
    out_ref[:, lane : lane + wide] = total.astype(BF16)


def whole(middle_ref, first_ref, next_ref, last_ref):
    part, members, _ = last_ref.shape
    middle = jnp.concatenate([middle_ref[...], first_ref[:part]], axis=0)
    groups = [
        jnp.concatenate([first_ref[part:], next_ref[:part]], axis=0),
        *(middle[k : k + 2 * part] for k in range(0, middle.shape[0], 2 * part)),
        jnp.concatenate([next_ref[part:], last_ref[...]], axis=0),
    ]
    return joined([group.reshape(-1, LANES) for group in groups])


def neighbour_kernel(*refs, others, blocks, turn):
    message_ref = refs[4]
    other_refs = refs[5 : 5 + others]
    cell_ref, level_ref = refs[5 + others : 7 + others]
    out_ref, table = refs[-2:]
    half = message_ref.shape[0] - 80
    rows = message_rows(half)
    odd = is_odd_tile()
    obs = 16 * LANES
    make_table(cell_ref, level_ref, table)
    field = whole(*refs[:4])
    base = 32 * turn
    parts = [message_ref[rows["list_high"] : rows["list_high"] + 32, :]]
    parts += [r[base : base + 32, :] for r in other_refs]
    high = gather_lists([part[:16, :] for part in parts], blocks)
    low = gather_lists([part[16:, :] for part in parts], blocks)
    index = (high * 64.0 + low).astype(jnp.int32)
    skip = jnp.where(odd, 0, 2 * obs) if turn == 0 else jnp.where(odd, 2 * obs, 0)
    level, column = read_places(table, index - skip)
    for lane in range(0, index.shape[1], 256):
        read_forecast(
            field, level[:, lane : lane + 256], column[:, lane : lane + 256], out_ref, lane
        )


def own_kernel(*refs, others, blocks, tiles):
    lists_ref = refs[4]
    other_refs = refs[5 : 5 + others]
    (
        cell_ref,
        level_ref,
        value_ref,
        rinv_ref,
        r_ref,
        weight_ref,
        target_ref,
        table,
    ) = refs[5 + others :]
    obs = 16 * LANES
    make_table(cell_ref, level_ref, table)
    field = whole(*refs[:4])

    parts = [lists_ref[...]] + [r[64:112, :] for r in other_refs]
    passed = [gather_lists([part[16 * k : 16 * k + 16, :] for part in parts], blocks) for k in range(3)]
    index = (passed[0] * 64.0 + passed[1]).astype(jnp.int32)
    weight = passed[2]
    wide = index.shape[1]
    level, column = read_places(table, index - obs)
    for lane in range(0, wide, 256):
        read_forecast(field, level[:, lane : lane + 256], column[:, lane : lane + 256], r_ref, lane)

    tile = lax.axis_index("tile")
    starts = [((tile + tiles + shift) % tiles) * 16 for shift in (-1, 0, 1)]
    one = jnp.where(iota((LANES, wide), 0) == index % LANES, 1.0, 0.0).astype(BF16)
    pick = iota((48, wide), 0) == index // LANES

    def looked_up(ref):
        window = jnp.concatenate([ref[pl.ds(pl.multiple_of(s, 16), 16), :] for s in starts], axis=0)
        high, middle, low = [dot(piece, one) for piece in split3(window)]
        return jnp.sum(jnp.where(pick, (high + middle) + low, 0.0), axis=0, keepdims=True)

    weight_ref[...] = jnp.broadcast_to(looked_up(rinv_ref) * (weight / 3.0), weight_ref.shape)
    target_ref[...] = jnp.broadcast_to(looked_up(value_ref), target_ref.shape)


def merge_kernel(one_ref, other_ref, *refs):
    out_ref = refs[-1]
    out_ref[...] = (one_ref[...].astype(F32) + other_ref[...].astype(F32)).astype(BF16)


def doubled(high, low):
    top = jnp.concatenate([high, low], axis=1)
    bottom = jnp.concatenate([high, jnp.zeros_like(low)], axis=1)
    return jnp.concatenate([top, bottom], axis=0)


def product(left, right):
    both = dot(left, right)
    wide = both.shape[1] // 2
    return both[:, :wide] + both[:, wide:]


def joined(pair):
    return jnp.concatenate(pair, axis=1)


def weights_kernel(*refs, others):
    r_refs = refs[: others + 1]
    weight_ref, target_ref = refs[others + 1 : others + 3]
    out_ref, pert, weighted, turned, gram_right, hat, inner, outer = refs[-8:]
    members, wide = r_refs[0].shape
    blocks = wide // LANES
    ensemble = members * (others + 1)
    free = ensemble - 1.0

    parts = [ref[...].astype(F32) for ref in r_refs]
    total = sum(jnp.sum(part, axis=0, keepdims=True) for part in parts)
    mean = total * (1.0 / ensemble)
    weight = weight_ref[0:1, :]
    for k, part in enumerate(parts):
        rounded = (part - mean).astype(BF16)
        pert[k * members : (k + 1) * members, :] = rounded
        weighted[k * members : (k + 1) * members, :] = (rounded.astype(F32) * weight).astype(BF16)
    departure = target_ref[0:1, :] - mean

    eye = iota((LANES, LANES), 0) == iota((LANES, LANES), 1)

    def spread(value):
        return jnp.where(eye, value, 0.0)

    scales, xs, zs, grams, lefts, inners = [], [], [], [], [], []
    for b in range(blocks):
        lanes = slice(b * LANES, (b + 1) * LANES)
        turned[b] = weighted[:, lanes].T
    for b in range(blocks):
        lanes = slice(b * LANES, (b + 1) * LANES)
        grams.append(dot(turned[b], pert[:, lanes]))
    for b in range(blocks):
        trace = jnp.sum(jnp.sum(spread(grams[b]), axis=0, keepdims=True), axis=1, keepdims=True)
        scales.append(jnp.broadcast_to(1.0 / (free + trace), (1, LANES)))
    for b in range(blocks):
        gram = grams[b] * scales[b]
        x = free * scales[b]
        gram_right[b] = doubled(*split2(gram))
        m = 1.5 - 0.5 * x
        factor = spread(m) - 0.5 * gram
        v = m * x
        inners.append(
            product(joined(split2(factor)), doubled(*split2(factor - spread(0.5 * x))))
            - spread(0.5 * v)
        )
        xs.append(m * v)
        zs.append(m)
    for b in range(blocks):
        inner[b] = inners[b]
        hat[b] = spread(xs[b]) + product(joined(split2(inners[b])), gram_right[b])

    for turn in range(1, NS_ITERS - 1):
        lefts, halves = [], []
        for b in range(blocks):
            x, z = xs[b], zs[b]
            factor = spread(jnp.full((1, LANES), 1.5, F32)) - 0.5 * hat[b]
            f_high, f_low = split2(factor)
            lefts.append(joined((f_high, f_low)))
            inside = inner[b]
            if turn == 1:
                halves.append(product(lefts[b], doubled(*split2(inside))) - (0.5 * x) * inside)
                outer[b] = -0.5 * factor - (0.5 * z) * inside
                continue
            i_high, i_low = split2(inside)
            o_high, o_low = split2(outer[b])
            right_high = joined((i_high, o_high))
            both = dot(lefts[b], jnp.concatenate([right_high, right_high], axis=0)) + dot(
                f_high, joined((i_low, o_low))
            )
            halves.append(both[:, :LANES] - (0.5 * x) * inside)
            outer[b] = both[:, LANES:] - (0.5 * z) * inside
        for b in range(blocks):
            m = 1.5 - 0.5 * xs[b]
            inner[b] = product(lefts[b], doubled(*split2(halves[b]))) - (0.5 * m * xs[b]) * inner[b]
        for b in range(blocks):
            m = 1.5 - 0.5 * xs[b]
            xs[b] = m * m * xs[b]
            zs[b] = m * zs[b]
            hat[b] = spread(xs[b]) + product(joined(split2(inner[b])), gram_right[b])

    own = iota((members, ensemble), 0) == iota((members, ensemble), 1)
    lasts, rights, rows, cores = [], [], [], []
    for b in range(blocks):
        x, z = xs[b], zs[b]
        factor = spread(jnp.full((1, LANES), 1.5, F32)) - 0.5 * hat[b]
        last = product(joined(split2(factor)), doubled(*split2(outer[b]))) - (0.5 * z) * inner[b]
        zs[b] = (1.5 - 0.5 * x) * z
        lasts.append(split2(last))
    for b in range(blocks):
        rights.append(doubled(*lasts[b]))
        rows.append(jnp.broadcast_to(departure[:, b * LANES : (b + 1) * LANES], (8, LANES)))
    for _ in range(2):
        moved = [product(joined(split2(rows[b])), rights[b]) for b in range(blocks)]
        moved = [product(joined(split2(moved[b])), gram_right[b]) for b in range(blocks)]
        rows = [zs[b] * rows[b] + moved[b] for b in range(blocks)]
    for b in range(blocks):
        mine = pert[:members, b * LANES : (b + 1) * LANES]
        cores.append(dot(joined((mine, mine)), jnp.concatenate(lasts[b], axis=0)))
    for b in range(blocks):
        root = jnp.sqrt(free * scales[b])
        core = cores[b] * (root * scales[b])
        row = rows[b] * scales[b]
        all_rows = joined(split2(jnp.concatenate([core, row, row], axis=0)))
        found = dot(all_rows, jnp.concatenate([turned[b], turned[b]], axis=0))
        diagonal = jnp.where(own, (root * zs[b])[:, 0:1], 0.0)
        out_ref[b] = (found[:members, :] + found[members : members + 1, :] + diagonal).astype(BF16)


def departures(pairs):
    count = len(pairs[0])
    ensemble = pairs[0][0].shape[0] * count
    parts = [joined([pair[k].astype(F32) for pair in pairs]) for k in range(count)]
    total = sum(jnp.sum(part, axis=0, keepdims=True) for part in parts)
    mean = total * (1.0 / ensemble)
    return jnp.concatenate([(part - mean).astype(BF16) for part in parts], axis=0), mean


def updated(left, moved, mean, width):
    members = left.shape[0] * width // LANES
    found = dot(left, moved)
    result = found[:members, :]
    lane = iota(result.shape, 1) % LANES
    for k in range(1, LANES // width):
        result = jnp.where(lane < k * width, result, found[k * members : (k + 1) * members, :])
    result = result + mean
    return [result[:, k : k + LANES] for k in range(0, result.shape[1], LANES)]


def weights_of(weight_ref, group, columns):
    per = weight_ref.shape[0] * LANES // columns
    return jnp.concatenate([weight_ref[group * per + k] for k in range(per)], axis=0)


def prepare_kernel(*refs, others):
    count = others + 1
    middles, firsts = [refs[k * count : (k + 1) * count] for k in range(2)]
    moved_ref, mean_ref = refs[2 * count :]
    slot = 0
    for piece in (middles, firsts):
        for k in range(0, piece[0].shape[0], 2):
            moved, mean = departures([[ref[k + j] for ref in piece] for j in range(2)])
            moved_ref[slot] = moved
            mean_ref[slot] = jnp.broadcast_to(mean, mean_ref.shape[1:])
            slot += 1


def update_kernel(*refs, others):
    afters = refs[: others + 1]
    moved_ref, mean_ref, weight_ref, out_hbm, rest_ref, stage, done, sems = refs[others + 1 :]
    members, levels, columns = out_hbm.shape
    width = columns // weight_ref.shape[0]
    part = levels // 2
    groups = columns // LANES

    def rows(level):
        return pl.ds(level, members, stride=levels)

    copies = []
    slot = 0
    for group in (*range(1, groups - 1), 0):
        left = weights_of(weight_ref, group, columns)
        for level in range(0, levels, 2):
            if group or level < part:
                moved, mean = moved_ref[slot], mean_ref[slot, 0:1, :]
                slot += 1
            else:
                moved, mean = departures([[ref[level - part + j] for ref in afters] for j in range(2)])
            for j, value in enumerate(updated(left, moved, mean, width)):
                stage[group, rows(level + j), :] = value
        done[group] = stage[group].reshape(members, levels, LANES).astype(BF16)
        lanes = slice(group * LANES, (group + 1) * LANES)
        copies.append(pltpu.make_async_copy(done.at[group], out_hbm.at[:, :, lanes], sems.at[group]))
        copies[-1].start()
    left = weights_of(weight_ref, groups - 1, columns)
    for level in range(0, part, 2):
        moved, mean = departures([[ref[part + level + j] for ref in afters] for j in range(2)])
        for j, value in enumerate(updated(left, moved, mean, width)):
            rest_ref[rows(level + j), :] = value
    for level in range(part, levels):
        rest_ref[rows(level), :] = jnp.zeros((members, LANES), F32)
    for copy in copies:
        copy.wait()


def finish_kernel(*refs, others):
    lasts = refs[: others + 1]
    weight_ref, rest_ref, _, out_hbm, stage, done, sem = refs[others + 1 :]
    members, levels, columns = out_hbm.shape
    width = columns // weight_ref.shape[0]
    part = levels // 2
    left = weights_of(weight_ref, columns // LANES - 1, columns)
    stage[...] = rest_ref[...]
    for level in range(0, part, 2):
        moved, mean = departures([[ref[level + j] for ref in lasts] for j in range(2)])
        for j, value in enumerate(updated(left, moved, mean, width)):
            stage[pl.ds(part + level + j, members, stride=levels), :] = value
    done[...] = stage[...].reshape(members, levels, LANES).astype(BF16)
    copy = pltpu.make_async_copy(done, out_hbm.at[:, :, columns - LANES : columns], sem)
    copy.start()
    copy.wait()


def vmem():
    return pl.BlockSpec(memory_space=pltpu.VMEM)


def group_spec(rows, group):
    return pl.BlockSpec((rows, LANES), lambda i: (0, group))


def call(kernel, outs, inputs, scratch=(), in_specs=None, out_specs=None, aliases=None, cost=0, limit=VMEM_LIMIT):
    return pl.pallas_call(
        kernel,
        grid=(1,),
        out_shape=outs,
        in_specs=in_specs or [vmem()] * len(inputs),
        out_specs=out_specs or [vmem()] * len(outs),
        scratch_shapes=list(scratch),
        input_output_aliases=aliases or {},
        compiler_params=pltpu.CompilerParams(vmem_limit_bytes=limit),
        cost_estimate=pl.CostEstimate(flops=cost << 30, bytes_accessed=1 << 10, transcendentals=0),
    )(*inputs)


def shards(
    fields,
    coefficients,
    neighbours,
    obs_cell,
    obs_level,
    obs_value,
    obs_rinv,
    obs_index,
    obs_weight,
):
    tiles = lax.axis_size("tile")
    sharers = lax.axis_size("mem")
    others = sharers - 1
    members, levels, columns = fields.shape
    blocks = obs_index.shape[0]
    entries = blocks * sharers * LANES
    half = members * levels // 2
    message = jax.ShapeDtypeStruct((half + 80, LANES), BF16)
    even_pairs = []
    odd_pairs = []
    for i in range(0, tiles, 2):
        even_pairs += [(i, i + 1), (i + 1, i)]
        low, high = i + 1, (i + 2) % tiles
        odd_pairs += [(low, high), (high, low)]
    turns = [[((i + r) % sharers, i) for i in range(sharers)] for r in range(1, sharers)]

    flat = fields.reshape(members * levels, columns)
    groups = columns // LANES
    hbm = pl.BlockSpec(memory_space=pltpu.HBM)
    a, b, lists, small = call(
        functools.partial(pack_kernel, tiles=tiles),
        [
            message,
            message,
            jax.ShapeDtypeStruct((48, LANES), BF16),
            jax.ShapeDtypeStruct((16, columns), F32),
        ],
        [flat, coefficients, neighbours, obs_index, obs_weight],
        [
            pltpu.VMEM((members * levels, LANES), F32),
            pltpu.VMEM((members * levels, LANES), F32),
            pltpu.VMEM((6, columns), F32),
            pltpu.VMEM((6, columns), jnp.int32),
            pltpu.VMEM(obs_index.shape, jnp.int32),
            pltpu.VMEM(obs_index.shape, jnp.int32),
            pltpu.SemaphoreType.DMA((6,)),
        ],
        in_specs=[hbm] * 5,
        limit=64 * 1024 * 1024,
    )
    from_b = lax.ppermute(b, "tile", even_pairs)
    from_a = lax.ppermute(a, "tile", odd_pairs)
    flat_rows = members * levels
    middle, kept, edge_high, edge_low, part, second = call(
        functools.partial(middle_kernel, groups=groups),
        [
            jax.ShapeDtypeStruct(((groups - 2) * levels - levels // 2, members, LANES), BF16),
            jax.ShapeDtypeStruct((levels // 2, members, LANES), BF16),
            jax.ShapeDtypeStruct((2, flat_rows, 2 * LANES), BF16),
            jax.ShapeDtypeStruct((2, flat_rows, 2 * LANES), BF16),
            jax.ShapeDtypeStruct((2, 2 * LANES, LANES), F32),
            jax.ShapeDtypeStruct((4, 2 * LANES, LANES), BF16),
        ],
        [flat] * groups + [small],
        [
            pltpu.VMEM((flat_rows, columns), BF16),
            pltpu.VMEM((flat_rows, columns), BF16),
            pltpu.VMEM((columns, columns - LANES), BF16),
            pltpu.VMEM((columns, columns - LANES), BF16),
            pltpu.VMEM((columns - LANES, columns - 2 * LANES), BF16),
            pltpu.VMEM((columns - LANES, columns - 2 * LANES), BF16),
        ],
        in_specs=[group_spec(flat_rows, group) for group in range(groups)] + [vmem()],
        cost=4,
    )
    passed = jnp.concatenate([from_a[half + 48 :], from_b[half + 48 :], lists], axis=0)

    def swapped(value, sent):
        return [value] + [lax.ppermute(sent, "mem", turn) for turn in turns]

    passed, sent = lax.optimization_barrier((passed, middle))
    middles = swapped(middle, sent)
    passed = [lax.ppermute(passed, "mem", turn) for turn in turns]
    first, after, last = call(
        edge_kernel,
        [
            jax.ShapeDtypeStruct((levels, members, LANES), BF16),
            jax.ShapeDtypeStruct((levels, members, LANES), BF16),
            jax.ShapeDtypeStruct((levels // 2, members, LANES), BF16),
        ],
        [from_a, from_b, small, edge_high, edge_low, part, second, kept],
        [pltpu.VMEM((2, flat_rows, 2 * LANES), BF16)],
        cost=2,
    )
    pieces = [middle, first, after, last]
    cell = obs_cell.reshape(16, LANES)
    level = obs_level.reshape(16, LANES)
    reading = jax.ShapeDtypeStruct((members, entries), BF16)
    table = pltpu.VMEM((48, LANES), BF16)
    to_neighbour = []
    for turn, received in enumerate((from_a, from_b)):
        inputs = [*pieces, received, *passed, cell, level]
        to_neighbour += call(
            functools.partial(
                neighbour_kernel, others=others, blocks=blocks, turn=turn
            ),
            [reading],
            [*inputs, *to_neighbour],
            [table],
            in_specs=[vmem()] * len(inputs) + [pl.BlockSpec(memory_space=pl.ANY)] * turn,
            cost=2,
        )
    to_a, to_b = to_neighbour
    to_b, sent = lax.optimization_barrier((to_b, first))
    firsts = swapped(first, sent)
    back_a = lax.ppermute(to_a, "tile", odd_pairs)
    back_b = lax.ppermute(to_b, "tile", even_pairs)
    vector = jax.ShapeDtypeStruct((8, entries), F32)
    own, weight, target = call(
        functools.partial(own_kernel, others=others, blocks=blocks, tiles=tiles),
        [reading, vector, vector],
        [
            *pieces,
            lists,
            *passed,
            cell,
            level,
            obs_value.reshape(-1, LANES),
            obs_rinv.reshape(-1, LANES),
        ],
        [table],
        cost=2,
    )
    unused = middles[1:]
    (readings,) = call(merge_kernel, [reading], [own, back_a], cost=2)
    (readings,) = call(
        merge_kernel,
        [reading],
        [readings, back_b, *unused],
        in_specs=[vmem()] * 2 + [pl.BlockSpec(memory_space=pl.ANY)] * len(unused),
        cost=0,
    )
    readings, sent, sent_last = lax.optimization_barrier((readings, after, last))
    readings = swapped(readings, readings)
    afters = swapped(after, sent)
    lasts = swapped(last, sent_last)
    unused = firsts[1:]
    ensemble = members * sharers
    total = blocks * sharers
    square = pltpu.VMEM((total, LANES, LANES), F32)
    (weights,) = call(
        functools.partial(weights_kernel, others=others),
        [jax.ShapeDtypeStruct((total, members, ensemble), BF16)],
        [*readings, weight, target, *unused],
        [
            pltpu.VMEM((ensemble, entries), BF16),
            pltpu.VMEM((ensemble, entries), BF16),
            pltpu.VMEM((total, LANES, ensemble), BF16),
            pltpu.VMEM((total, 2 * LANES, 2 * LANES), BF16),
            square,
            square,
            square,
        ],
        in_specs=[vmem()] * (sharers + 2) + [pl.BlockSpec(memory_space=pl.ANY)] * len(unused),
        cost=8,
    )
    rows = members * levels
    result = jax.ShapeDtypeStruct((members, levels, columns), BF16)
    pairs = (middle.shape[0] + first.shape[0]) // 2
    moved, mean = call(
        functools.partial(prepare_kernel, others=others),
        [
            jax.ShapeDtypeStruct((pairs, ensemble, 2 * LANES), BF16),
            jax.ShapeDtypeStruct((pairs, 8, 2 * LANES), F32),
        ],
        [*middles, *firsts],
        cost=2,
    )
    inputs = [*afters, moved, mean, weights]
    analysis, rest = call(
        functools.partial(update_kernel, others=others),
        [result, jax.ShapeDtypeStruct((rows, LANES), F32)],
        inputs,
        [
            pltpu.VMEM((groups - 1, rows, LANES), F32),
            pltpu.VMEM((groups - 1, members, levels, LANES), BF16),
            pltpu.SemaphoreType.DMA((groups - 1,)),
        ],
        out_specs=[hbm, vmem()],
        cost=2,
    )
    inputs = [*lasts, weights, rest, analysis]
    (analysis,) = call(
        functools.partial(finish_kernel, others=others),
        [result],
        inputs,
        [
            pltpu.VMEM((rows, LANES), F32),
            pltpu.VMEM((members, levels, LANES), BF16),
            pltpu.SemaphoreType.DMA,
        ],
        in_specs=[vmem()] * (len(inputs) - 1) + [hbm],
        out_specs=[hbm],
        aliases={len(inputs) - 1: 0},
        cost=1,
    )
    return analysis


def solution(mesh):
    in_specs = (
        P("mem", None, "tile"),
        P(None, "tile"),
        P(None, "tile"),
        P("tile"),
        P("tile"),
        P(),
        P(),
        P("mem", "tile", None),
        P("mem", "tile", None),
    )
    out_specs = P("mem", None, "tile")
    return jax.shard_map(shards, mesh=mesh, in_specs=in_specs, out_specs=out_specs, check_vma=False)
```

```python
import functools

import jax
import jax.numpy as jnp
from jax import lax
from jax.experimental import pallas as pl
from jax.experimental.pallas import tpu as pltpu
from jax.sharding import PartitionSpec as P

HALO = 32
NS_ITERS = 8
LANES = 128
F32 = jnp.float32
BF16 = jnp.bfloat16
VMEM_LIMIT = 48 * 1024 * 1024

NN = (((1,), (0,)), ((), ()))
NT = (((1,), (1,)), ((), ()))
TN = (((0,), (0,)), ((), ()))


def dot(a, b, dims=NN):
    return lax.dot_general(a, b, dims, preferred_element_type=F32)


def split2(x):
    high = x.astype(BF16)
    return high, (x - high.astype(F32)).astype(BF16)


def split3(x):
    high = x.astype(BF16)
    rest = x - high.astype(F32)
    middle = rest.astype(BF16)
    return high, middle, (rest - middle.astype(F32)).astype(BF16)


def iota(shape, dim):
    return lax.broadcasted_iota(jnp.int32, shape, dim)


def is_odd_tile():
    return lax.axis_index("tile") % 2 == 1


def message_rows(field_rows):
    names = ("coef_high", "coef_low", "offset", "list_high", "list_low")
    return {name: field_rows + 16 * place for place, name in enumerate(names)}


def pack_kernel(
    field_hbm,
    coef_hbm,
    nbr_hbm,
    index_hbm,
    weight_hbm,
    a_ref,
    b_ref,
    lists_ref,
    small_ref,
    left_ref,
    right_ref,
    coef_ref,
    nbr_ref,
    index_ref,
    weight_ref,
    sems,
    *,
    tiles,
):
    columns = coef_ref.shape[1]
    levels = 8
    half = left_ref.shape[0] // 2
    members = half // levels
    rows = message_rows(half)
    odd = is_odd_tile()
    total = columns * tiles
    copies = [
        pltpu.make_async_copy(source, target, sems.at[k])
        for k, (source, target) in enumerate(
            (
                (coef_hbm, coef_ref),
                (nbr_hbm, nbr_ref),
                (index_hbm, index_ref),
                (weight_hbm, weight_ref),
                (field_hbm.at[:, 0:LANES], left_ref),
                (field_hbm.at[:, columns - LANES : columns], right_ref),
            )
        )
    ]
    for copy in copies:
        copy.start()
    for copy in copies[:4]:
        copy.wait()

    place = lax.axis_index("tile") * columns + iota((6, columns), 1)
    offset = nbr_ref[...] - place
    offset = jnp.where(offset > HALO, offset - total, offset)
    offset = jnp.where(offset < -HALO, offset + total, offset).astype(F32)
    small_ref[...] = jnp.zeros_like(small_ref)
    small_ref[0:6, :] = coef_ref[...]
    small_ref[8:14, :] = offset
    coef_high, coef_low = split2(coef_ref[...])
    for name, value in (
        ("coef_high", coef_high.astype(F32)),
        ("coef_low", coef_low.astype(F32)),
        ("offset", offset),
    ):
        first = padded(value[:, :LANES], 10)
        last = padded(value[:, columns - LANES :], 10)
        start = rows[name]
        a_ref[start : start + 16, :] = jnp.where(odd, last, first).astype(BF16)
        b_ref[start : start + 16, :] = jnp.where(odd, first, last).astype(BF16)
    blocks = index_ref.shape[0]
    index = padded(index_ref[:, 0, :].astype(F32), 16 - blocks)
    high = jnp.floor(index * (1.0 / 64.0))
    for k, value in enumerate((high, index - 64.0 * high)):
        value = value.astype(BF16)
        start = rows["list_high"] + 16 * k
        a_ref[start : start + 16, :] = value
        b_ref[start : start + 16, :] = value
        lists_ref[16 * k : 16 * k + 16, :] = value
    lists_ref[32:48, :] = padded(weight_ref[:, 0, :].astype(F32), 16 - blocks).astype(BF16)

    for copy in copies[4:]:
        copy.wait()
    lane = iota((members, LANES), 1)
    for level in range(levels):
        top = pl.ds(level, members, stride=levels)
        low = pl.ds(level + half, members, stride=levels)
        spot = slice(level * members, (level + 1) * members)
        left = jnp.where(lane < 64, left_ref[top, :], pltpu.roll(left_ref[low, :], 64, axis=1))
        right = jnp.where(lane < 64, pltpu.roll(right_ref[top, :], 64, axis=1), right_ref[low, :])
        a_ref[spot, :] = jnp.where(odd, right, left).astype(BF16)
        b_ref[spot, :] = jnp.where(odd, left, right).astype(BF16)


def band(coefs, offsets):
    shape = (LANES + 2 * HALO, LANES)
    spot = iota(shape, 0)
    result = jnp.where(
        spot == iota(shape, 1) + HALO, 1.0 - jnp.sum(coefs, axis=0, keepdims=True), 0.0
    )
    target = iota(offsets.shape, 1) + HALO + offsets.astype(jnp.int32)
    for j in range(6):
        result = result + jnp.where(spot == target[j : j + 1, :], coefs[j : j + 1, :], 0.0)
    return result


def dot3(left, right):
    return dot(left[0], right[0]) + (dot(left[0], right[1]) + dot(left[1], right[0]))


def padded(value, count):
    return jnp.concatenate([value, jnp.zeros((count, value.shape[1]), value.dtype)], axis=0)


def operator_kernel(
    small_ref, both_ref, part_ref, second_ref, first_high, first_low, second_high, second_low
):
    columns = small_ref.shape[1]
    groups = columns // LANES
    coef = padded(small_ref[0:6, :], 2)
    reach = padded(small_ref[8:14, :], 2)
    moved_coef = pltpu.roll(coef, HALO, axis=1)
    moved_reach = pltpu.roll(reach, HALO, axis=1)

    def lanes(value, group):
        return value[:, group * LANES : (group + 1) * LANES]

    firsts = {
        g: split2(band(lanes(moved_coef, g), lanes(moved_reach, g))) for g in range(1, groups)
    }
    seconds = [split2(band(lanes(coef, g), lanes(reach, g))) for g in range(groups)]
    for ref in (first_high, first_low, second_high, second_low):
        ref[...] = jnp.zeros_like(ref)
    for g in range(1, groups):
        row, lane = g * LANES - 64, (g - 1) * LANES
        count = min(LANES + 2 * HALO, columns - row)
        first_high[row : row + count, lane : lane + LANES] = firsts[g][0][:count, :]
        first_low[row : row + count, lane : lane + LANES] = firsts[g][1][:count, :]
    for g in range(1, groups - 1):
        row, lane = (g - 1) * LANES, (g - 1) * LANES
        second_high[row : row + LANES + 2 * HALO, lane : lane + LANES] = seconds[g][0]
        second_low[row : row + LANES + 2 * HALO, lane : lane + LANES] = seconds[g][1]
    both_ref[...] = joined(
        split2(dot3((first_high[...], first_low[...]), (second_high[...], second_low[...])))
    )

    for k, g in enumerate((0, groups - 1)):
        second = [padded(value, 64) for value in seconds[g]]
        for j in range(2):
            second_ref[2 * k + j] = second[j]
        if k == 0:
            part = dot3([value[:128, :] for value in firsts[1]], [value[128:, :] for value in second])
            part_ref[k] = jnp.concatenate([jnp.zeros_like(part), part], axis=0)
        else:
            part_ref[k] = padded(dot3(firsts[g], [value[:128, :] for value in second]), 64)


def middle_kernel(*refs, groups):
    field_refs = refs[:groups]
    both_ref, middle_ref, kept_ref, edge_ref, fields = refs[groups:]
    early, members, _ = middle_ref.shape
    levels = field_refs[0].shape[0] // members
    lane = iota((members, LANES), 1)
    for level in range(levels):
        spot = slice(level * members, (level + 1) * members)
        own = [ref[pl.ds(level, members, stride=levels), :] for ref in field_refs]
        for group in range(groups):
            fields[spot, group * LANES : (group + 1) * LANES] = own[group].astype(BF16)
        turned = [pltpu.roll(own[g], 64, axis=1) for g in (0, 1, groups - 2, groups - 1)]
        zero = jnp.zeros_like(turned[0])
        edge_ref[0, spot, 0:LANES] = jnp.where(lane < 64, zero, turned[0]).astype(BF16)
        edge_ref[0, spot, LANES:] = jnp.where(lane < 64, turned[0], turned[1]).astype(BF16)
        edge_ref[1, spot, 0:LANES] = jnp.where(lane < 64, turned[2], turned[3]).astype(BF16)
        edge_ref[1, spot, LANES:] = jnp.where(lane < 64, turned[3], zero).astype(BF16)
    result = dot(fields[...], both_ref[...])
    half = result.shape[1] // 2
    result = result[:, :half] + result[:, half:]
    for k in range((groups - 2) * levels):
        level, lane = k % levels, (k // levels) * LANES
        value = result[level * members : (level + 1) * members, lane : lane + LANES].astype(BF16)
        if k < early:
            middle_ref[k] = value
        else:
            kept_ref[k - early] = value


def edge_kernel(
    a_ref, b_ref, small_ref, edge_ref, part_ref, second_ref, kept_ref, first_ref, next_ref, last_ref, fields
):
    levels, members, _ = next_ref.shape
    columns = small_ref.shape[1]
    half = members // 2
    rows = message_rows(levels * half)
    odd = is_odd_tile()

    def side(k, start, count):
        a = a_ref[start : start + count, :].astype(F32)
        b = b_ref[start : start + count, :].astype(F32)
        return jnp.where(odd, b, a) if k == 0 else jnp.where(odd, a, b)

    own_coef = padded(small_ref[0:6, :], 2)
    own_reach = padded(small_ref[8:14, :], 2)
    lane8 = iota((8, LANES), 1)
    lane = iota((half, LANES), 1)
    operators = []
    for k in range(2):
        near = side(k, rows["coef_high"], 16)[:8] + side(k, rows["coef_low"], 16)[:8]
        reach = side(k, rows["offset"], 16)[:8]
        if k == 0:
            own = (own_coef[:, :LANES], own_reach[:, :LANES])
            both = [
                jnp.where(
                    lane8 < HALO, pltpu.roll(x, HALO, axis=1), pltpu.roll(y, HALO, axis=1)
                )
                for x, y in zip((near, reach), own)
            ]
            first = split2(band(*both))
            second = [second_ref[j, :128, :] for j in range(2)]
            fresh = padded(dot3(first, second), 64)
        else:
            own = (own_coef[:, columns - LANES :], own_reach[:, columns - LANES :])
            both = [
                jnp.where(
                    lane8 < HALO, pltpu.roll(y, HALO, axis=1), pltpu.roll(x, HALO, axis=1)
                )
                for x, y in zip((near, reach), own)
            ]
            first = [value[:128, :] for value in split2(band(*both))]
            second = [second_ref[2 + j, 128:, :] for j in range(2)]
            fresh = dot3(first, second)
            fresh = jnp.concatenate([jnp.zeros_like(fresh), fresh], axis=0)
        operators.append(split2(part_ref[k] + fresh))
    for k in range(2):
        for level in range(levels):
            top = level * members
            halo = side(k, level * half, half)
            other = pltpu.roll(halo, 64, axis=1)
            pair = (halo, other) if k == 0 else (other, halo)
            for j in range(2):
                spot = slice(top + j * half, top + (j + 1) * half)
                if k == 0:
                    own = edge_ref[k, spot, 0:LANES].astype(F32)
                    fields[k, spot, 0:LANES] = jnp.where(lane < 64, pair[j], own).astype(BF16)
                    fields[k, spot, LANES:] = edge_ref[k, spot, LANES:]
                else:
                    own = edge_ref[k, spot, LANES:].astype(F32)
                    fields[k, spot, LANES:] = jnp.where(lane < 64, own, pair[j]).astype(BF16)
                    fields[k, spot, 0:LANES] = edge_ref[k, spot, 0:LANES]
        result = dot(fields[k], joined(operators[k]))
        result = result[:, :LANES] + result[:, LANES:]
        part = levels // 2
        kept = kept_ref.shape[0]
        if k == 0:
            first_ref[:kept] = kept_ref[...]
        for level in range(levels):
            value = result[level * members : (level + 1) * members, :].astype(BF16)
            if k == 0 and level < part:
                first_ref[kept + level] = value
            elif k == 0:
                next_ref[level - part] = value
            elif level < part:
                next_ref[part + level] = value
            else:
                last_ref[level - part] = value


def gather_lists(parts, blocks):
    count = len(parts)
    me = lax.axis_index("mem")
    rows = [
        jnp.concatenate([part[b : b + 1, :].astype(F32) for b in range(blocks)], axis=1)
        for part in parts
    ]
    placed = []
    for place in range(count):
        value = rows[0]
        for shift in range(1, count):
            value = jnp.where((me + shift) % count == place, rows[shift], value)
        placed.append(value)
    return jnp.concatenate(placed, axis=1)


def read_places(table_ref, slot):
    wide = slot.shape[1]
    valid = (slot >= 0) & (slot < 16 * LANES)
    slot = jnp.where(valid, slot, 0)
    one = jnp.where(iota((LANES, wide), 0) == slot % LANES, 1.0, 0.0).astype(BF16)
    found = dot(table_ref[...], one)
    pick = iota((16, wide), 0) == slot // LANES
    values = [
        jnp.sum(jnp.where(pick, found[16 * k : 16 * k + 16, :], 0.0), axis=0, keepdims=True)
        for k in range(3)
    ]
    column = (values[1] * 16.0 + values[2]).astype(jnp.int32)
    return values[0].astype(jnp.int32), jnp.where(valid, column, -1)


def make_table(cell_ref, level_ref, table):
    cell = cell_ref[...]
    table[0:16, :] = level_ref[...].astype(F32).astype(BF16)
    table[16:32, :] = (cell // 16).astype(F32).astype(BF16)
    table[32:48, :] = (cell % 16).astype(F32).astype(BF16)


def read_forecast(field, level, column, out_ref, lane):
    members = out_ref.shape[0]
    wide = level.shape[1]
    one = jnp.where(iota((field.shape[1], wide), 0) == column, 1.0, 0.0).astype(BF16)
    found = dot(field, one)
    total = jnp.zeros((members, wide), F32)
    for l in range(field.shape[0] // members):
        total = total + jnp.where(level == l, found[l * members : (l + 1) * members, :], 0.0)
    out_ref[:, lane : lane + wide] = total.astype(BF16)


def whole(middle_ref, first_ref, next_ref, last_ref):
    part, members, _ = last_ref.shape
    kept = first_ref.shape[0] - part
    middle = jnp.concatenate([middle_ref[...], first_ref[:kept]], axis=0)
    groups = [
        jnp.concatenate([first_ref[kept:], next_ref[:part]], axis=0),
        *(middle[k : k + 2 * part] for k in range(0, middle.shape[0], 2 * part)),
        jnp.concatenate([next_ref[part:], last_ref[...]], axis=0),
    ]
    return joined([group.reshape(-1, LANES) for group in groups])


def neighbour_kernel(*refs, others, blocks, turn):
    message_ref = refs[4]
    other_refs = refs[5 : 5 + others]
    cell_ref, level_ref = refs[5 + others : 7 + others]
    out_ref, table = refs[-2:]
    half = message_ref.shape[0] - 80
    rows = message_rows(half)
    odd = is_odd_tile()
    obs = 16 * LANES
    make_table(cell_ref, level_ref, table)
    field = whole(*refs[:4])
    base = 32 * turn
    parts = [message_ref[rows["list_high"] : rows["list_high"] + 32, :]]
    parts += [r[base : base + 32, :] for r in other_refs]
    high = gather_lists([part[:16, :] for part in parts], blocks)
    low = gather_lists([part[16:, :] for part in parts], blocks)
    index = (high * 64.0 + low).astype(jnp.int32)
    skip = jnp.where(odd, 0, 2 * obs) if turn == 0 else jnp.where(odd, 2 * obs, 0)
    level, column = read_places(table, index - skip)
    for lane in range(0, index.shape[1], 256):
        read_forecast(
            field, level[:, lane : lane + 256], column[:, lane : lane + 256], out_ref, lane
        )


def own_kernel(*refs, others, blocks, tiles):
    lists_ref = refs[4]
    other_refs = refs[5 : 5 + others]
    (
        cell_ref,
        level_ref,
        value_ref,
        rinv_ref,
        r_ref,
        weight_ref,
        target_ref,
        table,
    ) = refs[5 + others :]
    obs = 16 * LANES
    make_table(cell_ref, level_ref, table)
    field = whole(*refs[:4])

    parts = [lists_ref[...]] + [r[64:112, :] for r in other_refs]
    passed = [gather_lists([part[16 * k : 16 * k + 16, :] for part in parts], blocks) for k in range(3)]
    index = (passed[0] * 64.0 + passed[1]).astype(jnp.int32)
    weight = passed[2]
    wide = index.shape[1]
    level, column = read_places(table, index - obs)
    for lane in range(0, wide, 256):
        read_forecast(field, level[:, lane : lane + 256], column[:, lane : lane + 256], r_ref, lane)

    tile = lax.axis_index("tile")
    starts = [((tile + tiles + shift) % tiles) * 16 for shift in (-1, 0, 1)]
    one = jnp.where(iota((LANES, wide), 0) == index % LANES, 1.0, 0.0).astype(BF16)
    pick = iota((48, wide), 0) == index // LANES

    def looked_up(ref):
        window = jnp.concatenate([ref[pl.ds(pl.multiple_of(s, 16), 16), :] for s in starts], axis=0)
        high, middle, low = [dot(piece, one) for piece in split3(window)]
        return jnp.sum(jnp.where(pick, (high + middle) + low, 0.0), axis=0, keepdims=True)

    weight_ref[...] = jnp.broadcast_to(looked_up(rinv_ref) * (weight / 3.0), weight_ref.shape)
    target_ref[...] = jnp.broadcast_to(looked_up(value_ref), target_ref.shape)


def merge_kernel(one_ref, other_ref, *refs):
    out_ref = refs[-1]
    out_ref[...] = (one_ref[...].astype(F32) + other_ref[...].astype(F32)).astype(BF16)


def doubled(high, low):
    top = jnp.concatenate([high, low], axis=1)
    bottom = jnp.concatenate([high, jnp.zeros_like(low)], axis=1)
    return jnp.concatenate([top, bottom], axis=0)


def product(left, right):
    both = dot(left, right)
    wide = both.shape[1] // 2
    return both[:, :wide] + both[:, wide:]


def joined(pair):
    return jnp.concatenate(pair, axis=1)


def weights_kernel(*refs, others):
    r_refs = refs[: others + 1]
    weight_ref, target_ref = refs[others + 1 : others + 3]
    out_ref, pert, weighted, turned, gram_right, hat, inner, outer = refs[-8:]
    members, wide = r_refs[0].shape
    blocks = wide // LANES
    ensemble = members * (others + 1)
    free = ensemble - 1.0

    parts = [ref[...].astype(F32) for ref in r_refs]
    total = sum(jnp.sum(part, axis=0, keepdims=True) for part in parts)
    mean = total * (1.0 / ensemble)
    weight = weight_ref[0:1, :]
    for k, part in enumerate(parts):
        rounded = (part - mean).astype(BF16)
        pert[k * members : (k + 1) * members, :] = rounded
        weighted[k * members : (k + 1) * members, :] = (rounded.astype(F32) * weight).astype(BF16)
    departure = target_ref[0:1, :] - mean

    eye = iota((LANES, LANES), 0) == iota((LANES, LANES), 1)

    def spread(value):
        return jnp.where(eye, value, 0.0)

    scales, xs, zs, grams, lefts, inners = [], [], [], [], [], []
    for b in range(blocks):
        lanes = slice(b * LANES, (b + 1) * LANES)
        turned[b] = weighted[:, lanes].T
    for b in range(blocks):
        lanes = slice(b * LANES, (b + 1) * LANES)
        grams.append(dot(turned[b], pert[:, lanes]))
    for b in range(blocks):
        trace = jnp.sum(jnp.sum(spread(grams[b]), axis=0, keepdims=True), axis=1, keepdims=True)
        scales.append(jnp.broadcast_to(1.0 / (free + trace), (1, LANES)))
    for b in range(blocks):
        gram = grams[b] * scales[b]
        x = free * scales[b]
        gram_right[b] = doubled(*split2(gram))
        m = 1.5 - 0.5 * x
        factor = spread(m) - 0.5 * gram
        v = m * x
        inners.append(
            product(joined(split2(factor)), doubled(*split2(factor - spread(0.5 * x))))
            - spread(0.5 * v)
        )
        xs.append(m * v)
        zs.append(m)
    for b in range(blocks):
        inner[b] = inners[b]
        hat[b] = spread(xs[b]) + product(joined(split2(inners[b])), gram_right[b])

    for turn in range(1, NS_ITERS - 1):
        lefts, halves = [], []
        for b in range(blocks):
            x, z = xs[b], zs[b]
            factor = spread(jnp.full((1, LANES), 1.5, F32)) - 0.5 * hat[b]
            f_high, f_low = split2(factor)
            lefts.append(joined((f_high, f_low)))
            inside = inner[b]
            if turn == 1:
                halves.append(product(lefts[b], doubled(*split2(inside))) - (0.5 * x) * inside)
                outer[b] = -0.5 * factor - (0.5 * z) * inside
                continue
            i_high, i_low = split2(inside)
            o_high, o_low = split2(outer[b])
            right_high = joined((i_high, o_high))
            both = dot(lefts[b], jnp.concatenate([right_high, right_high], axis=0)) + dot(
                f_high, joined((i_low, o_low))
            )
            halves.append(both[:, :LANES] - (0.5 * x) * inside)
            outer[b] = both[:, LANES:] - (0.5 * z) * inside
        for b in range(blocks):
            m = 1.5 - 0.5 * xs[b]
            inner[b] = product(lefts[b], doubled(*split2(halves[b]))) - (0.5 * m * xs[b]) * inner[b]
        for b in range(blocks):
            m = 1.5 - 0.5 * xs[b]
            xs[b] = m * m * xs[b]
            zs[b] = m * zs[b]
            hat[b] = spread(xs[b]) + product(joined(split2(inner[b])), gram_right[b])

    own = iota((members, ensemble), 0) == iota((members, ensemble), 1)
    lasts, rights, rows, cores = [], [], [], []
    for b in range(blocks):
        x, z = xs[b], zs[b]
        factor = spread(jnp.full((1, LANES), 1.5, F32)) - 0.5 * hat[b]
        last = product(joined(split2(factor)), doubled(*split2(outer[b]))) - (0.5 * z) * inner[b]
        zs[b] = (1.5 - 0.5 * x) * z
        lasts.append(split2(last))
    for b in range(blocks):
        rights.append(doubled(*lasts[b]))
        rows.append(jnp.broadcast_to(departure[:, b * LANES : (b + 1) * LANES], (8, LANES)))
    for _ in range(2):
        moved = [product(joined(split2(rows[b])), rights[b]) for b in range(blocks)]
        moved = [product(joined(split2(moved[b])), gram_right[b]) for b in range(blocks)]
        rows = [zs[b] * rows[b] + moved[b] for b in range(blocks)]
    for b in range(blocks):
        mine = pert[:members, b * LANES : (b + 1) * LANES]
        cores.append(dot(joined((mine, mine)), jnp.concatenate(lasts[b], axis=0)))
    for b in range(blocks):
        root = jnp.sqrt(free * scales[b])
        core = cores[b] * (root * scales[b])
        row = rows[b] * scales[b]
        all_rows = joined(split2(jnp.concatenate([core, row, row], axis=0)))
        found = dot(all_rows, jnp.concatenate([turned[b], turned[b]], axis=0))
        diagonal = jnp.where(own, (root * zs[b])[:, 0:1], 0.0)
        out_ref[b] = (found[:members, :] + found[members : members + 1, :] + diagonal).astype(BF16)


def departures(pairs):
    count = len(pairs[0])
    ensemble = pairs[0][0].shape[0] * count
    parts = [joined([pair[k].astype(F32) for pair in pairs]) for k in range(count)]
    total = sum(jnp.sum(part, axis=0, keepdims=True) for part in parts)
    mean = total * (1.0 / ensemble)
    return jnp.concatenate([(part - mean).astype(BF16) for part in parts], axis=0), mean


def updated(left, moved, mean, width):
    members = left.shape[0] * width // LANES
    found = dot(left, moved)
    result = found[:members, :]
    lane = iota(result.shape, 1) % LANES
    for k in range(1, LANES // width):
        result = jnp.where(lane < k * width, result, found[k * members : (k + 1) * members, :])
    result = result + mean
    return [result[:, k : k + LANES] for k in range(0, result.shape[1], LANES)]


def weights_of(weight_ref, group, columns):
    per = weight_ref.shape[0] * LANES // columns
    return jnp.concatenate([weight_ref[group * per + k] for k in range(per)], axis=0)


def prepare_kernel(*refs, others):
    count = others + 1
    middles, firsts = [refs[k * count : (k + 1) * count] for k in range(2)]
    moved_ref, mean_ref = refs[2 * count :]
    slot = 0
    for piece in (middles, firsts):
        for k in range(0, piece[0].shape[0], 2):
            moved, mean = departures([[ref[k + j] for ref in piece] for j in range(2)])
            moved_ref[slot] = moved
            mean_ref[slot] = jnp.broadcast_to(mean, mean_ref.shape[1:])
            slot += 1


def update_kernel(*refs, others):
    afters = refs[: others + 1]
    moved_ref, mean_ref, weight_ref, out_hbm, rest_ref, stage, done, sems = refs[others + 1 :]
    members, levels, columns = out_hbm.shape
    width = columns // weight_ref.shape[0]
    part = levels // 2
    groups = columns // LANES

    def rows(level):
        return pl.ds(level, members, stride=levels)

    copies = []
    slot = 0
    for group in (*range(1, groups - 1), 0):
        left = weights_of(weight_ref, group, columns)
        for level in range(0, levels, 2):
            if group or level < part:
                moved, mean = moved_ref[slot], mean_ref[slot, 0:1, :]
                slot += 1
            else:
                moved, mean = departures([[ref[level - part + j] for ref in afters] for j in range(2)])
            for j, value in enumerate(updated(left, moved, mean, width)):
                stage[group, rows(level + j), :] = value
        done[group] = stage[group].reshape(members, levels, LANES).astype(BF16)
        lanes = slice(group * LANES, (group + 1) * LANES)
        copies.append(pltpu.make_async_copy(done.at[group], out_hbm.at[:, :, lanes], sems.at[group]))
        copies[-1].start()
    left = weights_of(weight_ref, groups - 1, columns)
    for level in range(0, part, 2):
        moved, mean = departures([[ref[part + level + j] for ref in afters] for j in range(2)])
        for j, value in enumerate(updated(left, moved, mean, width)):
            rest_ref[rows(level + j), :] = value
    for level in range(part, levels):
        rest_ref[rows(level), :] = jnp.zeros((members, LANES), F32)
    for copy in copies:
        copy.wait()


def finish_kernel(*refs, others):
    lasts = refs[: others + 1]
    weight_ref, rest_ref, _, out_hbm, stage, done, sem = refs[others + 1 :]
    members, levels, columns = out_hbm.shape
    width = columns // weight_ref.shape[0]
    part = levels // 2
    left = weights_of(weight_ref, columns // LANES - 1, columns)
    stage[...] = rest_ref[...]
    for level in range(0, part, 2):
        moved, mean = departures([[ref[level + j] for ref in lasts] for j in range(2)])
        for j, value in enumerate(updated(left, moved, mean, width)):
            stage[pl.ds(part + level + j, members, stride=levels), :] = value
    done[...] = stage[...].reshape(members, levels, LANES).astype(BF16)
    copy = pltpu.make_async_copy(done, out_hbm.at[:, :, columns - LANES : columns], sem)
    copy.start()
    copy.wait()


def vmem():
    return pl.BlockSpec(memory_space=pltpu.VMEM)


def group_spec(rows, group):
    return pl.BlockSpec((rows, LANES), lambda i: (0, group))


def call(kernel, outs, inputs, scratch=(), in_specs=None, out_specs=None, aliases=None, cost=0, limit=VMEM_LIMIT):
    return pl.pallas_call(
        kernel,
        grid=(1,),
        out_shape=outs,
        in_specs=in_specs or [vmem()] * len(inputs),
        out_specs=out_specs or [vmem()] * len(outs),
        scratch_shapes=list(scratch),
        input_output_aliases=aliases or {},
        compiler_params=pltpu.CompilerParams(vmem_limit_bytes=limit),
        cost_estimate=pl.CostEstimate(flops=cost << 30, bytes_accessed=1 << 10, transcendentals=0),
    )(*inputs)


def shards(
    fields,
    coefficients,
    neighbours,
    obs_cell,
    obs_level,
    obs_value,
    obs_rinv,
    obs_index,
    obs_weight,
):
    tiles = lax.axis_size("tile")
    sharers = lax.axis_size("mem")
    others = sharers - 1
    members, levels, columns = fields.shape
    blocks = obs_index.shape[0]
    entries = blocks * sharers * LANES
    half = members * levels // 2
    message = jax.ShapeDtypeStruct((half + 80, LANES), BF16)
    even_pairs = []
    odd_pairs = []
    for i in range(0, tiles, 2):
        even_pairs += [(i, i + 1), (i + 1, i)]
        low, high = i + 1, (i + 2) % tiles
        odd_pairs += [(low, high), (high, low)]
    turns = [[((i + r) % sharers, i) for i in range(sharers)] for r in range(1, sharers)]

    flat = fields.reshape(members * levels, columns)
    groups = columns // LANES
    hbm = pl.BlockSpec(memory_space=pltpu.HBM)
    a, b, lists, small = call(
        functools.partial(pack_kernel, tiles=tiles),
        [
            message,
            message,
            jax.ShapeDtypeStruct((48, LANES), BF16),
            jax.ShapeDtypeStruct((16, columns), F32),
        ],
        [flat, coefficients, neighbours, obs_index, obs_weight],
        [
            pltpu.VMEM((members * levels, LANES), F32),
            pltpu.VMEM((members * levels, LANES), F32),
            pltpu.VMEM((6, columns), F32),
            pltpu.VMEM((6, columns), jnp.int32),
            pltpu.VMEM(obs_index.shape, jnp.int32),
            pltpu.VMEM(obs_index.shape, jnp.int32),
            pltpu.SemaphoreType.DMA((6,)),
        ],
        in_specs=[hbm] * 5,
        limit=64 * 1024 * 1024,
    )
    from_b = lax.ppermute(b, "tile", even_pairs)
    from_a = lax.ppermute(a, "tile", odd_pairs)
    flat_rows = members * levels
    kept_levels = levels // 4
    both, part, second = call(
        operator_kernel,
        [
            jax.ShapeDtypeStruct((columns, 2 * (columns - 2 * LANES)), BF16),
            jax.ShapeDtypeStruct((2, 2 * LANES, LANES), F32),
            jax.ShapeDtypeStruct((4, 2 * LANES, LANES), BF16),
        ],
        [small],
        [
            pltpu.VMEM((columns, columns - LANES), BF16),
            pltpu.VMEM((columns, columns - LANES), BF16),
            pltpu.VMEM((columns - LANES, columns - 2 * LANES), BF16),
            pltpu.VMEM((columns - LANES, columns - 2 * LANES), BF16),
        ],
        cost=2,
    )
    middle, kept, border = call(
        functools.partial(middle_kernel, groups=groups),
        [
            jax.ShapeDtypeStruct(((groups - 2) * levels - kept_levels, members, LANES), BF16),
            jax.ShapeDtypeStruct((kept_levels, members, LANES), BF16),
            jax.ShapeDtypeStruct((2, flat_rows, 2 * LANES), BF16),
        ],
        [flat] * groups + [both],
        [pltpu.VMEM((flat_rows, columns), BF16)],
        in_specs=[group_spec(flat_rows, group) for group in range(groups)] + [vmem()],
        cost=3,
    )
    passed = jnp.concatenate([from_a[half + 48 :], from_b[half + 48 :], lists], axis=0)

    def swapped(value, sent):
        return [value] + [lax.ppermute(sent, "mem", turn) for turn in turns]

    passed, sent = lax.optimization_barrier((passed, middle))
    middles = swapped(middle, sent)
    passed = [lax.ppermute(passed, "mem", turn) for turn in turns]
    first, after, last = call(
        edge_kernel,
        [
            jax.ShapeDtypeStruct((kept_levels + levels // 2, members, LANES), BF16),
            jax.ShapeDtypeStruct((levels, members, LANES), BF16),
            jax.ShapeDtypeStruct((levels // 2, members, LANES), BF16),
        ],
        [from_a, from_b, small, border, part, second, kept],
        [pltpu.VMEM((2, flat_rows, 2 * LANES), BF16)],
        cost=2,
    )
    pieces = [middle, first, after, last]
    cell = obs_cell.reshape(16, LANES)
    level = obs_level.reshape(16, LANES)
    reading = jax.ShapeDtypeStruct((members, entries), BF16)
    table = pltpu.VMEM((48, LANES), BF16)
    to_neighbour = []
    for turn, received in enumerate((from_a, from_b)):
        inputs = [*pieces, received, *passed, cell, level]
        to_neighbour += call(
            functools.partial(
                neighbour_kernel, others=others, blocks=blocks, turn=turn
            ),
            [reading],
            [*inputs, *to_neighbour],
            [table],
            in_specs=[vmem()] * len(inputs) + [pl.BlockSpec(memory_space=pl.ANY)] * turn,
            cost=2,
        )
    to_a, to_b = to_neighbour
    to_b, sent = lax.optimization_barrier((to_b, first))
    firsts = swapped(first, sent)
    back_a = lax.ppermute(to_a, "tile", odd_pairs)
    back_b = lax.ppermute(to_b, "tile", even_pairs)
    vector = jax.ShapeDtypeStruct((8, entries), F32)
    own, weight, target = call(
        functools.partial(own_kernel, others=others, blocks=blocks, tiles=tiles),
        [reading, vector, vector],
        [
            *pieces,
            lists,
            *passed,
            cell,
            level,
            obs_value.reshape(-1, LANES),
            obs_rinv.reshape(-1, LANES),
        ],
        [table],
        cost=2,
    )
    unused = middles[1:]
    (readings,) = call(merge_kernel, [reading], [own, back_a], cost=2)
    (readings,) = call(
        merge_kernel,
        [reading],
        [readings, back_b, *unused],
        in_specs=[vmem()] * 2 + [pl.BlockSpec(memory_space=pl.ANY)] * len(unused),
        cost=0,
    )
    readings, sent, sent_last = lax.optimization_barrier((readings, after, last))
    readings = swapped(readings, readings)
    afters = swapped(after, sent)
    lasts = swapped(last, sent_last)
    unused = firsts[1:]
    ensemble = members * sharers
    total = blocks * sharers
    square = pltpu.VMEM((total, LANES, LANES), F32)
    (weights,) = call(
        functools.partial(weights_kernel, others=others),
        [jax.ShapeDtypeStruct((total, members, ensemble), BF16)],
        [*readings, weight, target, *unused],
        [
            pltpu.VMEM((ensemble, entries), BF16),
            pltpu.VMEM((ensemble, entries), BF16),
            pltpu.VMEM((total, LANES, ensemble), BF16),
            pltpu.VMEM((total, 2 * LANES, 2 * LANES), BF16),
            square,
            square,
            square,
        ],
        in_specs=[vmem()] * (sharers + 2) + [pl.BlockSpec(memory_space=pl.ANY)] * len(unused),
        cost=8,
    )
    rows = members * levels
    result = jax.ShapeDtypeStruct((members, levels, columns), BF16)
    pairs = (middle.shape[0] + first.shape[0]) // 2
    moved, mean = call(
        functools.partial(prepare_kernel, others=others),
        [
            jax.ShapeDtypeStruct((pairs, ensemble, 2 * LANES), BF16),
            jax.ShapeDtypeStruct((pairs, 8, 2 * LANES), F32),
        ],
        [*middles, *firsts],
        cost=2,
    )
    inputs = [*afters, moved, mean, weights]
    analysis, rest = call(
        functools.partial(update_kernel, others=others),
        [result, jax.ShapeDtypeStruct((rows, LANES), F32)],
        inputs,
        [
            pltpu.VMEM((groups - 1, rows, LANES), F32),
            pltpu.VMEM((groups - 1, members, levels, LANES), BF16),
            pltpu.SemaphoreType.DMA((groups - 1,)),
        ],
        out_specs=[hbm, vmem()],
        cost=2,
    )
    inputs = [*lasts, weights, rest, analysis]
    (analysis,) = call(
        functools.partial(finish_kernel, others=others),
        [result],
        inputs,
        [
            pltpu.VMEM((rows, LANES), F32),
            pltpu.VMEM((members, levels, LANES), BF16),
            pltpu.SemaphoreType.DMA,
        ],
        in_specs=[vmem()] * (len(inputs) - 1) + [hbm],
        out_specs=[hbm],
        aliases={len(inputs) - 1: 0},
        cost=1,
    )
    return analysis


def solution(mesh):
    in_specs = (
        P("mem", None, "tile"),
        P(None, "tile"),
        P(None, "tile"),
        P("tile"),
        P("tile"),
        P(),
        P(),
        P("mem", "tile", None),
        P("mem", "tile", None),
    )
    out_specs = P("mem", None, "tile")
    return jax.shard_map(shards, mesh=mesh, in_specs=in_specs, out_specs=out_specs, check_vma=False)
```

```python
import functools

import jax
import jax.numpy as jnp
from jax import lax
from jax.experimental import pallas as pl
from jax.experimental.pallas import tpu as pltpu
from jax.sharding import PartitionSpec as P

HALO = 32
NS_ITERS = 8
LANES = 128
F32 = jnp.float32
BF16 = jnp.bfloat16
VMEM_LIMIT = 48 * 1024 * 1024

NN = (((1,), (0,)), ((), ()))
NT = (((1,), (1,)), ((), ()))
TN = (((0,), (0,)), ((), ()))


def dot(a, b, dims=NN):
    return lax.dot_general(a, b, dims, preferred_element_type=F32)


def split2(x):
    high = x.astype(BF16)
    return high, (x - high.astype(F32)).astype(BF16)


def split3(x):
    high = x.astype(BF16)
    rest = x - high.astype(F32)
    middle = rest.astype(BF16)
    return high, middle, (rest - middle.astype(F32)).astype(BF16)


def iota(shape, dim):
    return lax.broadcasted_iota(jnp.int32, shape, dim)


def is_odd_tile():
    return lax.axis_index("tile") % 2 == 1


def message_rows(field_rows):
    return {name: field_rows + 16 * place for place, name in enumerate(("coef", "offset", "list"))}


MESSAGE_EXTRA = 48


def pack_kernel(
    field_hbm,
    coef_hbm,
    nbr_hbm,
    index_hbm,
    weight_hbm,
    a_ref,
    b_ref,
    lists_ref,
    small_ref,
    left_ref,
    right_ref,
    coef_ref,
    nbr_ref,
    index_ref,
    weight_ref,
    sems,
    *,
    tiles,
):
    columns = coef_ref.shape[1]
    levels = 8
    half = left_ref.shape[0] // 2
    members = half // levels
    rows = message_rows(half)
    odd = is_odd_tile()
    total = columns * tiles
    copies = [
        pltpu.make_async_copy(source, target, sems.at[k])
        for k, (source, target) in enumerate(
            (
                (coef_hbm, coef_ref),
                (nbr_hbm, nbr_ref),
                (index_hbm, index_ref),
                (weight_hbm, weight_ref),
                (field_hbm.at[:, 0:LANES], left_ref),
                (field_hbm.at[:, columns - LANES : columns], right_ref),
            )
        )
    ]
    for copy in copies:
        copy.start()
    for copy in copies[:4]:
        copy.wait()

    place = lax.axis_index("tile") * columns + iota((6, columns), 1)
    offset = nbr_ref[...] - place
    offset = jnp.where(offset > HALO, offset - total, offset)
    offset = jnp.where(offset < -HALO, offset + total, offset).astype(F32)
    small_ref[...] = jnp.zeros_like(small_ref)
    small_ref[0:6, :] = coef_ref[...]
    small_ref[8:14, :] = offset
    pieces = [padded(value.astype(F32), 2) for value in split2(coef_ref[...])]
    reach = padded(offset, 10)
    for name, value in (("coef", jnp.concatenate(pieces, axis=0)), ("offset", reach)):
        first = value[:, :LANES]
        last = value[:, columns - LANES :]
        start = rows[name]
        a_ref[start : start + 16, :] = jnp.where(odd, last, first).astype(BF16)
        b_ref[start : start + 16, :] = jnp.where(odd, first, last).astype(BF16)
    blocks = index_ref.shape[0]
    index = index_ref[:, 0, :]
    quotient = padded(((index // LANES) * 4 + weight_ref[:, 0, :]).astype(F32), 8 - blocks)
    entries = padded((index % LANES).astype(F32), 8 - blocks)
    entries = jnp.concatenate([quotient, entries], axis=0).astype(BF16)
    start = rows["list"]
    a_ref[start : start + 16, :] = entries
    b_ref[start : start + 16, :] = entries
    lists_ref[...] = entries

    for copy in copies[4:]:
        copy.wait()
    lane = iota((members, LANES), 1)
    for level in range(levels):
        top = pl.ds(level, members, stride=levels)
        low = pl.ds(level + half, members, stride=levels)
        spot = slice(level * members, (level + 1) * members)
        left = jnp.where(lane < 64, left_ref[top, :], pltpu.roll(left_ref[low, :], 64, axis=1))
        right = jnp.where(lane < 64, pltpu.roll(right_ref[top, :], 64, axis=1), right_ref[low, :])
        a_ref[spot, :] = jnp.where(odd, right, left).astype(BF16)
        b_ref[spot, :] = jnp.where(odd, left, right).astype(BF16)


def band(coefs, offsets):
    shape = (LANES + 2 * HALO, LANES)
    spot = iota(shape, 0)
    result = jnp.where(
        spot == iota(shape, 1) + HALO, 1.0 - jnp.sum(coefs, axis=0, keepdims=True), 0.0
    )
    target = iota(offsets.shape, 1) + HALO + offsets.astype(jnp.int32)
    for j in range(6):
        result = result + jnp.where(spot == target[j : j + 1, :], coefs[j : j + 1, :], 0.0)
    return result


def dot3(left, right):
    return dot(left[0], right[0]) + (dot(left[0], right[1]) + dot(left[1], right[0]))


def padded(value, count):
    if not count:
        return value
    return jnp.concatenate([value, jnp.zeros((count, value.shape[1]), value.dtype)], axis=0)


def operator_kernel(small_ref, both_ref, part_ref, second_ref):
    columns = small_ref.shape[1]
    groups = columns // LANES
    coef = padded(small_ref[0:6, :], 2)
    reach = padded(small_ref[8:14, :], 2)
    moved = pltpu.roll(coef, HALO, axis=1), pltpu.roll(reach, HALO, axis=1)

    def operator(values, group):
        lanes = slice(group * LANES, (group + 1) * LANES)
        return split2(band(*(value[:, lanes] for value in values)))

    firsts = {g: operator(moved, g) for g in range(1, groups)}
    seconds = [[padded(v, 64) for v in operator((coef, reach), g)] for g in range(groups)]

    def upper(g):
        return padded(dot3(firsts[g], [value[:LANES, :] for value in seconds[g]]), 64)

    def lower(g):
        result = dot3(
            [value[:LANES, :] for value in firsts[g + 1]],
            [value[LANES:, :] for value in seconds[g]],
        )
        return jnp.concatenate([jnp.zeros_like(result), result], axis=0)

    both_ref[...] = jnp.zeros_like(both_ref)
    half = both_ref.shape[1] // 2
    for g in range(1, groups - 1):
        row, lane = g * LANES - 64, (g - 1) * LANES
        for k, value in enumerate(split2(upper(g) + lower(g))):
            both_ref[row : row + 2 * LANES, k * half + lane : k * half + lane + LANES] = value
    part_ref[0] = lower(0)
    part_ref[1] = upper(groups - 1)
    for k, g in enumerate((0, groups - 1)):
        for j in range(2):
            second_ref[2 * k + j] = seconds[g][j]


def middle_kernel(*refs, groups):
    field_refs = refs[:groups]
    both_ref, middle_ref, kept_ref, edge_ref, edge_low_ref, fields, fields_low = refs[groups:]
    early, members, _ = middle_ref.shape
    levels = field_refs[0].shape[0] // members
    lane = iota((members, LANES), 1)
    for level in range(levels):
        spot = slice(level * members, (level + 1) * members)
        own = [ref[pl.ds(level, members, stride=levels), :] for ref in field_refs]
        for group in range(groups):
            lanes = slice(group * LANES, (group + 1) * LANES)
            fields[spot, lanes], fields_low[spot, lanes] = split2(own[group])
        pieces = [
            split2(pltpu.roll(own[g], 64, axis=1)) for g in (0, 1, groups - 2, groups - 1)
        ]
        for part, ref in enumerate((edge_ref, edge_low_ref)):
            turned = [piece[part].astype(F32) for piece in pieces]
            zero = jnp.zeros_like(turned[0])
            ref[0, spot, 0:LANES] = jnp.where(lane < 64, zero, turned[0]).astype(BF16)
            ref[0, spot, LANES:] = jnp.where(lane < 64, turned[0], turned[1]).astype(BF16)
            ref[1, spot, 0:LANES] = jnp.where(lane < 64, turned[2], turned[3]).astype(BF16)
            ref[1, spot, LANES:] = jnp.where(lane < 64, turned[3], zero).astype(BF16)
    result = dot(fields[...], both_ref[...])
    half = result.shape[1] // 2
    result = result[:, :half] + (result[:, half:] + dot(fields_low[...], both_ref[:, :half]))
    for k in range((groups - 2) * levels):
        level, lane = k % levels, (k // levels) * LANES
        value = result[level * members : (level + 1) * members, lane : lane + LANES].astype(BF16)
        if k < early:
            middle_ref[k] = value
        else:
            kept_ref[k - early] = value


def edge_kernel(
    a_ref, b_ref, small_ref, edge_ref, edge_low_ref, part_ref, second_ref, kept_ref, first_ref, next_ref, last_ref, fields
):
    _, members, _ = next_ref.shape
    levels = fields.shape[1] // members
    columns = small_ref.shape[1]
    half = members // 2
    rows = message_rows(levels * half)
    odd = is_odd_tile()

    def side(k, start, count):
        a = a_ref[start : start + count, :].astype(F32)
        b = b_ref[start : start + count, :].astype(F32)
        return jnp.where(odd, b, a) if k == 0 else jnp.where(odd, a, b)

    own_coef = padded(small_ref[0:6, :], 2)
    own_reach = padded(small_ref[8:14, :], 2)
    lane8 = iota((8, LANES), 1)
    lane = iota((half, LANES), 1)
    operators = []
    for k in range(2):
        near = side(k, rows["coef"], 16)
        near = near[:8] + near[8:]
        reach = side(k, rows["offset"], 16)[:8]
        if k == 0:
            own = (own_coef[:, :LANES], own_reach[:, :LANES])
            both = [
                jnp.where(
                    lane8 < HALO, pltpu.roll(x, HALO, axis=1), pltpu.roll(y, HALO, axis=1)
                )
                for x, y in zip((near, reach), own)
            ]
            first = split2(band(*both))
            second = [second_ref[j, :128, :] for j in range(2)]
            fresh = padded(dot3(first, second), 64)
        else:
            own = (own_coef[:, columns - LANES :], own_reach[:, columns - LANES :])
            both = [
                jnp.where(
                    lane8 < HALO, pltpu.roll(y, HALO, axis=1), pltpu.roll(x, HALO, axis=1)
                )
                for x, y in zip((near, reach), own)
            ]
            first = [value[:128, :] for value in split2(band(*both))]
            second = [second_ref[2 + j, 128:, :] for j in range(2)]
            fresh = dot3(first, second)
            fresh = jnp.concatenate([jnp.zeros_like(fresh), fresh], axis=0)
        operators.append(split2(part_ref[k] + fresh))
    for k in range(2):
        for level in range(levels):
            top = level * members
            halo = side(k, level * half, half)
            other = pltpu.roll(halo, 64, axis=1)
            pair = (halo, other) if k == 0 else (other, halo)
            for j in range(2):
                spot = slice(top + j * half, top + (j + 1) * half)
                if k == 0:
                    own = edge_ref[k, spot, 0:LANES].astype(F32)
                    fields[k, spot, 0:LANES] = jnp.where(lane < 64, pair[j], own).astype(BF16)
                    fields[k, spot, LANES:] = edge_ref[k, spot, LANES:]
                else:
                    own = edge_ref[k, spot, LANES:].astype(F32)
                    fields[k, spot, LANES:] = jnp.where(lane < 64, own, pair[j]).astype(BF16)
                    fields[k, spot, 0:LANES] = edge_ref[k, spot, 0:LANES]
        result = dot(fields[k], joined(operators[k]))
        result = result[:, :LANES] + (
            result[:, LANES:] + dot(edge_low_ref[k], operators[k][0])
        )
        kept = kept_ref.shape[0]
        if k == 0:
            first_ref[:kept] = kept_ref[...]
        places = [
            (ref, place)
            for ref, start in ((first_ref, kept), (next_ref, 0), (last_ref, 0))
            for place in range(start, ref.shape[0])
        ]
        for level in range(levels):
            ref, place = places[k * levels + level]
            ref[place] = result[level * members : (level + 1) * members, :].astype(BF16)


def in_order(parts):
    count = len(parts)
    me = lax.axis_index("mem")
    placed = []
    for place in range(count):
        value = parts[0]
        for shift in range(1, count):
            value = jnp.where((me + shift) % count == place, parts[shift], value)
        placed.append(value)
    return joined(placed)


def entries_of(part, blocks):
    part = part.astype(F32)
    quotient = joined([part[b : b + 1, :] for b in range(blocks)]).astype(jnp.int32)
    rest = joined([part[8 + b : 9 + b, :] for b in range(blocks)]).astype(jnp.int32)
    return (quotient // 4) * LANES + rest, quotient % 4


def read_places(table_ref, slot):
    wide = slot.shape[1]
    valid = (slot >= 0) & (slot < 16 * LANES)
    slot = jnp.where(valid, slot, 0)
    one = jnp.where(iota((LANES, wide), 0) == slot % LANES, 1.0, 0.0).astype(BF16)
    found = dot(table_ref[...], one)
    pick = iota((16, wide), 0) == slot // LANES
    values = [
        jnp.sum(jnp.where(pick, found[16 * k : 16 * k + 16, :], 0.0), axis=0, keepdims=True)
        for k in range(3)
    ]
    column = (values[1] * 16.0 + values[2]).astype(jnp.int32)
    return values[0].astype(jnp.int32), jnp.where(valid, column, -1)


def make_table(cell_ref, level_ref, table):
    cell = cell_ref[...]
    table[0:16, :] = level_ref[...].astype(F32).astype(BF16)
    table[16:32, :] = (cell // 16).astype(F32).astype(BF16)
    table[32:48, :] = (cell % 16).astype(F32).astype(BF16)


def read_some(field, levels, level, column):
    members = field.shape[0] // levels
    wide = level.shape[1]
    one = jnp.where(iota((field.shape[1], wide), 0) == column, 1.0, 0.0).astype(BF16)
    found = dot(field, one)
    total = jnp.zeros((members, wide), F32)
    for l in range(levels):
        total = total + jnp.where(level == l, found[l * members : (l + 1) * members, :], 0.0)
    return total


def read_forecast(field, levels, level, column):
    step = min(256, level.shape[1])
    return joined(
        [
            read_some(field, levels, level[:, k : k + step], column[:, k : k + step])
            for k in range(0, level.shape[1], step)
        ]
    )


def whole(middle_ref, first_ref, next_ref, last_ref, levels):
    runs = jnp.concatenate([ref[...] for ref in (middle_ref, first_ref, next_ref, last_ref)], axis=0)
    groups = [runs[k : k + levels].reshape(-1, LANES) for k in range(0, runs.shape[0], levels)]
    return joined([groups[-2], *groups[:-2], groups[-1]])


def neighbour_kernel(*refs, others, blocks, levels, turn, given):
    message_ref, cell_ref, level_ref = refs[4:7]
    passed_refs = refs[7 : 7 + others]
    out_ref, table = refs[-2:]
    half = message_ref.shape[0] - MESSAGE_EXTRA
    rows = message_rows(half)
    odd = is_odd_tile()
    obs = 16 * LANES
    make_table(cell_ref, level_ref, table)
    field = whole(*refs[:4], levels)
    skip = jnp.where(odd, 0, 2 * obs) if turn == 0 else jnp.where(odd, 2 * obs, 0)
    parts = [ref[16 * turn : 16 * turn + 16, :] for ref in passed_refs]
    if not given:
        parts = [message_ref[rows["list"] : rows["list"] + 16, :], *parts]
    index = joined([entries_of(part, blocks)[0] for part in parts])
    level, column = read_places(table, index - skip)
    found = read_forecast(field, levels, level, column)
    if others:
        mine = blocks * LANES
        found = [found[:, k : k + mine] for k in range(0, found.shape[1], mine)]
        if given:
            found = [refs[7 + others][...].astype(F32), *found]
        found = in_order(found)
    out_ref[...] = found.astype(BF16)


def own_kernel(*refs, others, blocks, levels, tiles):
    lists_ref = refs[4]
    other_refs = refs[5 : 5 + others]
    (
        cell_ref,
        level_ref,
        value_ref,
        rinv_ref,
        r_ref,
        weight_ref,
        target_ref,
        table,
    ) = refs[5 + others :]
    obs = 16 * LANES
    make_table(cell_ref, level_ref, table)
    field = whole(*refs[:4], levels)
    parts = [lists_ref[...]] + [r[32:48, :] for r in other_refs]
    parts = [entries_of(part, blocks) for part in parts]
    index = in_order([index for index, _ in parts])
    weight = in_order([weight for _, weight in parts]).astype(F32)
    wide = index.shape[1]
    level, column = read_places(table, index - obs)
    r_ref[...] = read_forecast(field, levels, level, column).astype(BF16)

    tile = lax.axis_index("tile")
    starts = [((tile + tiles + shift) % tiles) * 16 for shift in (-1, 0, 1)]
    one = jnp.where(iota((LANES, wide), 0) == index % LANES, 1.0, 0.0).astype(BF16)
    pick = iota((48, wide), 0) == index // LANES

    def looked_up(ref):
        window = jnp.concatenate([ref[pl.ds(pl.multiple_of(s, 16), 16), :] for s in starts], axis=0)
        high, middle, low = [dot(piece, one) for piece in split3(window)]
        return jnp.sum(jnp.where(pick, (high + middle) + low, 0.0), axis=0, keepdims=True)

    weight_ref[...] = jnp.broadcast_to(looked_up(rinv_ref) * (weight / 3.0), weight_ref.shape)
    target_ref[...] = jnp.broadcast_to(looked_up(value_ref), target_ref.shape)


def merge_kernel(one_ref, other_ref, *refs):
    out_ref = refs[-1]
    out_ref[...] = (one_ref[...].astype(F32) + other_ref[...].astype(F32)).astype(BF16)


def doubled(high, low):
    top = jnp.concatenate([high, low], axis=1)
    bottom = jnp.concatenate([high, jnp.zeros_like(low)], axis=1)
    return jnp.concatenate([top, bottom], axis=0)


def product(left, right):
    both = dot(left, right)
    wide = both.shape[1] // 2
    return both[:, :wide] + both[:, wide:]


def joined(pair):
    return jnp.concatenate(pair, axis=1)


def weights_kernel(*refs, others):
    r_refs = refs[: others + 1]
    weight_ref, target_ref = refs[others + 1 : others + 3]
    out_ref, pert, weighted, turned, gram_right, hat, inner, outer = refs[-8:]
    members, wide = r_refs[0].shape
    blocks = wide // LANES
    ensemble = members * (others + 1)
    free = ensemble - 1.0

    parts = [ref[...].astype(F32) for ref in r_refs]
    total = sum(jnp.sum(part, axis=0, keepdims=True) for part in parts)
    mean = total * (1.0 / ensemble)
    weight = weight_ref[0:1, :]
    for k, part in enumerate(parts):
        rounded = (part - mean).astype(BF16)
        pert[k * members : (k + 1) * members, :] = rounded
        weighted[k * members : (k + 1) * members, :] = (rounded.astype(F32) * weight).astype(BF16)
    departure = target_ref[0:1, :] - mean

    eye = iota((LANES, LANES), 0) == iota((LANES, LANES), 1)

    def spread(value):
        return jnp.where(eye, value, 0.0)

    scales, xs, zs, grams, lefts, inners = [], [], [], [], [], []
    for b in range(blocks):
        lanes = slice(b * LANES, (b + 1) * LANES)
        turned[b] = weighted[:, lanes].T
    for b in range(blocks):
        lanes = slice(b * LANES, (b + 1) * LANES)
        grams.append(dot(turned[b], pert[:, lanes]))
    for b in range(blocks):
        trace = jnp.sum(jnp.sum(spread(grams[b]), axis=0, keepdims=True), axis=1, keepdims=True)
        scales.append(jnp.broadcast_to(1.0 / (free + trace), (1, LANES)))
    for b in range(blocks):
        gram = grams[b] * scales[b]
        x = free * scales[b]
        gram_right[b] = doubled(*split2(gram))
        m = 1.5 - 0.5 * x
        factor = spread(m) - 0.5 * gram
        v = m * x
        inners.append(
            product(joined(split2(factor)), doubled(*split2(factor - spread(0.5 * x))))
            - spread(0.5 * v)
        )
        xs.append(m * v)
        zs.append(m)
    for b in range(blocks):
        inner[b] = inners[b]
        hat[b] = spread(xs[b]) + product(joined(split2(inners[b])), gram_right[b])

    for turn in range(1, NS_ITERS - 1):
        lefts, halves = [], []
        for b in range(blocks):
            x, z = xs[b], zs[b]
            factor = spread(jnp.full((1, LANES), 1.5, F32)) - 0.5 * hat[b]
            f_high, f_low = split2(factor)
            lefts.append(joined((f_high, f_low)))
            inside = inner[b]
            if turn == 1:
                halves.append(product(lefts[b], doubled(*split2(inside))) - (0.5 * x) * inside)
                outer[b] = -0.5 * factor - (0.5 * z) * inside
                continue
            i_high, i_low = split2(inside)
            o_high, o_low = split2(outer[b])
            right_high = joined((i_high, o_high))
            both = dot(lefts[b], jnp.concatenate([right_high, right_high], axis=0)) + dot(
                f_high, joined((i_low, o_low))
            )
            halves.append(both[:, :LANES] - (0.5 * x) * inside)
            outer[b] = both[:, LANES:] - (0.5 * z) * inside
        for b in range(blocks):
            m = 1.5 - 0.5 * xs[b]
            inner[b] = product(lefts[b], doubled(*split2(halves[b]))) - (0.5 * m * xs[b]) * inner[b]
        for b in range(blocks):
            m = 1.5 - 0.5 * xs[b]
            xs[b] = m * m * xs[b]
            zs[b] = m * zs[b]
            hat[b] = spread(xs[b]) + product(joined(split2(inner[b])), gram_right[b])

    own = iota((members, ensemble), 0) == iota((members, ensemble), 1)
    lasts, rights, rows, cores = [], [], [], []
    for b in range(blocks):
        x, z = xs[b], zs[b]
        factor = spread(jnp.full((1, LANES), 1.5, F32)) - 0.5 * hat[b]
        last = product(joined(split2(factor)), doubled(*split2(outer[b]))) - (0.5 * z) * inner[b]
        zs[b] = (1.5 - 0.5 * x) * z
        lasts.append(split2(last))
    for b in range(blocks):
        rights.append(doubled(*lasts[b]))
        rows.append(jnp.broadcast_to(departure[:, b * LANES : (b + 1) * LANES], (8, LANES)))
    for _ in range(2):
        moved = [product(joined(split2(rows[b])), rights[b]) for b in range(blocks)]
        moved = [product(joined(split2(moved[b])), gram_right[b]) for b in range(blocks)]
        rows = [zs[b] * rows[b] + moved[b] for b in range(blocks)]
    for b in range(blocks):
        mine = pert[:members, b * LANES : (b + 1) * LANES]
        cores.append(dot(joined((mine, mine)), jnp.concatenate(lasts[b], axis=0)))
    for b in range(blocks):
        root = jnp.sqrt(free * scales[b])
        core = cores[b] * (root * scales[b])
        row = rows[b] * scales[b]
        all_rows = joined(split2(jnp.concatenate([core, row, row], axis=0)))
        found = dot(all_rows, jnp.concatenate([turned[b], turned[b]], axis=0))
        diagonal = jnp.where(own, (root * zs[b])[:, 0:1], 0.0)
        out_ref[b] = (found[:members, :] + found[members : members + 1, :] + diagonal).astype(BF16)


def departures(pairs):
    count = len(pairs[0])
    ensemble = pairs[0][0].shape[0] * count
    parts = [joined([pair[k].astype(F32) for pair in pairs]) for k in range(count)]
    total = sum(jnp.sum(part, axis=0, keepdims=True) for part in parts)
    mean = total * (1.0 / ensemble)
    return jnp.concatenate([(part - mean).astype(BF16) for part in parts], axis=0), mean


def updated(left, moved, mean, width):
    members = left.shape[0] * width // LANES
    found = dot(left, moved)
    result = found[:members, :]
    lane = iota(result.shape, 1) % LANES
    for k in range(1, LANES // width):
        result = jnp.where(lane < k * width, result, found[k * members : (k + 1) * members, :])
    result = result + mean
    return [result[:, k : k + LANES] for k in range(0, result.shape[1], LANES)]


def weights_of(weight_ref, group, columns):
    per = weight_ref.shape[0] * LANES // columns
    return jnp.concatenate([weight_ref[group * per + k] for k in range(per)], axis=0)


def prepare_kernel(*refs, others):
    count = others + 1
    middles, firsts = [refs[k * count : (k + 1) * count] for k in range(2)]
    moved_ref, mean_ref = refs[2 * count :]
    slot = 0
    for piece in (middles, firsts):
        for k in range(0, piece[0].shape[0], 2):
            moved, mean = departures([[ref[k + j] for ref in piece] for j in range(2)])
            moved_ref[slot] = moved
            mean_ref[slot] = jnp.broadcast_to(mean, mean_ref.shape[1:])
            slot += 1


def update_kernel(*refs, others):
    afters = refs[: others + 1]
    moved_ref, mean_ref, weight_ref, out_hbm, rest_ref, stage, done, sems = refs[others + 1 :]
    members, levels, columns = out_hbm.shape
    width = columns // weight_ref.shape[0]
    groups = columns // LANES
    soon = 2 * moved_ref.shape[0] - (groups - 2) * levels
    part = afters[0].shape[0] - (levels - soon)

    def rows(level):
        return pl.ds(level, members, stride=levels)

    copies = []
    slot = 0
    for group in (*range(1, groups - 1), 0):
        left = weights_of(weight_ref, group, columns)
        for level in range(0, levels, 2):
            if group or level < soon:
                moved, mean = moved_ref[slot], mean_ref[slot, 0:1, :]
                slot += 1
            else:
                moved, mean = departures([[ref[level - soon + j] for ref in afters] for j in range(2)])
            for j, value in enumerate(updated(left, moved, mean, width)):
                stage[group, rows(level + j), :] = value
        done[group] = stage[group].reshape(members, levels, LANES).astype(BF16)
        lanes = slice(group * LANES, (group + 1) * LANES)
        copies.append(pltpu.make_async_copy(done.at[group], out_hbm.at[:, :, lanes], sems.at[group]))
        copies[-1].start()
    left = weights_of(weight_ref, groups - 1, columns)
    for level in range(0, part, 2):
        moved, mean = departures(
            [[ref[levels - soon + level + j] for ref in afters] for j in range(2)]
        )
        for j, value in enumerate(updated(left, moved, mean, width)):
            rest_ref[rows(level + j), :] = value
    for level in range(part, levels):
        rest_ref[rows(level), :] = jnp.zeros((members, LANES), F32)
    for copy in copies:
        copy.wait()


def finish_kernel(*refs, others):
    lasts = refs[: others + 1]
    weight_ref, rest_ref, _, out_hbm, stage, done, sem = refs[others + 1 :]
    members, levels, columns = out_hbm.shape
    width = columns // weight_ref.shape[0]
    count = lasts[0].shape[0]
    part = levels - count
    left = weights_of(weight_ref, columns // LANES - 1, columns)
    stage[...] = rest_ref[...]
    for level in range(0, count, 2):
        moved, mean = departures([[ref[level + j] for ref in lasts] for j in range(2)])
        for j, value in enumerate(updated(left, moved, mean, width)):
            stage[pl.ds(part + level + j, members, stride=levels), :] = value
    done[...] = stage[...].reshape(members, levels, LANES).astype(BF16)
    copy = pltpu.make_async_copy(done, out_hbm.at[:, :, columns - LANES : columns], sem)
    copy.start()
    copy.wait()


def vmem():
    return pl.BlockSpec(memory_space=pltpu.VMEM)


def group_spec(rows, group):
    return pl.BlockSpec((rows, LANES), lambda i: (0, group))


def call(kernel, outs, inputs, scratch=(), in_specs=None, out_specs=None, aliases=None, cost=0, limit=VMEM_LIMIT):
    return pl.pallas_call(
        kernel,
        grid=(1,),
        out_shape=outs,
        in_specs=in_specs or [vmem()] * len(inputs),
        out_specs=out_specs or [vmem()] * len(outs),
        scratch_shapes=list(scratch),
        input_output_aliases=aliases or {},
        compiler_params=pltpu.CompilerParams(vmem_limit_bytes=limit),
        cost_estimate=pl.CostEstimate(flops=cost << 30, bytes_accessed=1 << 10, transcendentals=0),
    )(*inputs)


def shards(
    fields,
    coefficients,
    neighbours,
    obs_cell,
    obs_level,
    obs_value,
    obs_rinv,
    obs_index,
    obs_weight,
):
    tiles = lax.axis_size("tile")
    sharers = lax.axis_size("mem")
    others = sharers - 1
    members, levels, columns = fields.shape
    blocks = obs_index.shape[0]
    entries = blocks * sharers * LANES
    half = members * levels // 2
    message = jax.ShapeDtypeStruct((half + MESSAGE_EXTRA, LANES), BF16)
    even_pairs = []
    odd_pairs = []
    for i in range(0, tiles, 2):
        even_pairs += [(i, i + 1), (i + 1, i)]
        low, high = i + 1, (i + 2) % tiles
        odd_pairs += [(low, high), (high, low)]
    turns = [[((i + r) % sharers, i) for i in range(sharers)] for r in range(1, sharers)]

    flat = fields.reshape(members * levels, columns)
    groups = columns // LANES
    hbm = pl.BlockSpec(memory_space=pltpu.HBM)
    a, b, lists, small = call(
        functools.partial(pack_kernel, tiles=tiles),
        [
            message,
            message,
            jax.ShapeDtypeStruct((16, LANES), BF16),
            jax.ShapeDtypeStruct((16, columns), F32),
        ],
        [flat, coefficients, neighbours, obs_index, obs_weight],
        [
            pltpu.VMEM((members * levels, LANES), F32),
            pltpu.VMEM((members * levels, LANES), F32),
            pltpu.VMEM((6, columns), F32),
            pltpu.VMEM((6, columns), jnp.int32),
            pltpu.VMEM(obs_index.shape, jnp.int32),
            pltpu.VMEM(obs_index.shape, jnp.int32),
            pltpu.SemaphoreType.DMA((6,)),
        ],
        in_specs=[hbm] * 5,
        limit=64 * 1024 * 1024,
    )
    from_b = lax.ppermute(b, "tile", even_pairs)
    from_a = lax.ppermute(a, "tile", odd_pairs)
    flat_rows = members * levels
    kept_levels = levels // 2
    soon_levels = levels // 4
    last_levels = levels // 2
    both, part, second = call(
        operator_kernel,
        [
            jax.ShapeDtypeStruct((columns, 2 * (columns - 2 * LANES)), BF16),
            jax.ShapeDtypeStruct((2, 2 * LANES, LANES), F32),
            jax.ShapeDtypeStruct((4, 2 * LANES, LANES), BF16),
        ],
        [small],
        cost=1,
    )
    middle, kept, border, border_low = call(
        functools.partial(middle_kernel, groups=groups),
        [
            jax.ShapeDtypeStruct(((groups - 2) * levels - kept_levels, members, LANES), BF16),
            jax.ShapeDtypeStruct((kept_levels, members, LANES), BF16),
            jax.ShapeDtypeStruct((2, flat_rows, 2 * LANES), BF16),
            jax.ShapeDtypeStruct((2, flat_rows, 2 * LANES), BF16),
        ],
        [flat] * groups + [both],
        [pltpu.VMEM((flat_rows, columns), BF16)] * 2,
        in_specs=[group_spec(flat_rows, group) for group in range(groups)] + [vmem()],
        cost=3,
    )
    passed = jnp.concatenate([from_a[half + 32 :], from_b[half + 32 :], lists], axis=0)

    def swapped(value, sent):
        return [value] + [lax.ppermute(sent, "mem", turn) for turn in turns]

    passed, sent = lax.optimization_barrier((passed, middle))
    middles = swapped(middle, sent)
    passed = [lax.ppermute(passed, "mem", turn) for turn in turns]
    first, after, last = call(
        edge_kernel,
        [
            *(
                jax.ShapeDtypeStruct((count, members, LANES), BF16)
                for count in (
                    kept_levels + soon_levels,
                    2 * levels - soon_levels - last_levels,
                    last_levels,
                )
            ),
        ],
        [from_a, from_b, small, border, border_low, part, second, kept],
        [pltpu.VMEM((2, flat_rows, 2 * LANES), BF16)],
        cost=2,
    )
    pieces = [middle, first, after, last]
    cell = obs_cell.reshape(16, LANES)
    level = obs_level.reshape(16, LANES)
    reading = jax.ShapeDtypeStruct((members, entries), BF16)
    table = pltpu.VMEM((48, LANES), BF16)
    def read_for(turn, received, passed, shape, held=(), unused=(), cost=2):
        inputs = [*pieces, received, cell, level, *passed, *held]
        (result,) = call(
            functools.partial(
                neighbour_kernel,
                others=len(passed),
                blocks=blocks,
                levels=levels,
                turn=turn,
                given=len(held),
            ),
            [shape],
            [*inputs, *unused],
            [table],
            in_specs=[vmem()] * len(inputs) + [pl.BlockSpec(memory_space=pl.ANY)] * len(unused),
            cost=cost,
        )
        return result

    mine = jax.ShapeDtypeStruct((members, blocks * LANES), BF16)
    mine = read_for(0, from_a, [], mine, cost=1)
    to_a = read_for(0, from_a, passed, reading, held=[mine], cost=1)
    to_b = read_for(1, from_b, passed, reading, unused=[to_a])
    to_b, sent = lax.optimization_barrier((to_b, first))
    firsts = swapped(first, sent)
    back_a = lax.ppermute(to_a, "tile", odd_pairs)
    back_b = lax.ppermute(to_b, "tile", even_pairs)
    vector = jax.ShapeDtypeStruct((8, entries), F32)
    own, weight, target = call(
        functools.partial(
            own_kernel, others=others, blocks=blocks, levels=levels, tiles=tiles
        ),
        [reading, vector, vector],
        [
            *pieces,
            lists,
            *passed,
            cell,
            level,
            obs_value.reshape(-1, LANES),
            obs_rinv.reshape(-1, LANES),
        ],
        [table],
        cost=2,
    )
    unused = middles[1:]
    (readings,) = call(merge_kernel, [reading], [own, back_a], cost=2)
    (readings,) = call(
        merge_kernel,
        [reading],
        [readings, back_b, *unused],
        in_specs=[vmem()] * 2 + [pl.BlockSpec(memory_space=pl.ANY)] * len(unused),
        cost=0,
    )
    readings, sent, sent_last = lax.optimization_barrier((readings, after, last))
    readings = swapped(readings, readings)
    afters = swapped(after, sent)
    lasts = swapped(last, sent_last)
    unused = firsts[1:]
    ensemble = members * sharers
    total = blocks * sharers
    square = pltpu.VMEM((total, LANES, LANES), F32)
    (weights,) = call(
        functools.partial(weights_kernel, others=others),
        [jax.ShapeDtypeStruct((total, members, ensemble), BF16)],
        [*readings, weight, target, *unused],
        [
            pltpu.VMEM((ensemble, entries), BF16),
            pltpu.VMEM((ensemble, entries), BF16),
            pltpu.VMEM((total, LANES, ensemble), BF16),
            pltpu.VMEM((total, 2 * LANES, 2 * LANES), BF16),
            square,
            square,
            square,
        ],
        in_specs=[vmem()] * (sharers + 2) + [pl.BlockSpec(memory_space=pl.ANY)] * len(unused),
        cost=8,
    )
    rows = members * levels
    result = jax.ShapeDtypeStruct((members, levels, columns), BF16)
    pairs = (middle.shape[0] + first.shape[0]) // 2
    moved, mean = call(
        functools.partial(prepare_kernel, others=others),
        [
            jax.ShapeDtypeStruct((pairs, ensemble, 2 * LANES), BF16),
            jax.ShapeDtypeStruct((pairs, 8, 2 * LANES), F32),
        ],
        [*middles, *firsts],
        cost=2,
    )
    inputs = [*afters, moved, mean, weights]
    analysis, rest = call(
        functools.partial(update_kernel, others=others),
        [result, jax.ShapeDtypeStruct((rows, LANES), F32)],
        inputs,
        [
            pltpu.VMEM((groups - 1, rows, LANES), F32),
            pltpu.VMEM((groups - 1, members, levels, LANES), BF16),
            pltpu.SemaphoreType.DMA((groups - 1,)),
        ],
        out_specs=[hbm, vmem()],
        cost=2,
    )
    inputs = [*lasts, weights, rest, analysis]
    (analysis,) = call(
        functools.partial(finish_kernel, others=others),
        [result],
        inputs,
        [
            pltpu.VMEM((rows, LANES), F32),
            pltpu.VMEM((members, levels, LANES), BF16),
            pltpu.SemaphoreType.DMA,
        ],
        in_specs=[vmem()] * (len(inputs) - 1) + [hbm],
        out_specs=[hbm],
        aliases={len(inputs) - 1: 0},
        cost=1,
    )
    return analysis


def solution(mesh):
    in_specs = (
        P("mem", None, "tile"),
        P(None, "tile"),
        P(None, "tile"),
        P("tile"),
        P("tile"),
        P(),
        P(),
        P("mem", "tile", None),
        P("mem", "tile", None),
    )
    out_specs = P("mem", None, "tile")
    return jax.shard_map(shards, mesh=mesh, in_specs=in_specs, out_specs=out_specs, check_vma=False)
```

```python
import functools

import jax
import jax.numpy as jnp
from jax import lax
from jax.experimental import pallas as pl
from jax.experimental.pallas import tpu as pltpu
from jax.sharding import PartitionSpec as P

HALO = 32
NS_ITERS = 8
LANES = 128
F32 = jnp.float32
BF16 = jnp.bfloat16
VMEM_LIMIT = 48 * 1024 * 1024

NN = (((1,), (0,)), ((), ()))
NT = (((1,), (1,)), ((), ()))
TN = (((0,), (0,)), ((), ()))


def dot(a, b, dims=NN):
    return lax.dot_general(a, b, dims, preferred_element_type=F32)


def split2(x):
    high = x.astype(BF16)
    return high, (x - high.astype(F32)).astype(BF16)


def split3(x):
    high = x.astype(BF16)
    rest = x - high.astype(F32)
    middle = rest.astype(BF16)
    return high, middle, (rest - middle.astype(F32)).astype(BF16)


def iota(shape, dim):
    return lax.broadcasted_iota(jnp.int32, shape, dim)


def is_odd_tile():
    return lax.axis_index("tile") % 2 == 1


def message_rows(field_rows):
    return {name: field_rows + 16 * place for place, name in enumerate(("coef", "offset", "list"))}


MESSAGE_EXTRA = 48
LISTS = 48


def pack_kernel(
    field_hbm,
    coef_hbm,
    nbr_hbm,
    index_hbm,
    weight_hbm,
    a_ref,
    b_ref,
    lists_ref,
    small_ref,
    left_ref,
    right_ref,
    coef_ref,
    nbr_ref,
    index_ref,
    weight_ref,
    sems,
    *,
    tiles,
):
    columns = coef_ref.shape[1]
    levels = 8
    half = left_ref.shape[0] // 2
    members = half // levels
    rows = message_rows(half)
    odd = is_odd_tile()
    total = columns * tiles
    copies = [
        pltpu.make_async_copy(source, target, sems.at[k])
        for k, (source, target) in enumerate(
            (
                (coef_hbm, coef_ref),
                (nbr_hbm, nbr_ref),
                (index_hbm, index_ref),
                (weight_hbm, weight_ref),
                (field_hbm.at[:, 0:LANES], left_ref),
                (field_hbm.at[:, columns - LANES : columns], right_ref),
            )
        )
    ]
    for copy in copies:
        copy.start()
    for copy in copies[:4]:
        copy.wait()

    place = lax.axis_index("tile") * columns + iota((6, columns), 1)
    offset = nbr_ref[...] - place
    offset = jnp.where(offset > HALO, offset - total, offset)
    offset = jnp.where(offset < -HALO, offset + total, offset).astype(F32)
    small_ref[...] = jnp.zeros_like(small_ref)
    small_ref[0:6, :] = coef_ref[...]
    small_ref[8:14, :] = offset
    pieces = [padded(value.astype(F32), 2) for value in split2(coef_ref[...])]
    reach = padded(offset, 10)
    for name, value in (("coef", jnp.concatenate(pieces, axis=0)), ("offset", reach)):
        first = value[:, :LANES]
        last = value[:, columns - LANES :]
        start = rows[name]
        a_ref[start : start + 16, :] = jnp.where(odd, last, first).astype(BF16)
        b_ref[start : start + 16, :] = jnp.where(odd, first, last).astype(BF16)
    blocks = index_ref.shape[0]
    index = index_ref[:, 0, :]
    quotient = padded(((index // LANES) * 4 + weight_ref[:, 0, :]).astype(F32), 8 - blocks)
    entries = padded((index % LANES).astype(F32), 8 - blocks)
    entries = jnp.concatenate([quotient, entries], axis=0).astype(BF16)
    start = rows["list"]
    a_ref[start : start + 16, :] = entries
    b_ref[start : start + 16, :] = entries
    lists_ref[...] = entries

    for copy in copies[4:]:
        copy.wait()
    lane = iota((members, LANES), 1)
    for level in range(levels):
        top = pl.ds(level, members, stride=levels)
        low = pl.ds(level + half, members, stride=levels)
        spot = slice(level * members, (level + 1) * members)
        left = jnp.where(lane < 64, left_ref[top, :], pltpu.roll(left_ref[low, :], 64, axis=1))
        right = jnp.where(lane < 64, pltpu.roll(right_ref[top, :], 64, axis=1), right_ref[low, :])
        a_ref[spot, :] = jnp.where(odd, right, left).astype(BF16)
        b_ref[spot, :] = jnp.where(odd, left, right).astype(BF16)


def band(coefs, offsets):
    shape = (LANES + 2 * HALO, LANES)
    spot = iota(shape, 0)
    result = jnp.where(
        spot == iota(shape, 1) + HALO, 1.0 - jnp.sum(coefs, axis=0, keepdims=True), 0.0
    )
    target = iota(offsets.shape, 1) + HALO + offsets.astype(jnp.int32)
    for j in range(6):
        result = result + jnp.where(spot == target[j : j + 1, :], coefs[j : j + 1, :], 0.0)
    return result


def dot3(left, right):
    return dot(left[0], right[0]) + (dot(left[0], right[1]) + dot(left[1], right[0]))


def padded(value, count):
    if not count:
        return value
    return jnp.concatenate([value, jnp.zeros((count, value.shape[1]), value.dtype)], axis=0)


def operator_kernel(small_ref, both_ref, part_ref, second_ref):
    columns = small_ref.shape[1]
    groups = columns // LANES
    coef = padded(small_ref[0:6, :], 2)
    reach = padded(small_ref[8:14, :], 2)
    moved = pltpu.roll(coef, HALO, axis=1), pltpu.roll(reach, HALO, axis=1)

    def operator(values, group):
        lanes = slice(group * LANES, (group + 1) * LANES)
        return split2(band(*(value[:, lanes] for value in values)))

    firsts = {g: operator(moved, g) for g in range(1, groups)}
    seconds = [[padded(v, 64) for v in operator((coef, reach), g)] for g in range(groups)]

    def upper(g):
        return padded(dot3(firsts[g], [value[:LANES, :] for value in seconds[g]]), 64)

    def lower(g):
        result = dot3(
            [value[:LANES, :] for value in firsts[g + 1]],
            [value[LANES:, :] for value in seconds[g]],
        )
        return jnp.concatenate([jnp.zeros_like(result), result], axis=0)

    both_ref[...] = jnp.zeros_like(both_ref)
    half = both_ref.shape[1] // 2
    for g in range(1, groups - 1):
        row, lane = g * LANES - 64, (g - 1) * LANES
        for k, value in enumerate(split2(upper(g) + lower(g))):
            both_ref[row : row + 2 * LANES, k * half + lane : k * half + lane + LANES] = value
    part_ref[0] = lower(0)
    part_ref[1] = upper(groups - 1)
    for k, g in enumerate((0, groups - 1)):
        for j in range(2):
            second_ref[2 * k + j] = seconds[g][j]


def middle_kernel(*refs, groups):
    field_refs = refs[:groups]
    both_ref, soon_ref, middle_ref, kept_ref, edge_ref, edge_low_ref, fields, fields_low = refs[groups:]
    members = middle_ref.shape[1]
    soon = (soon_ref.shape[0] - LISTS) // members
    levels = field_refs[0].shape[0] // members
    lane = iota((members, LANES), 1)
    for level in range(levels):
        spot = slice(level * members, (level + 1) * members)
        own = [ref[pl.ds(level, members, stride=levels), :] for ref in field_refs]
        for group in range(groups):
            lanes = slice(group * LANES, (group + 1) * LANES)
            fields[spot, lanes], fields_low[spot, lanes] = split2(own[group])
        pieces = [
            split2(pltpu.roll(own[g], 64, axis=1)) for g in (0, 1, groups - 2, groups - 1)
        ]
        for part, ref in enumerate((edge_ref, edge_low_ref)):
            turned = [piece[part].astype(F32) for piece in pieces]
            zero = jnp.zeros_like(turned[0])
            ref[0, spot, 0:LANES] = jnp.where(lane < 64, zero, turned[0]).astype(BF16)
            ref[0, spot, LANES:] = jnp.where(lane < 64, turned[0], turned[1]).astype(BF16)
            ref[1, spot, 0:LANES] = jnp.where(lane < 64, turned[2], turned[3]).astype(BF16)
            ref[1, spot, LANES:] = jnp.where(lane < 64, turned[3], zero).astype(BF16)
    result = dot(fields[...], both_ref[...])
    half = result.shape[1] // 2
    result = result[:, :half] + (result[:, half:] + dot(fields_low[...], both_ref[:, :half]))
    soon_ref[soon * members :, :] = jnp.zeros((LISTS, LANES), BF16)
    for k in range((groups - 2) * levels):
        level, lane = k % levels, (k // levels) * LANES
        value = result[level * members : (level + 1) * members, lane : lane + LANES].astype(BF16)
        if k < soon:
            soon_ref[k * members : (k + 1) * members, :] = value
        elif k < soon + middle_ref.shape[0]:
            middle_ref[k - soon] = value
        else:
            kept_ref[k - soon - middle_ref.shape[0]] = value


def edge_kernel(
    a_ref, b_ref, small_ref, edge_ref, edge_low_ref, part_ref, second_ref, kept_ref, first_ref, next_ref, last_ref, fields
):
    _, members, _ = next_ref.shape
    levels = fields.shape[1] // members
    columns = small_ref.shape[1]
    half = members // 2
    rows = message_rows(levels * half)
    odd = is_odd_tile()

    def side(k, start, count):
        a = a_ref[start : start + count, :].astype(F32)
        b = b_ref[start : start + count, :].astype(F32)
        return jnp.where(odd, b, a) if k == 0 else jnp.where(odd, a, b)

    own_coef = padded(small_ref[0:6, :], 2)
    own_reach = padded(small_ref[8:14, :], 2)
    lane8 = iota((8, LANES), 1)
    lane = iota((half, LANES), 1)
    operators = []
    for k in range(2):
        near = side(k, rows["coef"], 16)
        near = near[:8] + near[8:]
        reach = side(k, rows["offset"], 16)[:8]
        if k == 0:
            own = (own_coef[:, :LANES], own_reach[:, :LANES])
            both = [
                jnp.where(
                    lane8 < HALO, pltpu.roll(x, HALO, axis=1), pltpu.roll(y, HALO, axis=1)
                )
                for x, y in zip((near, reach), own)
            ]
            first = split2(band(*both))
            second = [second_ref[j, :128, :] for j in range(2)]
            fresh = padded(dot3(first, second), 64)
        else:
            own = (own_coef[:, columns - LANES :], own_reach[:, columns - LANES :])
            both = [
                jnp.where(
                    lane8 < HALO, pltpu.roll(y, HALO, axis=1), pltpu.roll(x, HALO, axis=1)
                )
                for x, y in zip((near, reach), own)
            ]
            first = [value[:128, :] for value in split2(band(*both))]
            second = [second_ref[2 + j, 128:, :] for j in range(2)]
            fresh = dot3(first, second)
            fresh = jnp.concatenate([jnp.zeros_like(fresh), fresh], axis=0)
        operators.append(split2(part_ref[k] + fresh))
    for k in range(2):
        for level in range(levels):
            top = level * members
            halo = side(k, level * half, half)
            other = pltpu.roll(halo, 64, axis=1)
            pair = (halo, other) if k == 0 else (other, halo)
            for j in range(2):
                spot = slice(top + j * half, top + (j + 1) * half)
                if k == 0:
                    own = edge_ref[k, spot, 0:LANES].astype(F32)
                    fields[k, spot, 0:LANES] = jnp.where(lane < 64, pair[j], own).astype(BF16)
                    fields[k, spot, LANES:] = edge_ref[k, spot, LANES:]
                else:
                    own = edge_ref[k, spot, LANES:].astype(F32)
                    fields[k, spot, LANES:] = jnp.where(lane < 64, own, pair[j]).astype(BF16)
                    fields[k, spot, 0:LANES] = edge_ref[k, spot, 0:LANES]
        result = dot(fields[k], joined(operators[k]))
        result = result[:, :LANES] + (
            result[:, LANES:] + dot(edge_low_ref[k], operators[k][0])
        )
        kept = kept_ref.shape[0]
        if k == 0:
            first_ref[:kept] = kept_ref[...]
        places = [
            (ref, place)
            for ref, start in ((first_ref, kept), (next_ref, 0), (last_ref, 0))
            for place in range(start, ref.shape[0])
        ]
        for level in range(levels):
            ref, place = places[k * levels + level]
            ref[place] = result[level * members : (level + 1) * members, :].astype(BF16)


def in_order(parts):
    count = len(parts)
    me = lax.axis_index("mem")
    placed = []
    for place in range(count):
        value = parts[0]
        for shift in range(1, count):
            value = jnp.where((me + shift) % count == place, parts[shift], value)
        placed.append(value)
    return joined(placed)


def entries_of(part, blocks):
    part = part.astype(F32)
    quotient = joined([part[b : b + 1, :] for b in range(blocks)]).astype(jnp.int32)
    rest = joined([part[8 + b : 9 + b, :] for b in range(blocks)]).astype(jnp.int32)
    return (quotient // 4) * LANES + rest, quotient % 4


def read_places(table_ref, slot):
    wide = slot.shape[1]
    valid = (slot >= 0) & (slot < 16 * LANES)
    slot = jnp.where(valid, slot, 0)
    one = jnp.where(iota((LANES, wide), 0) == slot % LANES, 1.0, 0.0).astype(BF16)
    found = dot(table_ref[...], one)
    pick = iota((16, wide), 0) == slot // LANES
    values = [
        jnp.sum(jnp.where(pick, found[16 * k : 16 * k + 16, :], 0.0), axis=0, keepdims=True)
        for k in range(3)
    ]
    column = (values[1] * 16.0 + values[2]).astype(jnp.int32)
    return values[0].astype(jnp.int32), jnp.where(valid, column, -1)


def make_table(cell_ref, level_ref, table):
    cell = cell_ref[...]
    table[0:16, :] = level_ref[...].astype(F32).astype(BF16)
    table[16:32, :] = (cell // 16).astype(F32).astype(BF16)
    table[32:48, :] = (cell % 16).astype(F32).astype(BF16)


def read_some(field, levels, level, column):
    members = field.shape[0] // levels
    wide = level.shape[1]
    one = jnp.where(iota((field.shape[1], wide), 0) == column, 1.0, 0.0).astype(BF16)
    found = dot(field, one)
    total = jnp.zeros((members, wide), F32)
    for l in range(levels):
        total = total + jnp.where(level == l, found[l * members : (l + 1) * members, :], 0.0)
    return total


def read_forecast(field, levels, level, column):
    step = min(256, level.shape[1])
    return joined(
        [
            read_some(field, levels, level[:, k : k + step], column[:, k : k + step])
            for k in range(0, level.shape[1], step)
        ]
    )


def whole(soon_ref, middle_ref, first_ref, next_ref, last_ref, levels):
    soon = soon_ref[: soon_ref.shape[0] - LISTS, :].reshape(-1, *middle_ref.shape[1:])
    rest = [ref[...] for ref in (middle_ref, first_ref, next_ref, last_ref)]
    runs = jnp.concatenate([soon, *rest], axis=0)
    groups = [runs[k : k + levels].reshape(-1, LANES) for k in range(0, runs.shape[0], levels)]
    return joined([groups[-2], *groups[:-2], groups[-1]])


def neighbour_kernel(*refs, others, blocks, levels, turn, given):
    message_ref, cell_ref, level_ref = refs[5:8]
    passed_refs = refs[8 : 8 + others]
    out_ref, table = refs[-2:]
    half = message_ref.shape[0] - MESSAGE_EXTRA
    rows = message_rows(half)
    odd = is_odd_tile()
    obs = 16 * LANES
    make_table(cell_ref, level_ref, table)
    field = whole(*refs[:5], levels)
    skip = jnp.where(odd, 0, 2 * obs) if turn == 0 else jnp.where(odd, 2 * obs, 0)
    base = refs[0].shape[0] - LISTS + 16 * turn
    parts = [ref[base : base + 16, :] for ref in passed_refs]
    if not given:
        parts = [message_ref[rows["list"] : rows["list"] + 16, :], *parts]
    index = joined([entries_of(part, blocks)[0] for part in parts])
    level, column = read_places(table, index - skip)
    found = read_forecast(field, levels, level, column)
    if others:
        mine = blocks * LANES
        found = [found[:, k : k + mine] for k in range(0, found.shape[1], mine)]
        if given:
            found = [refs[8 + others][...].astype(F32), *found]
        found = in_order(found)
    out_ref[...] = found.astype(BF16)


def own_kernel(*refs, others, blocks, levels, tiles):
    lists_ref = refs[5]
    other_refs = refs[6 : 6 + others]
    (
        cell_ref,
        level_ref,
        value_ref,
        rinv_ref,
        r_ref,
        weight_ref,
        target_ref,
        table,
    ) = refs[6 + others :]
    obs = 16 * LANES
    make_table(cell_ref, level_ref, table)
    field = whole(*refs[:5], levels)
    base = refs[0].shape[0] - LISTS + 32
    parts = [lists_ref[...]] + [r[base : base + 16, :] for r in other_refs]
    parts = [entries_of(part, blocks) for part in parts]
    index = in_order([index for index, _ in parts])
    weight = in_order([weight for _, weight in parts]).astype(F32)
    wide = index.shape[1]
    level, column = read_places(table, index - obs)
    r_ref[...] = read_forecast(field, levels, level, column).astype(BF16)

    tile = lax.axis_index("tile")
    starts = [((tile + tiles + shift) % tiles) * 16 for shift in (-1, 0, 1)]
    one = jnp.where(iota((LANES, wide), 0) == index % LANES, 1.0, 0.0).astype(BF16)
    pick = iota((48, wide), 0) == index // LANES

    def looked_up(ref):
        window = jnp.concatenate([ref[pl.ds(pl.multiple_of(s, 16), 16), :] for s in starts], axis=0)
        high, middle, low = [dot(piece, one) for piece in split3(window)]
        return jnp.sum(jnp.where(pick, (high + middle) + low, 0.0), axis=0, keepdims=True)

    weight_ref[...] = jnp.broadcast_to(looked_up(rinv_ref) * (weight / 3.0), weight_ref.shape)
    target_ref[...] = jnp.broadcast_to(looked_up(value_ref), target_ref.shape)


def merge_kernel(one_ref, other_ref, *refs):
    out_ref = refs[-1]
    out_ref[...] = (one_ref[...].astype(F32) + other_ref[...].astype(F32)).astype(BF16)


def doubled(high, low):
    top = jnp.concatenate([high, low], axis=1)
    bottom = jnp.concatenate([high, jnp.zeros_like(low)], axis=1)
    return jnp.concatenate([top, bottom], axis=0)


def product(left, right):
    both = dot(left, right)
    wide = both.shape[1] // 2
    return both[:, :wide] + both[:, wide:]


def joined(pair):
    return jnp.concatenate(pair, axis=1)


def weights_kernel(*refs, others):
    r_refs = refs[: others + 1]
    weight_ref, target_ref = refs[others + 1 : others + 3]
    out_ref, pert, weighted, turned, gram_right, hat, inner, outer = refs[-8:]
    members, wide = r_refs[0].shape
    blocks = wide // LANES
    ensemble = members * (others + 1)
    free = ensemble - 1.0

    parts = [ref[...].astype(F32) for ref in r_refs]
    total = sum(jnp.sum(part, axis=0, keepdims=True) for part in parts)
    mean = total * (1.0 / ensemble)
    weight = weight_ref[0:1, :]
    for k, part in enumerate(parts):
        rounded = (part - mean).astype(BF16)
        pert[k * members : (k + 1) * members, :] = rounded
        weighted[k * members : (k + 1) * members, :] = (rounded.astype(F32) * weight).astype(BF16)
    departure = target_ref[0:1, :] - mean

    eye = iota((LANES, LANES), 0) == iota((LANES, LANES), 1)

    def spread(value):
        return jnp.where(eye, value, 0.0)

    scales, xs, zs, grams, lefts, inners = [], [], [], [], [], []
    for b in range(blocks):
        lanes = slice(b * LANES, (b + 1) * LANES)
        turned[b] = weighted[:, lanes].T
    for b in range(blocks):
        lanes = slice(b * LANES, (b + 1) * LANES)
        grams.append(dot(turned[b], pert[:, lanes]))
    for b in range(blocks):
        trace = jnp.sum(jnp.sum(spread(grams[b]), axis=0, keepdims=True), axis=1, keepdims=True)
        scales.append(jnp.broadcast_to(1.0 / (free + trace), (1, LANES)))
    for b in range(blocks):
        gram = grams[b] * scales[b]
        x = free * scales[b]
        gram_right[b] = doubled(*split2(gram))
        m = 1.5 - 0.5 * x
        factor = spread(m) - 0.5 * gram
        v = m * x
        inners.append(
            product(joined(split2(factor)), doubled(*split2(factor - spread(0.5 * x))))
            - spread(0.5 * v)
        )
        xs.append(m * v)
        zs.append(m)
    for b in range(blocks):
        inner[b] = inners[b]
        hat[b] = spread(xs[b]) + product(joined(split2(inners[b])), gram_right[b])

    for turn in range(1, NS_ITERS - 1):
        lefts, halves = [], []
        for b in range(blocks):
            x, z = xs[b], zs[b]
            factor = spread(jnp.full((1, LANES), 1.5, F32)) - 0.5 * hat[b]
            f_high, f_low = split2(factor)
            lefts.append(joined((f_high, f_low)))
            inside = inner[b]
            if turn == 1:
                halves.append(product(lefts[b], doubled(*split2(inside))) - (0.5 * x) * inside)
                outer[b] = -0.5 * factor - (0.5 * z) * inside
                continue
            i_high, i_low = split2(inside)
            o_high, o_low = split2(outer[b])
            right_high = joined((i_high, o_high))
            both = dot(lefts[b], jnp.concatenate([right_high, right_high], axis=0)) + dot(
                f_high, joined((i_low, o_low))
            )
            halves.append(both[:, :LANES] - (0.5 * x) * inside)
            outer[b] = both[:, LANES:] - (0.5 * z) * inside
        for b in range(blocks):
            m = 1.5 - 0.5 * xs[b]
            inner[b] = product(lefts[b], doubled(*split2(halves[b]))) - (0.5 * m * xs[b]) * inner[b]
        for b in range(blocks):
            m = 1.5 - 0.5 * xs[b]
            xs[b] = m * m * xs[b]
            zs[b] = m * zs[b]
            hat[b] = spread(xs[b]) + product(joined(split2(inner[b])), gram_right[b])

    own = iota((members, ensemble), 0) == iota((members, ensemble), 1)
    lasts, rights, rows, cores = [], [], [], []
    for b in range(blocks):
        x, z = xs[b], zs[b]
        factor = spread(jnp.full((1, LANES), 1.5, F32)) - 0.5 * hat[b]
        last = product(joined(split2(factor)), doubled(*split2(outer[b]))) - (0.5 * z) * inner[b]
        zs[b] = (1.5 - 0.5 * x) * z
        lasts.append(split2(last))
    for b in range(blocks):
        rights.append(doubled(*lasts[b]))
        rows.append(jnp.broadcast_to(departure[:, b * LANES : (b + 1) * LANES], (8, LANES)))
    for _ in range(2):
        moved = [product(joined(split2(rows[b])), rights[b]) for b in range(blocks)]
        moved = [product(joined(split2(moved[b])), gram_right[b]) for b in range(blocks)]
        rows = [zs[b] * rows[b] + moved[b] for b in range(blocks)]
    for b in range(blocks):
        mine = pert[:members, b * LANES : (b + 1) * LANES]
        cores.append(dot(joined((mine, mine)), jnp.concatenate(lasts[b], axis=0)))
    for b in range(blocks):
        root = jnp.sqrt(free * scales[b])
        core = cores[b] * (root * scales[b])
        row = rows[b] * scales[b]
        all_rows = joined(split2(jnp.concatenate([core, row, row], axis=0)))
        found = dot(all_rows, jnp.concatenate([turned[b], turned[b]], axis=0))
        diagonal = jnp.where(own, (root * zs[b])[:, 0:1], 0.0)
        out_ref[b] = (found[:members, :] + found[members : members + 1, :] + diagonal).astype(BF16)


def departures(pairs):
    count = len(pairs[0])
    ensemble = pairs[0][0].shape[0] * count
    parts = [joined([pair[k].astype(F32) for pair in pairs]) for k in range(count)]
    total = sum(jnp.sum(part, axis=0, keepdims=True) for part in parts)
    mean = total * (1.0 / ensemble)
    return jnp.concatenate([(part - mean).astype(BF16) for part in parts], axis=0), mean


def updated(left, moved, mean, width):
    members = left.shape[0] * width // LANES
    found = dot(left, moved)
    result = found[:members, :]
    lane = iota(result.shape, 1) % LANES
    for k in range(1, LANES // width):
        result = jnp.where(lane < k * width, result, found[k * members : (k + 1) * members, :])
    result = result + mean
    return [result[:, k : k + LANES] for k in range(0, result.shape[1], LANES)]


def weights_of(weight_ref, group, columns):
    per = weight_ref.shape[0] * LANES // columns
    return jnp.concatenate([weight_ref[group * per + k] for k in range(per)], axis=0)


def prepare_kernel(*refs, others):
    count = others + 1
    soons, middles, firsts = [refs[k * count : (k + 1) * count] for k in range(3)]
    moved_ref, mean_ref = refs[3 * count :]
    members = middles[0].shape[1]
    soon = (soons[0].shape[0] - LISTS) // members
    runs = [[ref[k * members : (k + 1) * members, :] for ref in soons] for k in range(soon)]
    for piece in (middles, firsts):
        runs += [[ref[k] for ref in piece] for k in range(piece[0].shape[0])]
    for slot in range(len(runs) // 2):
        moved, mean = departures(runs[2 * slot : 2 * slot + 2])
        moved_ref[slot] = moved
        mean_ref[slot] = jnp.broadcast_to(mean, mean_ref.shape[1:])


def update_kernel(*refs, others):
    afters = refs[: others + 1]
    moved_ref, mean_ref, weight_ref, out_hbm, rest_ref, stage, done, sems = refs[others + 1 :]
    members, levels, columns = out_hbm.shape
    width = columns // weight_ref.shape[0]
    groups = columns // LANES
    soon = 2 * moved_ref.shape[0] - (groups - 2) * levels
    part = afters[0].shape[0] - (levels - soon)

    def rows(level):
        return pl.ds(level, members, stride=levels)

    copies = []
    slot = 0
    for group in (*range(1, groups - 1), 0):
        left = weights_of(weight_ref, group, columns)
        for level in range(0, levels, 2):
            if group or level < soon:
                moved, mean = moved_ref[slot], mean_ref[slot, 0:1, :]
                slot += 1
            else:
                moved, mean = departures([[ref[level - soon + j] for ref in afters] for j in range(2)])
            for j, value in enumerate(updated(left, moved, mean, width)):
                stage[group, rows(level + j), :] = value
        done[group] = stage[group].reshape(members, levels, LANES).astype(BF16)
        lanes = slice(group * LANES, (group + 1) * LANES)
        copies.append(pltpu.make_async_copy(done.at[group], out_hbm.at[:, :, lanes], sems.at[group]))
        copies[-1].start()
    left = weights_of(weight_ref, groups - 1, columns)
    for level in range(0, part, 2):
        moved, mean = departures(
            [[ref[levels - soon + level + j] for ref in afters] for j in range(2)]
        )
        for j, value in enumerate(updated(left, moved, mean, width)):
            rest_ref[rows(level + j), :] = value
    for level in range(part, levels):
        rest_ref[rows(level), :] = jnp.zeros((members, LANES), F32)
    for copy in copies:
        copy.wait()


def finish_kernel(*refs, others):
    lasts = refs[: others + 1]
    weight_ref, rest_ref, _, out_hbm, stage, done, sem = refs[others + 1 :]
    members, levels, columns = out_hbm.shape
    width = columns // weight_ref.shape[0]
    count = lasts[0].shape[0]
    part = levels - count
    left = weights_of(weight_ref, columns // LANES - 1, columns)
    stage[...] = rest_ref[...]
    for level in range(0, count, 2):
        moved, mean = departures([[ref[level + j] for ref in lasts] for j in range(2)])
        for j, value in enumerate(updated(left, moved, mean, width)):
            stage[pl.ds(part + level + j, members, stride=levels), :] = value
    done[...] = stage[...].reshape(members, levels, LANES).astype(BF16)
    copy = pltpu.make_async_copy(done, out_hbm.at[:, :, columns - LANES : columns], sem)
    copy.start()
    copy.wait()


def vmem():
    return pl.BlockSpec(memory_space=pltpu.VMEM)


def group_spec(rows, group):
    return pl.BlockSpec((rows, LANES), lambda i: (0, group))


def call(kernel, outs, inputs, scratch=(), in_specs=None, out_specs=None, aliases=None, cost=0, limit=VMEM_LIMIT):
    return pl.pallas_call(
        kernel,
        grid=(1,),
        out_shape=outs,
        in_specs=in_specs or [vmem()] * len(inputs),
        out_specs=out_specs or [vmem()] * len(outs),
        scratch_shapes=list(scratch),
        input_output_aliases=aliases or {},
        compiler_params=pltpu.CompilerParams(vmem_limit_bytes=limit),
        cost_estimate=pl.CostEstimate(flops=cost << 30, bytes_accessed=1 << 10, transcendentals=0),
    )(*inputs)


def shards(
    fields,
    coefficients,
    neighbours,
    obs_cell,
    obs_level,
    obs_value,
    obs_rinv,
    obs_index,
    obs_weight,
):
    tiles = lax.axis_size("tile")
    sharers = lax.axis_size("mem")
    others = sharers - 1
    members, levels, columns = fields.shape
    blocks = obs_index.shape[0]
    entries = blocks * sharers * LANES
    half = members * levels // 2
    message = jax.ShapeDtypeStruct((half + MESSAGE_EXTRA, LANES), BF16)
    even_pairs = []
    odd_pairs = []
    for i in range(0, tiles, 2):
        even_pairs += [(i, i + 1), (i + 1, i)]
        low, high = i + 1, (i + 2) % tiles
        odd_pairs += [(low, high), (high, low)]
    turns = [[((i + r) % sharers, i) for i in range(sharers)] for r in range(1, sharers)]

    flat = fields.reshape(members * levels, columns)
    groups = columns // LANES
    hbm = pl.BlockSpec(memory_space=pltpu.HBM)
    a, b, lists, small = call(
        functools.partial(pack_kernel, tiles=tiles),
        [
            message,
            message,
            jax.ShapeDtypeStruct((16, LANES), BF16),
            jax.ShapeDtypeStruct((16, columns), F32),
        ],
        [flat, coefficients, neighbours, obs_index, obs_weight],
        [
            pltpu.VMEM((members * levels, LANES), F32),
            pltpu.VMEM((members * levels, LANES), F32),
            pltpu.VMEM((6, columns), F32),
            pltpu.VMEM((6, columns), jnp.int32),
            pltpu.VMEM(obs_index.shape, jnp.int32),
            pltpu.VMEM(obs_index.shape, jnp.int32),
            pltpu.SemaphoreType.DMA((6,)),
        ],
        in_specs=[hbm] * 5,
        limit=64 * 1024 * 1024,
    )
    from_b = lax.ppermute(b, "tile", even_pairs)
    from_a = lax.ppermute(a, "tile", odd_pairs)
    flat_rows = members * levels
    kept_levels = levels // 4
    soon_sent = levels // 8
    soon_levels = levels // 2
    last_levels = levels // 2
    both, part, second = call(
        operator_kernel,
        [
            jax.ShapeDtypeStruct((columns, 2 * (columns - 2 * LANES)), BF16),
            jax.ShapeDtypeStruct((2, 2 * LANES, LANES), F32),
            jax.ShapeDtypeStruct((4, 2 * LANES, LANES), BF16),
        ],
        [small],
        cost=1,
    )
    soon, middle, kept, border, border_low = call(
        functools.partial(middle_kernel, groups=groups),
        [
            jax.ShapeDtypeStruct((soon_sent * members + LISTS, LANES), BF16),
            jax.ShapeDtypeStruct(
                ((groups - 2) * levels - soon_sent - kept_levels, members, LANES), BF16
            ),
            jax.ShapeDtypeStruct((kept_levels, members, LANES), BF16),
            jax.ShapeDtypeStruct((2, flat_rows, 2 * LANES), BF16),
            jax.ShapeDtypeStruct((2, flat_rows, 2 * LANES), BF16),
        ],
        [flat] * groups + [both],
        [pltpu.VMEM((flat_rows, columns), BF16)] * 2,
        in_specs=[group_spec(flat_rows, group) for group in range(groups)] + [vmem()],
        cost=3,
    )

    def swapped(value, sent):
        return [value] + [lax.ppermute(sent, "mem", turn) for turn in turns]

    passed = jnp.concatenate([from_a[half + 32 :], from_b[half + 32 :], lists], axis=0)
    soon = lax.dynamic_update_slice(soon, passed, (soon_sent * members, 0))
    soon, sent = lax.optimization_barrier((soon, middle))
    middles = swapped(middle, sent)
    soons = swapped(soon, soon)
    passed = soons[1:]
    first, after, last = call(
        edge_kernel,
        [
            *(
                jax.ShapeDtypeStruct((count, members, LANES), BF16)
                for count in (
                    kept_levels + soon_levels,
                    2 * levels - soon_levels - last_levels,
                    last_levels,
                )
            ),
        ],
        [from_a, from_b, small, border, border_low, part, second, kept],
        [pltpu.VMEM((2, flat_rows, 2 * LANES), BF16)],
        cost=2,
    )
    pieces = [soon, middle, first, after, last]
    cell = obs_cell.reshape(16, LANES)
    level = obs_level.reshape(16, LANES)
    reading = jax.ShapeDtypeStruct((members, entries), BF16)
    table = pltpu.VMEM((48, LANES), BF16)
    def read_for(turn, received, passed, shape, held=(), unused=(), cost=2):
        inputs = [*pieces, received, cell, level, *passed, *held]
        (result,) = call(
            functools.partial(
                neighbour_kernel,
                others=len(passed),
                blocks=blocks,
                levels=levels,
                turn=turn,
                given=len(held),
            ),
            [shape],
            [*inputs, *unused],
            [table],
            in_specs=[vmem()] * len(inputs) + [pl.BlockSpec(memory_space=pl.ANY)] * len(unused),
            cost=cost,
        )
        return result

    mine = jax.ShapeDtypeStruct((members, blocks * LANES), BF16)
    mine = read_for(0, from_a, [], mine, cost=1)
    to_a = read_for(0, from_a, passed, reading, held=[mine], cost=1)
    to_b = read_for(1, from_b, passed, reading, unused=[to_a])
    to_b, sent = lax.optimization_barrier((to_b, first))
    firsts = swapped(first, sent)
    back_a = lax.ppermute(to_a, "tile", odd_pairs)
    back_b = lax.ppermute(to_b, "tile", even_pairs)
    vector = jax.ShapeDtypeStruct((8, entries), F32)
    own, weight, target = call(
        functools.partial(
            own_kernel, others=others, blocks=blocks, levels=levels, tiles=tiles
        ),
        [reading, vector, vector],
        [
            *pieces,
            lists,
            *passed,
            cell,
            level,
            obs_value.reshape(-1, LANES),
            obs_rinv.reshape(-1, LANES),
        ],
        [table],
        cost=2,
    )
    unused = []
    (readings,) = call(merge_kernel, [reading], [own, back_a], cost=2)
    (readings,) = call(
        merge_kernel,
        [reading],
        [readings, back_b, *unused],
        in_specs=[vmem()] * 2 + [pl.BlockSpec(memory_space=pl.ANY)] * len(unused),
        cost=0,
    )
    readings, sent, sent_last = lax.optimization_barrier((readings, after, last))
    readings = swapped(readings, readings)
    afters = swapped(after, sent)
    lasts = swapped(last, sent_last)
    unused = [*middles[1:], *firsts[1:]]
    ensemble = members * sharers
    total = blocks * sharers
    square = pltpu.VMEM((total, LANES, LANES), F32)
    (weights,) = call(
        functools.partial(weights_kernel, others=others),
        [jax.ShapeDtypeStruct((total, members, ensemble), BF16)],
        [*readings, weight, target, *unused],
        [
            pltpu.VMEM((ensemble, entries), BF16),
            pltpu.VMEM((ensemble, entries), BF16),
            pltpu.VMEM((total, LANES, ensemble), BF16),
            pltpu.VMEM((total, 2 * LANES, 2 * LANES), BF16),
            square,
            square,
            square,
        ],
        in_specs=[vmem()] * (sharers + 2) + [pl.BlockSpec(memory_space=pl.ANY)] * len(unused),
        cost=8,
    )
    rows = members * levels
    result = jax.ShapeDtypeStruct((members, levels, columns), BF16)
    pairs = (soon_sent + middle.shape[0] + first.shape[0]) // 2
    moved, mean = call(
        functools.partial(prepare_kernel, others=others),
        [
            jax.ShapeDtypeStruct((pairs, ensemble, 2 * LANES), BF16),
            jax.ShapeDtypeStruct((pairs, 8, 2 * LANES), F32),
        ],
        [*soons, *middles, *firsts],
        cost=2,
    )
    inputs = [*afters, moved, mean, weights]
    analysis, rest = call(
        functools.partial(update_kernel, others=others),
        [result, jax.ShapeDtypeStruct((rows, LANES), F32)],
        inputs,
        [
            pltpu.VMEM((groups - 1, rows, LANES), F32),
            pltpu.VMEM((groups - 1, members, levels, LANES), BF16),
            pltpu.SemaphoreType.DMA((groups - 1,)),
        ],
        out_specs=[hbm, vmem()],
        cost=2,
    )
    inputs = [*lasts, weights, rest, analysis]
    (analysis,) = call(
        functools.partial(finish_kernel, others=others),
        [result],
        inputs,
        [
            pltpu.VMEM((rows, LANES), F32),
            pltpu.VMEM((members, levels, LANES), BF16),
            pltpu.SemaphoreType.DMA,
        ],
        in_specs=[vmem()] * (len(inputs) - 1) + [hbm],
        out_specs=[hbm],
        aliases={len(inputs) - 1: 0},
        cost=1,
    )
    return analysis


def solution(mesh):
    in_specs = (
        P("mem", None, "tile"),
        P(None, "tile"),
        P(None, "tile"),
        P("tile"),
        P("tile"),
        P(),
        P(),
        P("mem", "tile", None),
        P("mem", "tile", None),
    )
    out_specs = P("mem", None, "tile")
    return jax.shard_map(shards, mesh=mesh, in_specs=in_specs, out_specs=out_specs, check_vma=False)
```
